32 devices in a mesh: sp: 4 (over y, x), fsdp: 8 (over z, core).
Axes of the slice: x: 2, y: 2, z: 4, core: 2. Of those that a mesh axis runs over, the one named last changes fastest.
Arguments:
- tokens: bfloat16 [8, 1024, 2048], P('fsdp', 'sp'), may hold values from -6 to 6
- cotangent: bfloat16 [8, 1024, 2048], P('fsdp', 'sp'), may hold values from -6 to 6
- positions: int32 [8, 1024], P('fsdp', 'sp'), may hold values from 0 to 1023, as said below
- domain_ids: int32 [8], P('fsdp'), may hold values from 0 to 7
- counts: int32 [8], P('fsdp'), may hold values from 512 to 1024
- loss_weight: float32 [8], P('fsdp'), may hold values from 0.5 to 2
- domain_weights: float32 [8], replicated, may hold values from 0.5 to 2
- q_weight: bfloat16 [2048, 2048], P('fsdp'), may hold values from -0.125 to 0.125
- k_weight: bfloat16 [2048, 1024], P('fsdp'), may hold values from -0.125 to 0.125
- v_weight: bfloat16 [2048, 1024], P('fsdp'), may hold values from -0.125 to 0.125
- g_weight: bfloat16 [2048, 2048], P('fsdp'), may hold values from -0.125 to 0.125
- o_weight: bfloat16 [2048, 2048], P('fsdp'), may hold values from -2 to 2
- gate_weight: bfloat16 [2048, 6144], P('fsdp'), may hold values from -0.125 to 0.125
- up_weight: bfloat16 [2048, 6144], P('fsdp'), may hold values from -0.125 to 0.125
- down_weight: bfloat16 [6144, 2048], P('fsdp'), may hold values from -0.078125 to 0.078125
- attn_gain: bfloat16 [2048], P('fsdp'), may hold values from 0.5 to 1.5
- mlp_gain: bfloat16 [2048], P('fsdp'), may hold values from 0.5 to 1.5
- q_gain: bfloat16 [128], P('fsdp'), may hold values from 0.099609375 to 1.8984375
- k_gain: bfloat16 [128], P('fsdp'), may hold values from 0.099609375 to 1.8984375
Outputs:
- block_out: bfloat16 [8, 1024, 2048], P('fsdp', 'sp')
- input_grad: float32 [8, 1024, 2048], P('fsdp', 'sp')
- q_weight_grad: float32 [2048, 2048], P('fsdp')
- k_weight_grad: float32 [2048, 1024], P('fsdp')
- v_weight_grad: float32 [2048, 1024], P('fsdp')
- g_weight_grad: float32 [2048, 2048], P('fsdp')
- o_weight_grad: float32 [2048, 2048], P('fsdp')
- gate_weight_grad: float32 [2048, 6144], P('fsdp')
- up_weight_gradient: float32 [2048, 6144], P('fsdp')
- down_weight_grad: float32 [6144, 2048], P('fsdp')
- attn_gain_grad: float32 [2048], P('fsdp')
- mlp_gain_grad: float32 [2048], P('fsdp')
- q_gain_grad: float32 [128], P('fsdp')
- k_gain_grad: float32 [128], P('fsdp')
The draws below stay inside these ranges and needn't reach their ends.
Inputs may be any that keep to these rules, and one draw needn't show every extreme that they name: `positions`: within each sequence a position is 0 at the first token and at a few other tokens, and one more than the position before it elsewhere; one sequence has no such restart after its first token.
All inputs are finite; a program needn't handle non-finite values.
Results may differ from the reference program's by a relative error of at most 0.022.
Values may be sent and summed in bfloat16 or wider, within the bound.
No kernel may reach another device: no remote copies, remote signals or barrier semaphores. Data moves between devices by JAX's collectives and lax.ppermute only.
A program may use at most 448 MiB of HBM per device.

```python
import math
import jax
import jax.numpy as jnp
from jax import lax

D = 2048
HEADS = 16
KV_HEADS = 8
HEAD = 128
FF = 6144
SEQ_LEN = 1024
SEQS_DEV = 1
DOMAINS = 8
SEQUENCES = 8


def draw_positions(key, part):
    key = jax.random.fold_in(key, 11)
    marks = jax.random.randint(key, (SEQUENCES, SEQ_LEN), 0, 128)
    steady = jax.random.randint(jax.random.fold_in(key, 5), (), 0, SEQUENCES)
    places = lax.broadcasted_iota(jnp.int32, (SEQUENCES, SEQ_LEN), 1)
    rows_index = lax.broadcasted_iota(jnp.int32, (SEQUENCES, SEQ_LEN), 0)
    starts = jnp.where((marks == 0) & (rows_index != steady) | (places == 0), places, 0)
    starts = lax.cummax(starts, axis=1)
    return (places - starts).astype(jnp.int32)


def touch_ends(values, key, least, largest):
    place = [jax.random.randint(jax.random.fold_in(key, axis), (), 0, length) for axis, length in enumerate(values.shape)]
    main_axis = values.shape.index(max(values.shape))
    neighbour = place[:main_axis] + [(place[main_axis] + 1) % values.shape[main_axis]] + place[main_axis + 1:]
    return values.at[tuple(place)].set(least).at[tuple(neighbour)].set(largest)


def block_scale(key, extent, cuts, least, high):
    factor_of = 1.0
    for dim, shards_of in cuts:
        draws = jax.random.uniform(jax.random.fold_in(jax.random.fold_in(key, 6), dim), (shards_of,), jnp.float32, least / len(cuts), high / len(cuts))
        factor_of = factor_of * jnp.repeat(jnp.exp(draws), extent[dim] // shards_of).reshape((-1,) + (1,) * (len(extent) - 1 - dim))
    return factor_of


def normal_values(rng, extent, deviation, reach, cuts=(), kind=jnp.bfloat16):
    loudness = block_scale(rng, extent, cuts, -0.22, 0.18) if cuts else 1.0
    values = jax.random.normal(rng, extent, jnp.float32) * deviation * loudness
    return jnp.minimum(jnp.maximum(values, -reach), reach).astype(kind)


def setup_inputs(seed: int = 0) -> dict:
    seeds = jax.random.split(jax.random.key(seed), 20)
    tokens = normal_values(seeds[0], (SEQUENCES, SEQ_LEN, D), 1.0, 6.0, ((0, 8), (1, 4)))
    cotangent = normal_values(seeds[1], (SEQUENCES, SEQ_LEN, D), 1.0, 6.0, ((0, 8), (1, 4)))
    positions = draw_positions(jax.random.fold_in(seeds[19], 71), 0)
    domain_ids = touch_ends(jax.random.randint(seeds[3], (SEQUENCES,), 0, DOMAINS), jax.random.fold_in(seeds[3], 1), 0, DOMAINS - 1).astype(jnp.int32)
    counts = touch_ends(jax.random.randint(seeds[4], (SEQUENCES,), SEQ_LEN // 2, SEQ_LEN + 1), jax.random.fold_in(seeds[4], 1), SEQ_LEN // 2, SEQ_LEN).astype(jnp.int32)
    loss_weight = jnp.clip(jnp.exp(math.log(2.0) - 1.3862944 * jax.random.uniform(seeds[5], (SEQUENCES,), jnp.float32) ** block_scale(seeds[5], (SEQUENCES,), ((0, 8),), -0.2, 0.2)), 0.5, 2.0)
    domain_weights = jnp.clip(jnp.exp(jax.random.uniform(seeds[6], (DOMAINS,), jnp.float32, math.log(0.5), math.log(2.0))), 0.5, 2.0)
    q_weight = normal_values(seeds[7], (D, HEADS * HEAD), D ** -0.5, 0.125, ((0, 8),))
    k_weight = normal_values(seeds[8], (D, KV_HEADS * HEAD), D ** -0.5, 0.125, ((0, 8),))
    v_weight = normal_values(seeds[9], (D, KV_HEADS * HEAD), D ** -0.5, 0.125, ((0, 8),))
    g_weight = normal_values(seeds[10], (D, HEADS * HEAD), D ** -0.5, 0.125, ((0, 8),))
    o_weight = normal_values(seeds[11], (HEADS * HEAD, D), (HEADS * HEAD // 256) ** -0.5, 2.0, ((0, 8),))
    gate_weight = normal_values(seeds[12], (D, FF), D ** -0.5, 0.125, ((0, 8),))
    up_weight = normal_values(seeds[13], (D, FF), D ** -0.5, 0.125, ((0, 8),))
    down_weight = normal_values(seeds[14], (FF, D), FF ** -0.5, 0.078125, ((0, 8),))
    attn_gain = jnp.clip(1.0 + 0.1 * jax.random.normal(seeds[15], (D,), jnp.float32), 0.5, 1.5).astype(jnp.bfloat16)
    mlp_gain = jnp.clip(1.0 + 0.1 * jax.random.normal(seeds[16], (D,), jnp.float32), 0.5, 1.5).astype(jnp.bfloat16)
    q_gain = jnp.clip(1.0 + 0.18 * jax.random.normal(seeds[17], (HEAD,), jnp.float32), 0.099609375, 1.8984375).astype(jnp.bfloat16)
    k_gain = jnp.clip(1.0 + 0.18 * jax.random.normal(seeds[18], (HEAD,), jnp.float32), 0.099609375, 1.8984375).astype(jnp.bfloat16)
    return {"tokens": tokens, "cotangent": cotangent, "positions": positions, "domain_ids": domain_ids, "counts": counts, "loss_weight": loss_weight, "domain_weights": domain_weights, "q_weight": q_weight, "k_weight": k_weight, "v_weight": v_weight, "g_weight": g_weight, "o_weight": o_weight, "gate_weight": gate_weight, "up_weight": up_weight, "down_weight": down_weight, "attn_gain": attn_gain, "mlp_gain": mlp_gain, "q_gain": q_gain, "k_gain": k_gain}


EPS = 1e-06
ROPE_BASE = 1000000.0
HIGH = lax.Precision.HIGHEST

@jax.custom_vjp
def low(v):
    return lax.optimization_barrier(v.astype(jnp.bfloat16)).astype(jnp.float32)

@jax.custom_vjp
def low_back(v):
    return v

def low_keep(v):
    return (low(v), None)

def low_pass(kept, grad):
    return (grad,)

def back_keep(v):
    return (v, None)

def back_low(kept, grad):
    return (low(grad),)
low.defvjp(low_keep, low_pass)
low_back.defvjp(back_keep, back_low)

def rms_scale(values, gain):
    return values * lax.rsqrt(lax.optimization_barrier(jnp.mean(values * values, axis=-1, keepdims=True)) + EPS) * gain

def rotate(values, cosines, sines):
    half_size = values.shape[-1] // 2
    first_half = values[..., :half_size]
    second_half = values[..., half_size:]
    return jnp.concatenate([first_half * cosines - second_half * sines, second_half * cosines + first_half * sines], axis=-1)

def rope_tables(positions, head_width):
    half_size = head_width // 2
    inverse = ROPE_BASE ** (-(2.0 * jnp.arange(half_size, dtype=jnp.float32)) / head_width)
    angles = positions.astype(jnp.float32)[..., None] * inverse
    return (jnp.cos(angles)[..., None, :], jnp.sin(angles)[..., None, :])

def normed_rotary(raw_values, gain, cosines, sines):
    return rotate(rms_scale(raw_values, gain), cosines, sines)

def project(values, weight):
    return jnp.einsum('slc,cw->slw', values, weight, precision=HIGH)

def attend(queries, keys_in, values):
    length = queries.shape[0]
    groups = queries.shape[1] // keys_in.shape[1]
    keys_all = jnp.repeat(keys_in, groups, axis=1)
    values_all = jnp.repeat(values, groups, axis=1)
    products = low_back(jnp.einsum('qhd,khd->hqk', queries, keys_all, precision=HIGH))
    row_index = lax.broadcasted_iota(jnp.int32, (length, length), 0)
    col_index = lax.broadcasted_iota(jnp.int32, (length, length), 1)
    scores = jnp.where(row_index >= col_index, products * queries.shape[2] ** (-0.5), -1e+30)
    peaks = lax.optimization_barrier(jnp.max(scores, axis=-1, keepdims=True))
    lifted = jnp.exp(scores - peaks)
    chances = low(lifted / lax.optimization_barrier(jnp.sum(lifted, axis=-1, keepdims=True)))
    return low_back(jnp.einsum('hqk,khd->qhd', chances, values_all, precision=HIGH))

def layer(params, inputs, cosines, sines):
    query_w, key_w, value_w, logit_w, output_w, gate_w, up_w, down_projection_weight, first_gain, second_gain, query_norm_scale, key_gain = params
    seq_count, length = (inputs.shape[0], inputs.shape[1])
    first = low(rms_scale(inputs, first_gain))
    query_unnormed = low_back(project(first, query_w)).reshape(seq_count, length, -1, HEAD)
    key_raw = low_back(project(first, key_w)).reshape(seq_count, length, -1, HEAD)
    queries = low(low_back(normed_rotary(query_unnormed, query_norm_scale, cosines, sines)))
    keys_all = low(low_back(normed_rotary(key_raw, key_gain, cosines, sines)))
    values = low(low_back(project(first, value_w))).reshape(seq_count, length, -1, HEAD)
    logits = low(low_back(project(first, logit_w))).reshape(seq_count, length, -1, HEAD)
    mixture = lax.map(jax.checkpoint(lambda pieces: attend(pieces[0], pieces[1], pieces[2])), (queries, keys_all, values))
    gated = low(low_back(mixture * jax.nn.sigmoid(logits))).reshape(seq_count, length, -1)
    middle = inputs + low_back(project(gated, output_w))
    second = low(rms_scale(middle, second_gain))
    gate_act = low_back(project(second, gate_w))
    up_act = low_back(project(second, up_w))
    hidden = low(jax.nn.silu(gate_act) * up_act)
    return middle + low_back(project(hidden, down_projection_weight))

def reference(tokens, cotangent, positions, domain_ids, counts, loss_weight, domain_weights, q_weight, k_weight, v_weight, g_weight, o_weight, gate_weight, up_weight, down_weight, attn_gain, mlp_gain, q_gain, k_gain):
    params = tuple((weight.astype(jnp.float32) for weight in (q_weight, k_weight, v_weight, g_weight, o_weight, gate_weight, up_weight, down_weight, attn_gain, mlp_gain, q_gain, k_gain)))
    seq_scale = loss_weight.astype(jnp.float32) * domain_weights.astype(jnp.float32)[domain_ids] * SEQ_LEN / counts.astype(jnp.float32)
    group_size = SEQS_DEV
    batches = SEQUENCES // group_size

    def regroup(array):
        return array.reshape((batches, group_size) + array.shape[1:])

    def advance(totals, pieces):
        inputs, upstream, places, scales = pieces
        cosines, sines = rope_tables(places, HEAD)
        result, pullback = jax.vjp(lambda weights, values: layer(weights, values, cosines, sines), params, inputs)
        grad_params, grad_inputs = pullback(upstream * scales[:, None, None])
        return (jax.tree.map(jnp.add, totals, grad_params), (result.astype(jnp.bfloat16), grad_inputs))
    initial = jax.tree.map(jnp.zeros_like, params)
    totals, (outputs, grads) = lax.scan(advance, initial, (regroup(tokens.astype(jnp.float32)), regroup(cotangent.astype(jnp.float32)), regroup(positions), regroup(seq_scale)))
    return (outputs.reshape(tokens.shape), grads.reshape(tokens.shape), totals[0], totals[1], totals[2], totals[3], totals[4], totals[5], totals[6], totals[7], totals[8], totals[9], totals[10], totals[11])
```

```python
import functools

import jax
import jax.numpy as jnp
from jax import lax
from jax.experimental import pallas as pl
from jax.experimental.pallas import tpu as pltpu
from jax.sharding import PartitionSpec as P

HEAD = 128
HALF = HEAD // 2
SEQ_LEN = 1024
EPS = 1e-06
ROPE_BASE = 1000000.0
SCALE = HEAD ** (-0.5)
LOG2E = 1.4426950408889634
VMEM_LIMIT = 56 * 1024 * 1024
NT = (((1,), (1,)), ((), ()))
NN = (((1,), (0,)), ((), ()))
TN = (((0,), (0,)), ((), ()))
F32 = jnp.float32
BF16 = jnp.bfloat16


def mm(left, right, dims=NN):
    return lax.dot_general(left, right, dims, preferred_element_type=F32)


def head_norm(raw):
    return lax.rsqrt(jnp.mean(raw * raw, axis=-1, keepdims=True) + EPS)


def turn(values, cosines, sines):
    return values * cosines + pltpu.roll(values, HALF, 1) * sines


def turn_back(values, cosines, sines):
    return values * cosines - pltpu.roll(values, HALF, 1) * sines


def norm_turn(raw, gain, cosines, sines):
    return turn(raw * head_norm(raw) * gain, cosines, sines).astype(BF16)


def norm_turn_back(raw, gain, grad, cosines, sines):
    back = turn_back(grad, cosines, sines)
    scale = head_norm(raw)
    pulled = back * gain
    inner = jnp.mean(raw * pulled, axis=-1, keepdims=True)
    gain_part = jnp.sum(raw * scale * back, axis=0, keepdims=True)
    return scale * pulled - raw * (scale * scale * scale * inner), gain_part


def diagonal_mask(rows, groups):
    keys = lax.broadcasted_iota(jnp.int32, (rows, groups * rows), 0)
    places = lax.broadcasted_iota(jnp.int32, (rows, groups * rows), 1)
    return keys <= lax.rem(places, rows)


def row_block(block, rank, rows):
    return pl.ds(pl.multiple_of(jnp.bitwise_xor(block, rank) * rows, rows), rows)


def attend_fwd_kernel(
    blocks, rows, groups,
    rank_ref, q_ref, k_ref, v_ref, g_ref, cos_ref, sin_ref, qg_ref, kg_ref,
    gated_ref, mix_ref, lse_ref, keys, vals_t,
):
    rank = rank_ref[0]
    factor = SCALE * LOG2E
    for a in range(blocks):
        place = row_block(a, rank, rows)
        here = slice(a * rows, (a + 1) * rows)
        keys[here, :] = norm_turn(k_ref[place, :], kg_ref[...], cos_ref[place, :], sin_ref[place, :])
        vals_t[:, here] = v_ref[place, :].T.astype(BF16)
    mask = diagonal_mask(rows, groups)
    for a in range(blocks):
        place = row_block(a, rank, rows)
        cosines, sines = cos_ref[place, :], sin_ref[place, :]
        queries = jnp.concatenate(
            [
                norm_turn(q_ref[place, h * HEAD : (h + 1) * HEAD], qg_ref[...], cosines, sines)
                for h in range(groups)
            ],
            axis=0,
        )
        low, high = a * rows, (a + 1) * rows
        near = jnp.where(mask, mm(keys[low:high, :], queries, NT), -1e30)
        peak = jnp.max(near, axis=0, keepdims=True)
        if a:
            far = mm(keys[:low, :], queries, NT)
            peak = jnp.maximum(peak, jnp.max(far, axis=0, keepdims=True))
        near = jnp.exp2((near - peak) * factor)
        total = jnp.sum(near, axis=0, keepdims=True)
        if a:
            far = jnp.exp2((far - peak) * factor)
            total = total + jnp.sum(far, axis=0, keepdims=True)
        inverse = 1.0 / total
        mix_t = mm(vals_t[:, low:high], (near * inverse).astype(BF16))
        if a:
            mix_t = mix_t + mm(vals_t[:, :low], (far * inverse).astype(BF16))
        mix = mix_t.T
        for h in range(groups):
            cols = slice(h * HEAD, (h + 1) * HEAD)
            part = mix[h * rows : (h + 1) * rows, :]
            opening = jax.nn.sigmoid(g_ref[place, cols].astype(BF16).astype(F32))
            mix_ref[place, cols] = part
            gated_ref[place, cols] = (part * opening).astype(BF16)
        lse_ref[0, a : a + 1, :] = peak * factor + jnp.log2(total)


def attend_bwd_kernel(
    blocks, rows, groups, kv_local,
    rank_ref, q_ref, k_ref, v_ref, g_ref, cos_ref, sin_ref, qg_ref, kg_ref, mix_ref, lse_ref, up_ref,
    grad_ref, qgain_ref, kgain_ref, keys, keys_t, vals, dkeys, dvals,
):
    rank = rank_ref[0]
    step = pl.program_id(0)
    factor = SCALE * LOG2E
    width = groups * HEAD

    @pl.when(step == 0)
    def _():
        qgain_ref[...] = jnp.zeros_like(qgain_ref)
        kgain_ref[...] = jnp.zeros_like(kgain_ref)

    for a in range(blocks):
        place = row_block(a, rank, rows)
        here = slice(a * rows, (a + 1) * rows)
        block = norm_turn(k_ref[place, :], kg_ref[...], cos_ref[place, :], sin_ref[place, :])
        keys[here, :] = block
        keys_t[:, here] = block.astype(F32).T.astype(BF16)
        vals[here, :] = v_ref[place, :].astype(BF16)
    mask = diagonal_mask(rows, groups)
    qgain = jnp.zeros((1, HEAD), F32)
    for a in reversed(range(blocks)):
        place = row_block(a, rank, rows)
        cosines, sines = cos_ref[place, :], sin_ref[place, :]
        queries, grads = [], []
        for h in range(groups):
            cols = slice(h * HEAD, (h + 1) * HEAD)
            queries.append(norm_turn(q_ref[place, cols], qg_ref[...], cosines, sines))
            upstream = up_ref[place, cols].astype(F32)
            opening = jax.nn.sigmoid(g_ref[place, cols].astype(BF16).astype(F32))
            opened = upstream * opening
            grads.append(opened.astype(BF16))
            grad_ref[
                place, pl.ds((kv_local * (groups + 2)) * HEAD + step * width + h * HEAD, HEAD)
            ] = (opened * mix_ref[place, cols] * (1.0 - opening)).astype(BF16)
        queries = jnp.concatenate(queries, axis=0)
        grads = jnp.concatenate(grads, axis=0)
        lse = lse_ref[0, a : a + 1, :]
        low, high = a * rows, (a + 1) * rows
        spans = [(low, high)] + ([(0, low)] if a else [])
        chances, grad_chances = [], []
        centre = jnp.zeros((1, groups * rows), F32)
        for start, stop in spans:
            part = jnp.exp2(mm(keys[start:stop, :], queries, NT) * factor - lse)
            if start == low:
                part = jnp.where(mask, part, 0.0)
            pull = mm(vals[start:stop, :], grads, NT)
            centre = centre + jnp.sum(part * pull, axis=0, keepdims=True)
            chances.append(part)
            grad_chances.append(pull)
        dq_t = jnp.zeros((HEAD, groups * rows), F32)
        for (start, stop), part, pull in zip(spans, chances, grad_chances):
            grad_products = (part * (pull - centre) * SCALE).astype(BF16)
            dval = mm(part.astype(BF16), grads)
            dkey = mm(grad_products, queries)
            if a == blocks - 1:
                dvals[start:stop, :] = dval
                dkeys[start:stop, :] = dkey
            else:
                dvals[start:stop, :] += dval
                dkeys[start:stop, :] += dkey
            dq_t = dq_t + mm(keys_t[:, start:stop], grad_products)
        dq = dq_t.T
        for h in range(groups):
            grad = dq[h * rows : (h + 1) * rows, :].astype(BF16).astype(F32)
            cols = slice(h * HEAD, (h + 1) * HEAD)
            raw, gain_part = norm_turn_back(q_ref[place, cols], qg_ref[...], grad, cosines, sines)
            grad_ref[place, pl.ds(step * width + h * HEAD, HEAD)] = raw.astype(BF16)
            qgain = qgain + gain_part
    kgain = jnp.zeros((1, HEAD), F32)
    for a in range(blocks):
        place = row_block(a, rank, rows)
        here = slice(a * rows, (a + 1) * rows)
        grad = dkeys[here, :].astype(BF16).astype(F32)
        raw, gain_part = norm_turn_back(
            k_ref[place, :], kg_ref[...], grad, cos_ref[place, :], sin_ref[place, :]
        )
        kgain = kgain + gain_part
        grad_ref[place, pl.ds(kv_local * width + step * HEAD, HEAD)] = raw.astype(BF16)
        grad_ref[place, pl.ds(kv_local * (width + HEAD) + step * HEAD, HEAD)] = dvals[
            here, :
        ].astype(BF16)
    qgain_ref[...] += qgain
    kgain_ref[...] += kgain


def attention_specs(length, groups, kv_local):
    width = groups * HEAD
    return [
        pl.BlockSpec((length, width), lambda g, r: (0, g)),
        pl.BlockSpec((length, HEAD), lambda g, r: (0, kv_local * groups + g)),
        pl.BlockSpec((length, HEAD), lambda g, r: (0, kv_local * (groups + 1) + g)),
        pl.BlockSpec((length, width), lambda g, r: (0, kv_local * (groups + 2) // groups + g)),
        pl.BlockSpec((length, HEAD), lambda g, r: (0, 0)),
        pl.BlockSpec((length, HEAD), lambda g, r: (0, 0)),
        pl.BlockSpec((1, HEAD), lambda g, r: (0, 0)),
        pl.BlockSpec((1, HEAD), lambda g, r: (0, 0)),
    ]


def attend_forward(rank, raw, cosines, sines, q_gain, k_gain, blocks, groups, kv_local):
    length = raw.shape[0]
    rows = length // blocks
    width = groups * HEAD
    flops = 4 * kv_local * groups * length * length * HEAD * (blocks + 1) // (2 * blocks)
    return pl.pallas_call(
        functools.partial(attend_fwd_kernel, blocks, rows, groups),
        grid_spec=pltpu.PrefetchScalarGridSpec(
            num_scalar_prefetch=1,
            grid=(kv_local,),
            in_specs=attention_specs(length, groups, kv_local),
            out_specs=[
                pl.BlockSpec((length, width), lambda g, r: (0, g)),
                pl.BlockSpec((length, width), lambda g, r: (0, g)),
                pl.BlockSpec((1, blocks, groups * rows), lambda g, r: (g, 0, 0)),
            ],
            scratch_shapes=[pltpu.VMEM((length, HEAD), BF16), pltpu.VMEM((HEAD, length), BF16)],
        ),
        out_shape=[
            jax.ShapeDtypeStruct((length, kv_local * width), BF16),
            jax.ShapeDtypeStruct((length, kv_local * width), F32),
            jax.ShapeDtypeStruct((kv_local, blocks, groups * rows), F32),
        ],
        compiler_params=pltpu.CompilerParams(
            dimension_semantics=("arbitrary",), vmem_limit_bytes=VMEM_LIMIT
        ),
        cost_estimate=pl.CostEstimate(
            flops=4 * flops,
            bytes_accessed=raw.size * 4 + length * kv_local * width * 6,
            transcendentals=kv_local * groups * length * length // 2,
        ),
        name="attend_forward",
    )(rank, raw, raw, raw, raw, cosines, sines, q_gain, k_gain)


def attend_backward(
    rank, raw, cosines, sines, q_gain, k_gain, mix, lse, upstream, blocks, groups, kv_local
):
    length = raw.shape[0]
    rows = length // blocks
    width = groups * HEAD
    flops = 10 * kv_local * groups * length * length * HEAD * (blocks + 1) // (2 * blocks)
    return pl.pallas_call(
        functools.partial(attend_bwd_kernel, blocks, rows, groups, kv_local),
        grid_spec=pltpu.PrefetchScalarGridSpec(
            num_scalar_prefetch=1,
            grid=(kv_local,),
            in_specs=attention_specs(length, groups, kv_local)
            + [
                pl.BlockSpec((length, width), lambda g, r: (0, g)),
                pl.BlockSpec((1, blocks, groups * rows), lambda g, r: (g, 0, 0)),
                pl.BlockSpec((length, width), lambda g, r: (0, g)),
            ],
            out_specs=[
                pl.BlockSpec(raw.shape, lambda g, r: (0, 0)),
                pl.BlockSpec((1, HEAD), lambda g, r: (0, 0)),
                pl.BlockSpec((1, HEAD), lambda g, r: (0, 0)),
            ],
            scratch_shapes=[
                pltpu.VMEM((length, HEAD), BF16),
                pltpu.VMEM((HEAD, length), BF16),
                pltpu.VMEM((length, HEAD), BF16),
                pltpu.VMEM((length, HEAD), F32),
                pltpu.VMEM((length, HEAD), F32),
            ],
        ),
        out_shape=[
            jax.ShapeDtypeStruct(raw.shape, BF16),
            jax.ShapeDtypeStruct((1, HEAD), F32),
            jax.ShapeDtypeStruct((1, HEAD), F32),
        ],
        compiler_params=pltpu.CompilerParams(
            dimension_semantics=("arbitrary",), vmem_limit_bytes=VMEM_LIMIT
        ),
        cost_estimate=pl.CostEstimate(
            flops=4 * flops,
            bytes_accessed=raw.size * 6 + length * kv_local * width * 6,
            transcendentals=kv_local * groups * length * length // 2,
        ),
        name="attend_backward",
    )(rank, raw, raw, raw, raw, cosines, sines, q_gain, k_gain, mix, lse, upstream)


def swap(values, bit, axis="sp"):
    return lax.ppermute(values, axis, [(i, i ^ bit) for i in range(lax.axis_size(axis))])


def gather_blocks(block):
    count = lax.axis_size("sp")
    if count != 4:
        return [block] + [swap(block, j) for j in range(1, count)]
    half = block.shape[0] // 2
    along_x, along_y = swap(block, 1), swap(block, 2)
    corner = jnp.concatenate([swap(along_y[:half], 1), swap(along_x[half:], 2)], axis=0)
    return [block, along_x, along_y, corner]


def scatter_sum(parts):
    count = lax.axis_size("sp")
    if count != 4:
        total = parts[0]
        for j in range(1, count):
            total = total + swap(parts[j].astype(BF16), j).astype(F32)
        return total
    half = parts[0].shape[0] // 2
    corner = parts[3].astype(BF16)
    from_x, from_y = swap(corner[:half], 1), swap(corner[half:], 2)
    to_y = jnp.concatenate([parts[2][:half] + from_x.astype(F32), parts[2][half:]], axis=0)
    to_x = jnp.concatenate([parts[1][:half], parts[1][half:] + from_y.astype(F32)], axis=0)
    return (
        parts[0]
        + swap(to_x.astype(BF16), 1).astype(F32)
        + swap(to_y.astype(BF16), 2).astype(F32)
    )


def row_parts(make, count, rows):
    if count != 4:
        whole = make(0, count * rows)
        return [whole[j * rows : (j + 1) * rows] for j in range(count)]
    corner = make(3 * rows, 4 * rows)
    middle = make(rows, 3 * rows)
    own = make(0, rows)
    return [own, middle[:rows], middle[rows:], corner]


def place_blocks(blocks, rank, axis):
    size = blocks[0].shape[axis]
    shape = list(blocks[0].shape)
    shape[axis] = size * len(blocks)
    whole = jnp.zeros(shape, blocks[0].dtype)
    for j, block in enumerate(blocks):
        whole = lax.dynamic_update_slice_in_dim(
            whole, block, jnp.bitwise_xor(rank, j) * size, axis
        )
    return whole


def sum_all(values):
    for axis in ("sp", "fsdp"):
        bit = 1
        while bit < lax.axis_size(axis):
            values = values + swap(values, bit, axis)
            bit *= 2
    return values


def rms_back(values, gain, grad):
    scale = lax.rsqrt(jnp.mean(values * values, axis=-1, keepdims=True) + EPS)
    pulled = grad * gain
    inner = jnp.mean(values * pulled, axis=-1, keepdims=True)
    return (
        scale * pulled - values * (scale * scale * scale * inner),
        jnp.sum(values * scale * grad, axis=0),
    )


def rms_low(values, gain):
    scale = lax.rsqrt(jnp.mean(values * values, axis=-1, keepdims=True) + EPS)
    return (values * scale * gain).astype(BF16)


def on_device(
    tokens, cotangent, positions, domain_ids, counts, loss_weight, domain_weights,
    q_weight, k_weight, v_weight, g_weight, o_weight, gate_weight, up_weight, down_weight,
    attn_gain, mlp_gain, q_gain, k_gain,
):
    count, shards = lax.axis_size("sp"), lax.axis_size("fsdp")
    rank, shard = lax.axis_index("sp"), lax.axis_index("fsdp")
    rank_ref = rank.astype(jnp.int32).reshape(1)
    _, rows, width = tokens.shape
    heads_local = q_weight.shape[1] // HEAD // count
    kv_local = k_weight.shape[1] // HEAD // count
    groups = heads_local // kv_local
    qcols, kcols = heads_local * HEAD, kv_local * HEAD
    dcols = width // count
    units = down_weight.shape[0] // count
    ffs = units * shards

    def columns(weight, size):
        return lax.dynamic_slice_in_dim(weight, rank * size, size, 1)

    def gather(weight):
        return lax.all_gather(weight, "fsdp", axis=0, tiled=True)

    def unit_columns(weight):
        spread = weight.reshape(weight.shape[0], shards, count, units)
        return lax.dynamic_slice_in_dim(spread, rank, 1, 2).reshape(weight.shape[0], ffs)

    attn_share = jnp.concatenate(
        [
            columns(q_weight, qcols), columns(k_weight, kcols), columns(v_weight, kcols),
            columns(g_weight, qcols), columns(o_weight, dcols),
        ],
        axis=1,
    )
    attn_full = gather(attn_share)
    in_cols = 2 * (qcols + kcols)
    w_in = attn_full[:, :in_cols]
    o_slices = attn_full[:, in_cols:].reshape(count, qcols, dcols)
    w_out = place_blocks(
        [
            swap(lax.dynamic_index_in_dim(o_slices, jnp.bitwise_xor(rank, j), 0, False), j)
            if j
            else lax.dynamic_index_in_dim(o_slices, rank, 0, False)
            for j in range(count)
        ],
        rank,
        1,
    )
    gateup = gather(jnp.concatenate([unit_columns(gate_weight), unit_columns(up_weight)], axis=1))
    w_gate, w_up = gateup[:, :ffs], gateup[:, ffs:]
    w_down = gather(lax.dynamic_slice_in_dim(down_weight, rank * units, units, 0))

    gains = lax.all_gather(
        jnp.concatenate([attn_gain, mlp_gain, q_gain, k_gain]), "fsdp", axis=0
    ).astype(F32)
    part = attn_gain.shape[0]
    first_gain = gains[:, :part].reshape(-1)
    second_gain = gains[:, part : 2 * part].reshape(-1)
    piece = q_gain.shape[0]
    query_gain = gains[:, 2 * part : 2 * part + piece].reshape(1, HEAD)
    key_gain = gains[:, 2 * part + piece :].reshape(1, HEAD)

    onehot = (domain_ids[:, None] == jnp.arange(domain_weights.shape[0], dtype=jnp.int32)).astype(F32)
    seq_scale = loss_weight * jnp.sum(onehot * domain_weights[None, :], axis=1) * SEQ_LEN
    seq_scale = (seq_scale / counts.astype(F32))[0]
    upstream = cotangent[0].astype(F32) * seq_scale
    inputs = tokens[0].astype(F32)
    tokens_all = jnp.concatenate(gather_blocks(tokens[0]), axis=0)
    places = jnp.concatenate([positions[0]] + [swap(positions[0], j) for j in range(1, count)])
    upstream_all = jnp.concatenate(gather_blocks(upstream.astype(BF16)), axis=0)

    inverse = ROPE_BASE ** (-(2.0 * jnp.arange(HALF, dtype=F32)) / HEAD)
    angles = places.astype(F32)[:, None] * inverse
    cosines, sines = jnp.cos(angles), jnp.sin(angles)
    cosines = jnp.concatenate([cosines, cosines], axis=1)
    sines = jnp.concatenate([-sines, sines], axis=1)

    first = rms_low(tokens_all.astype(F32), first_gain)
    raw = mm(first, w_in)
    gated, mix, lse = attend_forward(
        rank_ref, raw, cosines, sines, query_gain, key_gain, count, groups, kv_local
    )
    middle = inputs + scatter_sum(
        row_parts(lambda lo, hi: mm(gated[lo:hi], w_out), count, rows)
    )
    second = jnp.concatenate(gather_blocks(rms_low(middle, second_gain)), axis=0)

    gate_act = mm(second, w_gate)
    up_act = mm(second, w_up)
    opening = jax.nn.sigmoid(gate_act)
    silu = gate_act * opening
    hidden = (silu * up_act).astype(BF16)
    block_out = (
        middle + scatter_sum(row_parts(lambda lo, hi: mm(hidden[lo:hi], w_down), count, rows))
    ).astype(BF16)
    grad_hidden = mm(upstream_all, w_down, NT)
    grad_gate = (grad_hidden * up_act * opening * (1.0 + gate_act * (1.0 - opening))).astype(BF16)
    grad_up = (grad_hidden * silu).astype(BF16)
    grad_second = scatter_sum(
        row_parts(
            lambda lo, hi: mm(grad_gate[lo:hi], w_gate, NT) + mm(grad_up[lo:hi], w_up, NT),
            count,
            rows,
        )
    )
    pulled, second_gain_part = rms_back(middle, second_gain, grad_second)
    grad_middle = upstream + pulled

    grad_attn = jnp.concatenate(gather_blocks(grad_middle.astype(BF16)), axis=0)
    grad_gated = mm(grad_attn, w_out, NT).astype(BF16)
    grad_raw, query_gain_part, key_gain_part = attend_backward(
        rank_ref, raw, cosines, sines, query_gain, key_gain, mix, lse, grad_gated,
        count, groups, kv_local,
    )
    grad_first = scatter_sum(row_parts(lambda lo, hi: mm(grad_raw[lo:hi], w_in, NT), count, rows))
    pulled, first_gain_part = rms_back(inputs, first_gain, grad_first)
    input_grad = grad_middle + pulled

    def scatter(grad):
        return lax.psum_scatter(grad.astype(BF16), "fsdp", scatter_dimension=0, tiled=True)

    down_share = scatter(mm(hidden, upstream_all, TN))
    gateup_share = scatter(
        jnp.concatenate([mm(second, grad_gate, TN), mm(second, grad_up, TN)], axis=1).astype(BF16)
    )
    out_grad = mm(gated, grad_attn, TN).astype(BF16)
    out_slices = jnp.stack([out_grad[:, j * dcols : (j + 1) * dcols] for j in range(count)])
    out_grad = place_blocks(
        [
            swap(lax.dynamic_index_in_dim(out_slices, jnp.bitwise_xor(rank, j), 0, False), j)
            if j
            else lax.dynamic_index_in_dim(out_slices, rank, 0, False)
            for j in range(count)
        ],
        rank,
        0,
    )
    attn_shares = scatter(
        jnp.concatenate([mm(first, grad_raw, TN).astype(BF16), out_grad], axis=1)
    )

    down_grad = place_blocks(gather_blocks(down_share), rank, 0).astype(F32)
    gateup_blocks = gather_blocks(gateup_share)
    gateup_all = jnp.stack(gateup_blocks).reshape(count, -1, 2, shards, units)
    order = jnp.bitwise_xor(jnp.arange(count), rank)
    gateup_all = jnp.transpose(jnp.take(gateup_all, order, axis=0), (2, 1, 3, 0, 4)).reshape(
        2, gate_weight.shape[0], -1
    )
    attn_blocks = gather_blocks(attn_shares)

    def attn_grad(start, size):
        return place_blocks([b[:, start : start + size] for b in attn_blocks], rank, 1).astype(F32)

    total = sum_all(
        jnp.concatenate([first_gain_part, query_gain_part[0], key_gain_part[0], second_gain_part])
    )

    def own(values):
        size = values.shape[0] // shards
        return lax.dynamic_slice_in_dim(values, shard * size, size, 0)

    return (
        block_out[None],
        input_grad[None],
        attn_grad(0, qcols),
        attn_grad(qcols, kcols),
        attn_grad(qcols + kcols, kcols),
        attn_grad(qcols + 2 * kcols, qcols),
        attn_grad(in_cols, dcols),
        gateup_all[0].astype(F32),
        gateup_all[1].astype(F32),
        down_grad,
        own(total[:width]),
        own(total[width + 2 * HEAD :]),
        own(total[width : width + HEAD]),
        own(total[width + HEAD : width + 2 * HEAD]),
    )


def solution(mesh):
    both, over_fsdp = P("fsdp", "sp", None), P("fsdp", None)
    return jax.shard_map(
        on_device,
        mesh=mesh,
        in_specs=(both, both, P("fsdp", "sp"), P("fsdp"), P("fsdp"), P("fsdp"), P())
        + (over_fsdp,) * 8
        + (P("fsdp"),) * 4,
        out_specs=(both, both) + (over_fsdp,) * 8 + (P("fsdp"),) * 4,
        check_vma=False,
    )
```

```python
import functools

import jax
import jax.numpy as jnp
from jax import lax
from jax.experimental import pallas as pl
from jax.experimental.pallas import tpu as pltpu
from jax.sharding import PartitionSpec as P

HEAD = 128
HALF = HEAD // 2
SEQ_LEN = 1024
EPS = 1e-06
ROPE_BASE = 1000000.0
SCALE = HEAD ** (-0.5)
LOG2E = 1.4426950408889634
VMEM_LIMIT = 56 * 1024 * 1024
NT = (((1,), (1,)), ((), ()))
NN = (((1,), (0,)), ((), ()))
TN = (((0,), (0,)), ((), ()))
F32 = jnp.float32
BF16 = jnp.bfloat16


def mm(left, right, dims=NN):
    return lax.dot_general(left, right, dims, preferred_element_type=F32)


def head_norm(raw):
    return lax.rsqrt(jnp.mean(raw * raw, axis=-1, keepdims=True) + EPS)


def turn(values, cosines, sines):
    return values * cosines + pltpu.roll(values, HALF, 1) * sines


def turn_back(values, cosines, sines):
    return values * cosines - pltpu.roll(values, HALF, 1) * sines


def norm_turn(raw, gain, cosines, sines):
    return turn(raw * head_norm(raw) * gain, cosines, sines).astype(BF16)


def norm_turn_back(raw, gain, grad, cosines, sines):
    back = turn_back(grad, cosines, sines)
    scale = head_norm(raw)
    pulled = back * gain
    inner = jnp.mean(raw * pulled, axis=-1, keepdims=True)
    gain_part = jnp.sum(raw * scale * back, axis=0, keepdims=True)
    return scale * pulled - raw * (scale * scale * scale * inner), gain_part


def diagonal_mask(rows, groups):
    keys = lax.broadcasted_iota(jnp.int32, (rows, groups * rows), 0)
    places = lax.broadcasted_iota(jnp.int32, (rows, groups * rows), 1)
    return keys <= lax.rem(places, rows)


def row_block(block, rank, rows):
    return pl.ds(pl.multiple_of(jnp.bitwise_xor(block, rank) * rows, rows), rows)


def attend_fwd_kernel(
    blocks, rows, groups,
    rank_ref, q_ref, k_ref, v_ref, g_ref, cos_ref, sin_ref, qg_ref, kg_ref,
    gated_ref, mix_ref, lse_ref, keys, vals_t,
):
    rank = rank_ref[0]
    factor = SCALE * LOG2E
    for a in range(blocks):
        place = row_block(a, rank, rows)
        here = slice(a * rows, (a + 1) * rows)
        keys[here, :] = norm_turn(k_ref[place, :], kg_ref[...], cos_ref[place, :], sin_ref[place, :])
        vals_t[:, here] = v_ref[place, :].T.astype(BF16)
    mask = diagonal_mask(rows, groups)
    for a in range(blocks):
        place = row_block(a, rank, rows)
        cosines, sines = cos_ref[place, :], sin_ref[place, :]
        queries = jnp.concatenate(
            [
                norm_turn(q_ref[place, h * HEAD : (h + 1) * HEAD], qg_ref[...], cosines, sines)
                for h in range(groups)
            ],
            axis=0,
        )
        low, high = a * rows, (a + 1) * rows
        near = jnp.where(mask, mm(keys[low:high, :], queries, NT), -1e30)
        peak = jnp.max(near, axis=0, keepdims=True)
        if a:
            far = mm(keys[:low, :], queries, NT)
            peak = jnp.maximum(peak, jnp.max(far, axis=0, keepdims=True))
        near = jnp.exp2((near - peak) * factor)
        total = jnp.sum(near, axis=0, keepdims=True)
        if a:
            far = jnp.exp2((far - peak) * factor)
            total = total + jnp.sum(far, axis=0, keepdims=True)
        inverse = 1.0 / total
        mix_t = mm(vals_t[:, low:high], (near * inverse).astype(BF16))
        if a:
            mix_t = mix_t + mm(vals_t[:, :low], (far * inverse).astype(BF16))
        mix = mix_t.T
        for h in range(groups):
            cols = slice(h * HEAD, (h + 1) * HEAD)
            part = mix[h * rows : (h + 1) * rows, :]
            opening = jax.nn.sigmoid(g_ref[place, cols].astype(BF16).astype(F32))
            mix_ref[place, cols] = part
            gated_ref[place, cols] = (part * opening).astype(BF16)
        lse_ref[0, a : a + 1, :] = peak * factor + jnp.log2(total)


def attend_bwd_kernel(
    blocks, rows, groups, kv_local,
    rank_ref, q_ref, k_ref, v_ref, g_ref, cos_ref, sin_ref, qg_ref, kg_ref, mix_ref, lse_ref, up_ref,
    grad_ref, qgain_ref, kgain_ref, keys, keys_t, vals, dkeys, dvals,
):
    rank = rank_ref[0]
    step = pl.program_id(0)
    factor = SCALE * LOG2E
    width = groups * HEAD

    @pl.when(step == 0)
    def _():
        qgain_ref[...] = jnp.zeros_like(qgain_ref)
        kgain_ref[...] = jnp.zeros_like(kgain_ref)

    for a in range(blocks):
        place = row_block(a, rank, rows)
        here = slice(a * rows, (a + 1) * rows)
        block = norm_turn(k_ref[place, :], kg_ref[...], cos_ref[place, :], sin_ref[place, :])
        keys[here, :] = block
        keys_t[:, here] = block.astype(F32).T.astype(BF16)
        vals[here, :] = v_ref[place, :].astype(BF16)
    mask = diagonal_mask(rows, groups)
    qgain = jnp.zeros((1, HEAD), F32)
    for a in reversed(range(blocks)):
        place = row_block(a, rank, rows)
        cosines, sines = cos_ref[place, :], sin_ref[place, :]
        queries, grads = [], []
        for h in range(groups):
            cols = slice(h * HEAD, (h + 1) * HEAD)
            queries.append(norm_turn(q_ref[place, cols], qg_ref[...], cosines, sines))
            upstream = up_ref[place, cols].astype(F32)
            opening = jax.nn.sigmoid(g_ref[place, cols].astype(BF16).astype(F32))
            opened = upstream * opening
            grads.append(opened.astype(BF16))
            grad_ref[
                place, pl.ds((kv_local * (groups + 2)) * HEAD + step * width + h * HEAD, HEAD)
            ] = (opened * mix_ref[place, cols] * (1.0 - opening)).astype(BF16)
        queries = jnp.concatenate(queries, axis=0)
        grads = jnp.concatenate(grads, axis=0)
        lse = lse_ref[0, a : a + 1, :]
        low, high = a * rows, (a + 1) * rows
        spans = [(low, high)] + ([(0, low)] if a else [])
        chances, grad_chances = [], []
        centre = jnp.zeros((1, groups * rows), F32)
        for start, stop in spans:
            part = jnp.exp2(mm(keys[start:stop, :], queries, NT) * factor - lse)
            if start == low:
                part = jnp.where(mask, part, 0.0)
            pull = mm(vals[start:stop, :], grads, NT)
            centre = centre + jnp.sum(part * pull, axis=0, keepdims=True)
            chances.append(part)
            grad_chances.append(pull)
        dq_t = jnp.zeros((HEAD, groups * rows), F32)
        for (start, stop), part, pull in zip(spans, chances, grad_chances):
            grad_products = (part * (pull - centre) * SCALE).astype(BF16)
            dval = mm(part.astype(BF16), grads)
            dkey = mm(grad_products, queries)
            if a == blocks - 1:
                dvals[start:stop, :] = dval
                dkeys[start:stop, :] = dkey
            else:
                dvals[start:stop, :] += dval
                dkeys[start:stop, :] += dkey
            dq_t = dq_t + mm(keys_t[:, start:stop], grad_products)
        dq = dq_t.T
        for h in range(groups):
            grad = dq[h * rows : (h + 1) * rows, :].astype(BF16).astype(F32)
            cols = slice(h * HEAD, (h + 1) * HEAD)
            raw, gain_part = norm_turn_back(q_ref[place, cols], qg_ref[...], grad, cosines, sines)
            grad_ref[place, pl.ds(step * width + h * HEAD, HEAD)] = raw.astype(BF16)
            qgain = qgain + gain_part
    kgain = jnp.zeros((1, HEAD), F32)
    for a in range(blocks):
        place = row_block(a, rank, rows)
        here = slice(a * rows, (a + 1) * rows)
        grad = dkeys[here, :].astype(BF16).astype(F32)
        raw, gain_part = norm_turn_back(
            k_ref[place, :], kg_ref[...], grad, cos_ref[place, :], sin_ref[place, :]
        )
        kgain = kgain + gain_part
        grad_ref[place, pl.ds(kv_local * width + step * HEAD, HEAD)] = raw.astype(BF16)
        grad_ref[place, pl.ds(kv_local * (width + HEAD) + step * HEAD, HEAD)] = dvals[
            here, :
        ].astype(BF16)
    qgain_ref[...] += qgain
    kgain_ref[...] += kgain


def attention_specs(length, groups, kv_local):
    width = groups * HEAD
    return [
        pl.BlockSpec((length, width), lambda g, r: (0, g)),
        pl.BlockSpec((length, HEAD), lambda g, r: (0, kv_local * groups + g)),
        pl.BlockSpec((length, HEAD), lambda g, r: (0, kv_local * (groups + 1) + g)),
        pl.BlockSpec((length, width), lambda g, r: (0, kv_local * (groups + 2) // groups + g)),
        pl.BlockSpec((length, HEAD), lambda g, r: (0, 0)),
        pl.BlockSpec((length, HEAD), lambda g, r: (0, 0)),
        pl.BlockSpec((1, HEAD), lambda g, r: (0, 0)),
        pl.BlockSpec((1, HEAD), lambda g, r: (0, 0)),
    ]


def attend_forward(rank, raw, cosines, sines, q_gain, k_gain, blocks, groups, kv_local):
    length = raw.shape[0]
    rows = length // blocks
    width = groups * HEAD
    flops = 4 * kv_local * groups * length * length * HEAD * (blocks + 1) // (2 * blocks)
    return pl.pallas_call(
        functools.partial(attend_fwd_kernel, blocks, rows, groups),
        grid_spec=pltpu.PrefetchScalarGridSpec(
            num_scalar_prefetch=1,
            grid=(kv_local,),
            in_specs=attention_specs(length, groups, kv_local),
            out_specs=[
                pl.BlockSpec((length, width), lambda g, r: (0, g)),
                pl.BlockSpec((length, width), lambda g, r: (0, g)),
                pl.BlockSpec((1, blocks, groups * rows), lambda g, r: (g, 0, 0)),
            ],
            scratch_shapes=[pltpu.VMEM((length, HEAD), BF16), pltpu.VMEM((HEAD, length), BF16)],
        ),
        out_shape=[
            jax.ShapeDtypeStruct((length, kv_local * width), BF16),
            jax.ShapeDtypeStruct((length, kv_local * width), F32),
            jax.ShapeDtypeStruct((kv_local, blocks, groups * rows), F32),
        ],
        compiler_params=pltpu.CompilerParams(
            dimension_semantics=("arbitrary",), vmem_limit_bytes=VMEM_LIMIT
        ),
        cost_estimate=pl.CostEstimate(
            flops=4 * flops,
            bytes_accessed=raw.size * 4 + length * kv_local * width * 6,
            transcendentals=kv_local * groups * length * length // 2,
        ),
        name="attend_forward",
    )(rank, raw, raw, raw, raw, cosines, sines, q_gain, k_gain)


def attend_backward(
    rank, raw, cosines, sines, q_gain, k_gain, mix, lse, upstream, blocks, groups, kv_local
):
    length = raw.shape[0]
    rows = length // blocks
    width = groups * HEAD
    flops = 10 * kv_local * groups * length * length * HEAD * (blocks + 1) // (2 * blocks)
    return pl.pallas_call(
        functools.partial(attend_bwd_kernel, blocks, rows, groups, kv_local),
        grid_spec=pltpu.PrefetchScalarGridSpec(
            num_scalar_prefetch=1,
            grid=(kv_local,),
            in_specs=attention_specs(length, groups, kv_local)
            + [
                pl.BlockSpec((length, width), lambda g, r: (0, g)),
                pl.BlockSpec((1, blocks, groups * rows), lambda g, r: (g, 0, 0)),
                pl.BlockSpec((length, width), lambda g, r: (0, g)),
            ],
            out_specs=[
                pl.BlockSpec(raw.shape, lambda g, r: (0, 0)),
                pl.BlockSpec((1, HEAD), lambda g, r: (0, 0)),
                pl.BlockSpec((1, HEAD), lambda g, r: (0, 0)),
            ],
            scratch_shapes=[
                pltpu.VMEM((length, HEAD), BF16),
                pltpu.VMEM((HEAD, length), BF16),
                pltpu.VMEM((length, HEAD), BF16),
                pltpu.VMEM((length, HEAD), F32),
                pltpu.VMEM((length, HEAD), F32),
            ],
        ),
        out_shape=[
            jax.ShapeDtypeStruct(raw.shape, BF16),
            jax.ShapeDtypeStruct((1, HEAD), F32),
            jax.ShapeDtypeStruct((1, HEAD), F32),
        ],
        compiler_params=pltpu.CompilerParams(
            dimension_semantics=("arbitrary",), vmem_limit_bytes=VMEM_LIMIT
        ),
        cost_estimate=pl.CostEstimate(
            flops=4 * flops,
            bytes_accessed=raw.size * 6 + length * kv_local * width * 6,
            transcendentals=kv_local * groups * length * length // 2,
        ),
        name="attend_backward",
    )(rank, raw, raw, raw, raw, cosines, sines, q_gain, k_gain, mix, lse, upstream)


def middle_kernel(tokens_ref, own_ref, x_ref, y_ref, gain_ref, middle_ref, second_ref):
    middle = tokens_ref[...].astype(F32) + own_ref[...]
    middle = middle + x_ref[...].astype(F32) + y_ref[...].astype(F32)
    scale = lax.rsqrt(jnp.mean(middle * middle, axis=-1, keepdims=True) + EPS)
    middle_ref[...] = middle
    second_ref[...] = (middle * scale * gain_ref[...]).astype(BF16)


def norm_back_kernel(low, values_ref, base_ref, own_ref, x_ref, y_ref, gain_ref, grad_ref, part_ref, *low_ref):
    values = values_ref[...].astype(F32)
    grad = own_ref[...] + x_ref[...].astype(F32) + y_ref[...].astype(F32)
    scale = lax.rsqrt(jnp.mean(values * values, axis=-1, keepdims=True) + EPS)
    normed = values * scale
    pulled = grad * gain_ref[...]
    inner = jnp.mean(normed * pulled, axis=-1, keepdims=True)
    total = base_ref[...] + scale * (pulled - normed * inner)
    grad_ref[...] = total
    if low:
        low_ref[0][...] = total.astype(BF16)

    @pl.when(pl.program_id(0) == 0)
    def _():
        part_ref[...] = jnp.zeros_like(part_ref)

    part_ref[...] += jnp.sum(normed * grad, axis=0, keepdims=True)


def row_call(kernel, name, arrays, gain, outs):
    rows, width = arrays[0].shape
    tile = rows // 4

    def spec(shape):
        if shape[0] == rows:
            return pl.BlockSpec((tile, width), lambda i: (i, 0))
        return pl.BlockSpec((1, width), lambda i: (0, 0))

    return pl.pallas_call(
        kernel,
        grid=(4,),
        in_specs=[spec(a.shape) for a in arrays] + [spec(gain.shape)],
        out_specs=[spec(o.shape) for o in outs],
        out_shape=outs,
        compiler_params=pltpu.CompilerParams(
            dimension_semantics=("arbitrary",), vmem_limit_bytes=VMEM_LIMIT
        ),
        cost_estimate=pl.CostEstimate(
            flops=16 * rows * width, bytes_accessed=18 * rows * width, transcendentals=rows
        ),
        name=name,
    )(*arrays, gain)


def two_addends(came):
    if len(came) == 2:
        return came
    return [sum(part.astype(F32) for part in came[:-1]), came[-1]]


def middle_and_second(tokens, own, came, gain):
    return row_call(
        middle_kernel, "middle_and_second", [tokens, own, *two_addends(came)], gain[None],
        [jax.ShapeDtypeStruct(own.shape, F32), jax.ShapeDtypeStruct(own.shape, BF16)],
    )


def norm_back(values, base, own, came, gain, low):
    outs = [
        jax.ShapeDtypeStruct(own.shape, F32), jax.ShapeDtypeStruct((1, own.shape[1]), F32),
    ] + [jax.ShapeDtypeStruct(own.shape, BF16)] * low
    return row_call(
        functools.partial(norm_back_kernel, low), "norm_back",
        [values, base, own, *two_addends(came)], gain[None], outs,
    )


def split_columns_kernel(count, sizes, rank_ref, *refs):
    sources, outs = refs[:count], refs[count:]
    block = jnp.bitwise_xor(pl.program_id(0), rank_ref[0])
    for j in range(count):

        @pl.when(block == j)
        def _(j=j):
            start = 0
            for size, out in zip(sizes, outs):
                out[...] = sources[j][:, start : start + size].astype(F32)
                start += size


def split_columns(rank, blocks, sizes):
    count, rows = len(blocks), blocks[0].shape[0]
    return pl.pallas_call(
        functools.partial(split_columns_kernel, count, sizes),
        grid_spec=pltpu.PrefetchScalarGridSpec(
            num_scalar_prefetch=1,
            grid=(count,),
            in_specs=[pl.BlockSpec(b.shape, lambda a, r: (0, 0)) for b in blocks],
            out_specs=[pl.BlockSpec((rows, size), lambda a, r: (0, a)) for size in sizes],
        ),
        out_shape=[jax.ShapeDtypeStruct((rows, count * size), F32) for size in sizes],
        compiler_params=pltpu.CompilerParams(
            dimension_semantics=("arbitrary",), vmem_limit_bytes=VMEM_LIMIT
        ),
        cost_estimate=pl.CostEstimate(
            flops=0, bytes_accessed=6 * rows * count * sum(sizes), transcendentals=0
        ),
        name="split_columns",
    )(rank, *blocks)


def stack_rows_kernel(count, rank_ref, *refs):
    block = jnp.bitwise_xor(pl.program_id(0), rank_ref[0])
    for j in range(count):

        @pl.when(block == j)
        def _(j=j):
            refs[count][...] = refs[j][...].astype(F32)


def stack_rows(rank, blocks):
    count, (rows, width) = len(blocks), blocks[0].shape
    return pl.pallas_call(
        functools.partial(stack_rows_kernel, count),
        grid_spec=pltpu.PrefetchScalarGridSpec(
            num_scalar_prefetch=1,
            grid=(count,),
            in_specs=[pl.BlockSpec(b.shape, lambda a, r: (0, 0)) for b in blocks],
            out_specs=pl.BlockSpec((rows, width), lambda a, r: (a, 0)),
        ),
        out_shape=jax.ShapeDtypeStruct((count * rows, width), F32),
        compiler_params=pltpu.CompilerParams(
            dimension_semantics=("arbitrary",), vmem_limit_bytes=VMEM_LIMIT
        ),
        cost_estimate=pl.CostEstimate(
            flops=0, bytes_accessed=6 * rows * count * width, transcendentals=0
        ),
        name="stack_rows",
    )(rank, *blocks)


def weave_units_kernel(count, shards, units, rank_ref, *refs):
    sources, out, held = refs[:count], refs[count], refs[count + 1]
    for j in range(count):
        held[jnp.bitwise_xor(rank_ref[0], j)] = sources[j][...].astype(F32)
    for a in range(count):
        for f in range(shards):
            start = (f * count + a) * units
            out[:, start : start + units] = held[a, :, f * units : (f + 1) * units]


def weave_units(rank, blocks, shards):
    count, (rows, ffs) = len(blocks), blocks[0].shape
    tile = rows // 4
    return pl.pallas_call(
        functools.partial(weave_units_kernel, count, shards, ffs // shards),
        grid_spec=pltpu.PrefetchScalarGridSpec(
            num_scalar_prefetch=1,
            grid=(rows // tile,),
            in_specs=[pl.BlockSpec((tile, ffs), lambda i, r: (i, 0)) for _ in blocks],
            out_specs=pl.BlockSpec((tile, count * ffs), lambda i, r: (i, 0)),
            scratch_shapes=[pltpu.VMEM((count, tile, ffs), F32)],
        ),
        out_shape=jax.ShapeDtypeStruct((rows, count * ffs), F32),
        compiler_params=pltpu.CompilerParams(
            dimension_semantics=("arbitrary",), vmem_limit_bytes=VMEM_LIMIT
        ),
        cost_estimate=pl.CostEstimate(
            flops=0, bytes_accessed=6 * rows * count * ffs, transcendentals=0
        ),
        name="weave_units",
    )(rank, *blocks)


def swap(values, bit, axis="sp"):
    return lax.ppermute(values, axis, [(i, i ^ bit) for i in range(lax.axis_size(axis))])


def sync(*values):
    return lax.optimization_barrier(values)


def gather_start(block):
    return [block] + [swap(block, j) for j in range(1, lax.axis_size("sp"))][: 2 if lax.axis_size("sp") == 4 else None]


def gather_turn(held):
    if lax.axis_size("sp") != 4:
        return held
    half = held[0].shape[0] // 2
    return held + [swap(held[2][:half], 1), swap(held[1][half:], 2)]


def gather_end(held):
    if lax.axis_size("sp") != 4:
        return held
    return held[:3] + [jnp.concatenate(held[3:], axis=0)]


def gather_blocks(block):
    return gather_end(gather_turn(gather_start(block)))


def scatter_start(corner):
    if lax.axis_size("sp") != 4:
        return []
    half = corner.shape[0] // 2
    return [swap(corner[:half], 1), swap(corner[half:], 2)]


def scatter_turn(others, came):
    if lax.axis_size("sp") != 4:
        return [swap(part.astype(BF16), j + 1) for j, part in enumerate(others)]
    half = others[0].shape[0] // 2
    to_x = jnp.concatenate([others[0][:half], others[0][half:] + came[1].astype(F32)], axis=0)
    to_y = jnp.concatenate([others[1][:half] + came[0].astype(F32), others[1][half:]], axis=0)
    return [swap(to_x.astype(BF16), 1), swap(to_y.astype(BF16), 2)]


def scatter_end(own, came):
    for part in came:
        own = own + part.astype(F32)
    return own


def corner_rows(make, rows):
    count = lax.axis_size("sp")
    return make((count - 1) * rows, count * rows).astype(BF16) if count == 4 else None


def other_rows(make, rows):
    count = lax.axis_size("sp")
    stop = 3 if count == 4 else count
    whole = make(rows, stop * rows)
    return [whole[j * rows : (j + 1) * rows] for j in range(stop - 1)]


def place_blocks(blocks, rank, axis):
    size = blocks[0].shape[axis]
    shape = list(blocks[0].shape)
    shape[axis] = size * len(blocks)
    whole = jnp.zeros(shape, blocks[0].dtype)
    for j, block in enumerate(blocks):
        whole = lax.dynamic_update_slice_in_dim(
            whole, block, jnp.bitwise_xor(rank, j) * size, axis
        )
    return whole


def halve_start(held, bit):
    shard = lax.axis_index("fsdp")
    mine = jnp.bitwise_and(lax.div(shard, jnp.int32(bit)), 1)
    pairs = held.reshape(held.shape[0] // 2, 2, held.shape[1], held.shape[2])
    sent = lax.dynamic_index_in_dim(pairs, 1 - mine, 1, False)
    kept = lax.dynamic_index_in_dim(pairs, mine, 1, False)
    return kept, swap(sent, bit, "fsdp")


def halve_end(state):
    return (state[0].astype(F32) + state[1].astype(F32)).astype(BF16)


def halve_open(grad):
    shards = lax.axis_size("fsdp")
    return halve_start(grad.reshape(shards, grad.shape[0] // shards, grad.shape[1]), 1)


def halve_next(state, bit):
    return halve_start(halve_end(state), bit)


def halve_close(state):
    held = halve_end(state)
    while held.shape[0] > 1:
        held = halve_end(halve_start(held, lax.axis_size("fsdp") // held.shape[0]))
    return held[0]


def double_over(values, axis):
    bit = 1
    while bit < lax.axis_size(axis):
        values = jnp.concatenate([values, swap(values, bit, axis)], axis=0)
        bit *= 2
    return values


def sum_all(values):
    for axis in ("sp", "fsdp"):
        bit = 1
        while bit < lax.axis_size(axis):
            values = values + swap(values, bit, axis)
            bit *= 2
    return values


def rms_low(values, gain):
    scale = lax.rsqrt(jnp.mean(values * values, axis=-1, keepdims=True) + EPS)
    return (values * scale * gain).astype(BF16)


def on_device(
    tokens, cotangent, positions, domain_ids, counts, loss_weight, domain_weights,
    q_weight, k_weight, v_weight, g_weight, o_weight, gate_weight, up_weight, down_weight,
    attn_gain, mlp_gain, q_gain, k_gain,
):
    count, shards = lax.axis_size("sp"), lax.axis_size("fsdp")
    rank, shard = lax.axis_index("sp"), lax.axis_index("fsdp")
    rank_ref = rank.astype(jnp.int32).reshape(1)
    _, rows, width = tokens.shape
    heads_local = q_weight.shape[1] // HEAD // count
    kv_local = k_weight.shape[1] // HEAD // count
    groups = heads_local // kv_local
    qcols, kcols = heads_local * HEAD, kv_local * HEAD
    dcols = width // count
    units = down_weight.shape[0] // count
    ffs = units * shards

    def columns(weight, size):
        return lax.dynamic_slice_in_dim(weight, rank * size, size, 1)

    def gather(weight):
        return lax.all_gather(weight, "fsdp", axis=0, tiled=True)

    def unit_columns(weight):
        spread = weight.reshape(weight.shape[0], shards, count, units)
        return lax.dynamic_slice_in_dim(spread, rank, 1, 2).reshape(weight.shape[0], ffs)

    def scatter(grad):
        return lax.psum_scatter(grad, "fsdp", scatter_dimension=0, tiled=True)

    tokens_held = gather_start(tokens[0])
    places = double_over(positions[0][None], "sp").reshape(-1)
    gains = double_over(jnp.concatenate([attn_gain, mlp_gain, q_gain, k_gain])[None], "fsdp")
    attn_full = gather(
        jnp.concatenate(
            [
                columns(q_weight, qcols), columns(k_weight, kcols), columns(v_weight, kcols),
                columns(g_weight, qcols), columns(o_weight, dcols),
            ],
            axis=1,
        )
    )
    in_cols = 2 * (qcols + kcols)
    onehot = (domain_ids[:, None] == jnp.arange(domain_weights.shape[0], dtype=jnp.int32)).astype(F32)
    seq_scale = loss_weight * jnp.sum(onehot * domain_weights[None, :], axis=1) * SEQ_LEN
    seq_scale = (seq_scale / counts.astype(F32))[0]
    upstream = cotangent[0].astype(F32) * seq_scale
    tokens_held, places, gains = sync(tokens_held, places, gains)
    tokens_held = gather_turn(tokens_held)
    gateup_share = jnp.concatenate([unit_columns(gate_weight), unit_columns(up_weight)], axis=1)
    tokens_held, upstream_low, gateup_share = sync(
        tokens_held, upstream.astype(BF16), gateup_share
    )
    gateup = gather(gateup_share)
    w_gate, w_up = gateup[:, :ffs], gateup[:, ffs:]
    upstream_held = gather_start(upstream_low)
    tokens_all = jnp.concatenate(gather_end(tokens_held), axis=0)

    order = jnp.bitwise_xor(jnp.arange(shards, dtype=jnp.int32), shard.astype(jnp.int32))
    gains = jnp.take(gains, order, axis=0).astype(F32)
    part = attn_gain.shape[0]
    first_gain = gains[:, :part].reshape(-1)
    second_gain = gains[:, part : 2 * part].reshape(-1)
    piece = q_gain.shape[0]
    query_gain = gains[:, 2 * part : 2 * part + piece].reshape(1, HEAD)
    key_gain = gains[:, 2 * part + piece :].reshape(1, HEAD)
    inverse = ROPE_BASE ** (-(2.0 * jnp.arange(HALF, dtype=F32)) / HEAD)
    angles = places.astype(F32)[:, None] * inverse
    cosines, sines = jnp.cos(angles), jnp.sin(angles)
    cosines = jnp.concatenate([cosines, cosines], axis=1)
    sines = jnp.concatenate([-sines, sines], axis=1)
    first = rms_low(tokens_all.astype(F32), first_gain)

    upstream_held, first, cosines, sines = sync(upstream_held, first, cosines, sines)
    upstream_held = gather_turn(upstream_held)
    first, upstream_held = sync(first, upstream_held)
    upstream_all = jnp.concatenate(gather_end(upstream_held), axis=0)
    first, upstream_all = sync(first, upstream_all)

    w_in = attn_full[:, :in_cols]
    o_slices = attn_full[:, in_cols:].reshape(count, qcols, dcols)
    o_blocks = [
        lax.dynamic_index_in_dim(o_slices, jnp.bitwise_xor(rank, j), 0, False) for j in range(count)
    ]
    first, o_blocks = sync(first, o_blocks)
    o_blocks = [swap(block, j) if j else block for j, block in enumerate(o_blocks)]
    raw = mm(first, w_in)
    raw, o_blocks = sync(raw, o_blocks)
    w_out = place_blocks(o_blocks, rank, 1)
    gated, mix, lse = attend_forward(
        rank_ref, raw, cosines, sines, query_gain, key_gain, count, groups, kv_local
    )
    down_share = lax.dynamic_slice_in_dim(down_weight, rank * units, units, 0)
    down_share, gated = sync(down_share, gated)
    w_down = gather(down_share)

    def out_rows(lo, hi):
        return mm(gated[lo:hi], w_out)

    corner = scatter_start(corner_rows(out_rows, rows))
    others = other_rows(out_rows, rows)
    own_part = out_rows(0, rows)
    middle, second = middle_and_second(
        tokens[0], own_part, scatter_turn(others, corner), second_gain
    )
    second = jnp.concatenate(gather_blocks(second), axis=0)

    gate_act = mm(second, w_gate)
    up_act = mm(second, w_up)
    opening = jax.nn.sigmoid(gate_act)
    silu = gate_act * opening
    hidden = (silu * up_act).astype(BF16)
    down_grad, upstream_now = sync(mm(hidden, upstream_all, TN).astype(BF16), upstream_all)
    down_share = scatter(down_grad)
    grad_hidden = mm(upstream_now, w_down, NT)
    grad_gate = (grad_hidden * up_act * opening * (1.0 + gate_act * (1.0 - opening))).astype(BF16)
    grad_up = (grad_hidden * silu).astype(BF16)

    def second_rows(lo, hi):
        return mm(grad_gate[lo:hi], w_gate, NT) + mm(grad_up[lo:hi], w_up, NT)

    corner = scatter_start(corner_rows(second_rows, rows))
    others = other_rows(second_rows, rows)
    own_part = second_rows(0, rows)
    own_part, corner, others, grad_gate, grad_up, second = sync(
        own_part, corner, others, grad_gate, grad_up, second
    )
    came = scatter_turn(others, corner)
    gateup_grad = mm(second, jnp.concatenate([grad_gate, grad_up], axis=1), TN).astype(BF16)
    gateup_grad, came = sync(gateup_grad, came)
    gateup_share = scatter(gateup_grad)
    came, down_share = sync(came, down_share)
    down_held = gather_start(down_share)
    grad_middle, second_gain_part, grad_attn = norm_back(
        middle, upstream, own_part, came, second_gain, True
    )
    grad_attn, hidden = sync(grad_attn, hidden)
    grad_attn = gather_start(grad_attn)

    def down_rows(lo, hi):
        return mm(hidden[lo:hi], w_down)

    corner = corner_rows(down_rows, rows)
    others = other_rows(down_rows, rows)
    own_part = down_rows(0, rows)
    grad_attn, corner, others, own_part, down_held = sync(
        grad_attn, corner, others, own_part, down_held
    )
    grad_attn = jnp.concatenate(gather_end(gather_turn(grad_attn)), axis=0)

    grad_gated = mm(grad_attn, w_out, NT).astype(BF16)
    out_grad = mm(gated, grad_attn, TN).astype(BF16)
    out_blocks = [
        lax.dynamic_slice_in_dim(out_grad, jnp.bitwise_xor(rank, j) * dcols, dcols, 1)
        for j in range(count)
    ]
    grad_gated, out_blocks = sync(grad_gated, out_blocks)
    out_blocks = [swap(block, j) if j else block for j, block in enumerate(out_blocks)]
    grad_raw, query_gain_part, key_gain_part = attend_backward(
        rank_ref, raw, cosines, sines, query_gain, key_gain, mix, lse, grad_gated,
        count, groups, kv_local,
    )
    grad_raw, out_blocks, corner, down_held = sync(grad_raw, out_blocks, corner, down_held)
    corner = scatter_start(corner)
    down_held = gather_turn(down_held)
    attn_grad = mm(first, grad_raw, TN).astype(BF16)
    out_grad = place_blocks(out_blocks, rank, 0)
    attn_grad, grad_raw, corner, down_held = sync(attn_grad, grad_raw, corner, down_held)
    came = scatter_turn(others, corner)

    def first_rows(lo, hi):
        return mm(grad_raw[lo:hi], w_in, NT)

    corner = corner_rows(first_rows, rows)
    others = other_rows(first_rows, rows)
    first_part = first_rows(0, rows)
    down_grad = stack_rows(rank_ref, gather_end(down_held))
    attn_grad, out_grad, corner, others, first_part = sync(
        attn_grad, out_grad, corner, others, first_part
    )
    came, corner, down_grad, attn_grad, out_grad = sync(came, corner, down_grad, attn_grad, out_grad)
    corner = scatter_start(corner)
    gateup_share, attn_grad = sync(gateup_share, attn_grad)
    attn_share = scatter(attn_grad)
    gateup_held = gather_start(gateup_share)
    out_grad, gateup_share = sync(out_grad, gateup_share)
    out_share = scatter(out_grad)
    block_out = (middle + scatter_end(own_part, came)).astype(BF16)
    corner, block_out = sync(corner, block_out)
    came = scatter_turn(others, corner)
    came, gateup_held = sync(came, gateup_held)
    gateup_held = gather_turn(gateup_held)
    input_grad, first_gain_part = norm_back(
        tokens[0], grad_middle, first_part, came, first_gain, False
    )
    attn_share, input_grad = sync(attn_share, input_grad)
    attn_held = gather_start(attn_share)
    total = sum_all(
        jnp.concatenate(
            [first_gain_part, query_gain_part, key_gain_part, second_gain_part], axis=1
        )[0]
    )
    gateup_held, attn_held = sync(gateup_held, attn_held)
    attn_held = gather_turn(attn_held)
    gateup_blocks = gather_end(gateup_held)
    gate_grad = weave_units(rank_ref, [b[:, :ffs] for b in gateup_blocks], shards)
    up_grad = weave_units(rank_ref, [b[:, ffs:] for b in gateup_blocks], shards)
    out_share, gate_grad, up_grad = sync(out_share, gate_grad, up_grad)
    out_held = gather_start(out_share)
    out_held, attn_held = sync(out_held, attn_held)
    out_held = gather_turn(out_held)
    attn_grads = split_columns(rank_ref, gather_end(attn_held), (qcols, kcols, kcols, qcols))
    (out_grad,) = split_columns(rank_ref, gather_end(out_held), (dcols,))

    def own(values):
        size = values.shape[0] // shards
        return lax.dynamic_slice_in_dim(values, shard * size, size, 0)

    return (
        block_out[None],
        input_grad[None],
        *attn_grads,
        out_grad,
        gate_grad,
        up_grad,
        down_grad,
        own(total[:width]),
        own(total[width + 2 * HEAD :]),
        own(total[width : width + HEAD]),
        own(total[width + HEAD : width + 2 * HEAD]),
    )


def solution(mesh):
    both, over_fsdp = P("fsdp", "sp", None), P("fsdp", None)
    return jax.shard_map(
        on_device,
        mesh=mesh,
        in_specs=(both, both, P("fsdp", "sp"), P("fsdp"), P("fsdp"), P("fsdp"), P())
        + (over_fsdp,) * 8
        + (P("fsdp"),) * 4,
        out_specs=(both, both) + (over_fsdp,) * 8 + (P("fsdp"),) * 4,
        check_vma=False,
    )
```

```python
import functools

import jax
import jax.numpy as jnp
from jax import lax
from jax.experimental import pallas as pl
from jax.experimental.pallas import tpu as pltpu
from jax.sharding import PartitionSpec as P

HEAD = 128
HALF = HEAD // 2
SEQ_LEN = 1024
EPS = 1e-06
ROPE_BASE = 1000000.0
SCALE = HEAD ** (-0.5)
LOG2E = 1.4426950408889634
VMEM_LIMIT = 56 * 1024 * 1024
NT = (((1,), (1,)), ((), ()))
NN = (((1,), (0,)), ((), ()))
TN = (((0,), (0,)), ((), ()))
F32 = jnp.float32
BF16 = jnp.bfloat16


def mm(left, right, dims=NN):
    return lax.dot_general(left, right, dims, preferred_element_type=F32)


def head_norm(raw):
    return lax.rsqrt(jnp.mean(raw * raw, axis=-1, keepdims=True) + EPS)


def turn(values, cosines, sines):
    return values * cosines + pltpu.roll(values, HALF, 1) * sines


def turn_back(values, cosines, sines):
    return values * cosines - pltpu.roll(values, HALF, 1) * sines


def norm_turn(raw, gain, cosines, sines):
    return turn(raw * head_norm(raw) * gain, cosines, sines).astype(BF16)


def norm_turn_back(raw, gain, grad, cosines, sines):
    back = turn_back(grad, cosines, sines)
    scale = head_norm(raw)
    pulled = back * gain
    inner = jnp.mean(raw * pulled, axis=-1, keepdims=True)
    gain_part = jnp.sum(raw * scale * back, axis=0, keepdims=True)
    return scale * pulled - raw * (scale * scale * scale * inner), gain_part


def diagonal_mask(rows, groups):
    keys = lax.broadcasted_iota(jnp.int32, (rows, groups * rows), 0)
    places = lax.broadcasted_iota(jnp.int32, (rows, groups * rows), 1)
    return keys <= lax.rem(places, rows)


def row_block(block, rank, rows):
    return pl.ds(pl.multiple_of(jnp.bitwise_xor(block, rank) * rows, rows), rows)


def attend_fwd_kernel(
    blocks, rows, groups,
    rank_ref, q_ref, k_ref, v_ref, g_ref, cos_ref, sin_ref, qg_ref, kg_ref,
    gated_ref, mix_ref, lse_ref, keys, vals_t,
):
    rank = rank_ref[0]
    factor = SCALE * LOG2E
    for a in range(blocks):
        place = row_block(a, rank, rows)
        here = slice(a * rows, (a + 1) * rows)
        keys[here, :] = norm_turn(k_ref[place, :], kg_ref[...], cos_ref[place, :], sin_ref[place, :])
        vals_t[:, here] = v_ref[place, :].T.astype(BF16)
    mask = diagonal_mask(rows, groups)
    for a in range(blocks):
        place = row_block(a, rank, rows)
        cosines, sines = cos_ref[place, :], sin_ref[place, :]
        queries = jnp.concatenate(
            [
                norm_turn(q_ref[place, h * HEAD : (h + 1) * HEAD], qg_ref[...], cosines, sines)
                for h in range(groups)
            ],
            axis=0,
        )
        low, high = a * rows, (a + 1) * rows
        near = jnp.where(mask, mm(keys[low:high, :], queries, NT), -1e30)
        peak = jnp.max(near, axis=0, keepdims=True)
        if a:
            far = mm(keys[:low, :], queries, NT)
            peak = jnp.maximum(peak, jnp.max(far, axis=0, keepdims=True))
        near = jnp.exp2((near - peak) * factor)
        total = jnp.sum(near, axis=0, keepdims=True)
        if a:
            far = jnp.exp2((far - peak) * factor)
            total = total + jnp.sum(far, axis=0, keepdims=True)
        inverse = 1.0 / total
        mix_t = mm(vals_t[:, low:high], (near * inverse).astype(BF16))
        if a:
            mix_t = mix_t + mm(vals_t[:, :low], (far * inverse).astype(BF16))
        mix = mix_t.T
        for h in range(groups):
            cols = slice(h * HEAD, (h + 1) * HEAD)
            part = mix[h * rows : (h + 1) * rows, :]
            opening = jax.nn.sigmoid(g_ref[place, cols].astype(BF16).astype(F32))
            mix_ref[place, cols] = part
            gated_ref[place, cols] = (part * opening).astype(BF16)
        lse_ref[0, a : a + 1, :] = peak * factor + jnp.log2(total)


def attend_bwd_kernel(
    blocks, rows, groups, kv_local,
    rank_ref, q_ref, k_ref, v_ref, g_ref, cos_ref, sin_ref, qg_ref, kg_ref, mix_ref, lse_ref, up_ref,
    grad_ref, qgain_ref, kgain_ref, keys, keys_t, vals, dkeys, dvals,
):
    rank = rank_ref[0]
    step = pl.program_id(0)
    factor = SCALE * LOG2E
    width = groups * HEAD

    @pl.when(step == 0)
    def _():
        qgain_ref[...] = jnp.zeros_like(qgain_ref)
        kgain_ref[...] = jnp.zeros_like(kgain_ref)

    for a in range(blocks):
        place = row_block(a, rank, rows)
        here = slice(a * rows, (a + 1) * rows)
        block = norm_turn(k_ref[place, :], kg_ref[...], cos_ref[place, :], sin_ref[place, :])
        keys[here, :] = block
        keys_t[:, here] = block.astype(F32).T.astype(BF16)
        vals[here, :] = v_ref[place, :].astype(BF16)
    mask = diagonal_mask(rows, groups)
    qgain = jnp.zeros((1, HEAD), F32)
    for a in reversed(range(blocks)):
        place = row_block(a, rank, rows)
        cosines, sines = cos_ref[place, :], sin_ref[place, :]
        queries, grads = [], []
        for h in range(groups):
            cols = slice(h * HEAD, (h + 1) * HEAD)
            queries.append(norm_turn(q_ref[place, cols], qg_ref[...], cosines, sines))
            upstream = up_ref[place, cols].astype(F32)
            opening = jax.nn.sigmoid(g_ref[place, cols].astype(BF16).astype(F32))
            opened = upstream * opening
            grads.append(opened.astype(BF16))
            grad_ref[
                place, pl.ds((kv_local * (groups + 2)) * HEAD + step * width + h * HEAD, HEAD)
            ] = (opened * mix_ref[place, cols] * (1.0 - opening)).astype(BF16)
        queries = jnp.concatenate(queries, axis=0)
        grads = jnp.concatenate(grads, axis=0)
        lse = lse_ref[0, a : a + 1, :]
        low, high = a * rows, (a + 1) * rows
        spans = [(low, high)] + ([(0, low)] if a else [])
        chances, grad_chances = [], []
        centre = jnp.zeros((1, groups * rows), F32)
        for start, stop in spans:
            part = jnp.exp2(mm(keys[start:stop, :], queries, NT) * factor - lse)
            if start == low:
                part = jnp.where(mask, part, 0.0)
            pull = mm(vals[start:stop, :], grads, NT)
            centre = centre + jnp.sum(part * pull, axis=0, keepdims=True)
            chances.append(part)
            grad_chances.append(pull)
        dq_t = jnp.zeros((HEAD, groups * rows), F32)
        for (start, stop), part, pull in zip(spans, chances, grad_chances):
            grad_products = (part * (pull - centre) * SCALE).astype(BF16)
            dval = mm(part.astype(BF16), grads)
            dkey = mm(grad_products, queries)
            if a == blocks - 1:
                dvals[start:stop, :] = dval
                dkeys[start:stop, :] = dkey
            else:
                dvals[start:stop, :] += dval
                dkeys[start:stop, :] += dkey
            dq_t = dq_t + mm(keys_t[:, start:stop], grad_products)
        dq = dq_t.T
        for h in range(groups):
            grad = dq[h * rows : (h + 1) * rows, :].astype(BF16).astype(F32)
            cols = slice(h * HEAD, (h + 1) * HEAD)
            raw, gain_part = norm_turn_back(q_ref[place, cols], qg_ref[...], grad, cosines, sines)
            grad_ref[place, pl.ds(step * width + h * HEAD, HEAD)] = raw.astype(BF16)
            qgain = qgain + gain_part
    kgain = jnp.zeros((1, HEAD), F32)
    for a in range(blocks):
        place = row_block(a, rank, rows)
        here = slice(a * rows, (a + 1) * rows)
        grad = dkeys[here, :].astype(BF16).astype(F32)
        raw, gain_part = norm_turn_back(
            k_ref[place, :], kg_ref[...], grad, cos_ref[place, :], sin_ref[place, :]
        )
        kgain = kgain + gain_part
        grad_ref[place, pl.ds(kv_local * width + step * HEAD, HEAD)] = raw.astype(BF16)
        grad_ref[place, pl.ds(kv_local * (width + HEAD) + step * HEAD, HEAD)] = dvals[
            here, :
        ].astype(BF16)
    qgain_ref[...] += qgain
    kgain_ref[...] += kgain


def attention_specs(length, groups, kv_local):
    width = groups * HEAD
    return [
        pl.BlockSpec((length, width), lambda g, r: (0, g)),
        pl.BlockSpec((length, HEAD), lambda g, r: (0, kv_local * groups + g)),
        pl.BlockSpec((length, HEAD), lambda g, r: (0, kv_local * (groups + 1) + g)),
        pl.BlockSpec((length, width), lambda g, r: (0, kv_local * (groups + 2) // groups + g)),
        pl.BlockSpec((length, HEAD), lambda g, r: (0, 0)),
        pl.BlockSpec((length, HEAD), lambda g, r: (0, 0)),
        pl.BlockSpec((1, HEAD), lambda g, r: (0, 0)),
        pl.BlockSpec((1, HEAD), lambda g, r: (0, 0)),
    ]


def attend_forward(rank, raw, cosines, sines, q_gain, k_gain, blocks, groups, kv_local):
    length = raw.shape[0]
    rows = length // blocks
    width = groups * HEAD
    flops = 4 * kv_local * groups * length * length * HEAD * (blocks + 1) // (2 * blocks)
    return pl.pallas_call(
        functools.partial(attend_fwd_kernel, blocks, rows, groups),
        grid_spec=pltpu.PrefetchScalarGridSpec(
            num_scalar_prefetch=1,
            grid=(kv_local,),
            in_specs=attention_specs(length, groups, kv_local),
            out_specs=[
                pl.BlockSpec((length, width), lambda g, r: (0, g)),
                pl.BlockSpec((length, width), lambda g, r: (0, g)),
                pl.BlockSpec((1, blocks, groups * rows), lambda g, r: (g, 0, 0)),
            ],
            scratch_shapes=[pltpu.VMEM((length, HEAD), BF16), pltpu.VMEM((HEAD, length), BF16)],
        ),
        out_shape=[
            jax.ShapeDtypeStruct((length, kv_local * width), BF16),
            jax.ShapeDtypeStruct((length, kv_local * width), F32),
            jax.ShapeDtypeStruct((kv_local, blocks, groups * rows), F32),
        ],
        compiler_params=pltpu.CompilerParams(
            dimension_semantics=("arbitrary",), vmem_limit_bytes=VMEM_LIMIT
        ),
        cost_estimate=pl.CostEstimate(
            flops=4 * flops,
            bytes_accessed=raw.size * 4 + length * kv_local * width * 6,
            transcendentals=kv_local * groups * length * length // 2,
        ),
        name="attend_forward",
    )(rank, raw, raw, raw, raw, cosines, sines, q_gain, k_gain)


def attend_backward(
    rank, raw, cosines, sines, q_gain, k_gain, mix, lse, upstream, blocks, groups, kv_local
):
    length = raw.shape[0]
    rows = length // blocks
    width = groups * HEAD
    flops = 10 * kv_local * groups * length * length * HEAD * (blocks + 1) // (2 * blocks)
    return pl.pallas_call(
        functools.partial(attend_bwd_kernel, blocks, rows, groups, kv_local),
        grid_spec=pltpu.PrefetchScalarGridSpec(
            num_scalar_prefetch=1,
            grid=(kv_local,),
            in_specs=attention_specs(length, groups, kv_local)
            + [
                pl.BlockSpec((length, width), lambda g, r: (0, g)),
                pl.BlockSpec((1, blocks, groups * rows), lambda g, r: (g, 0, 0)),
                pl.BlockSpec((length, width), lambda g, r: (0, g)),
            ],
            out_specs=[
                pl.BlockSpec(raw.shape, lambda g, r: (0, 0)),
                pl.BlockSpec((1, HEAD), lambda g, r: (0, 0)),
                pl.BlockSpec((1, HEAD), lambda g, r: (0, 0)),
            ],
            scratch_shapes=[
                pltpu.VMEM((length, HEAD), BF16),
                pltpu.VMEM((HEAD, length), BF16),
                pltpu.VMEM((length, HEAD), BF16),
                pltpu.VMEM((length, HEAD), F32),
                pltpu.VMEM((length, HEAD), F32),
            ],
        ),
        out_shape=[
            jax.ShapeDtypeStruct(raw.shape, BF16),
            jax.ShapeDtypeStruct((1, HEAD), F32),
            jax.ShapeDtypeStruct((1, HEAD), F32),
        ],
        compiler_params=pltpu.CompilerParams(
            dimension_semantics=("arbitrary",), vmem_limit_bytes=VMEM_LIMIT
        ),
        cost_estimate=pl.CostEstimate(
            flops=4 * flops,
            bytes_accessed=raw.size * 6 + length * kv_local * width * 6,
            transcendentals=kv_local * groups * length * length // 2,
        ),
        name="attend_backward",
    )(rank, raw, raw, raw, raw, cosines, sines, q_gain, k_gain, mix, lse, upstream)


def middle_kernel(tokens_ref, own_ref, x_ref, y_ref, gain_ref, middle_ref, second_ref):
    middle = tokens_ref[...].astype(F32) + own_ref[...]
    middle = middle + x_ref[...].astype(F32) + y_ref[...].astype(F32)
    scale = lax.rsqrt(jnp.mean(middle * middle, axis=-1, keepdims=True) + EPS)
    middle_ref[...] = middle
    second_ref[...] = (middle * scale * gain_ref[...]).astype(BF16)


def norm_back_kernel(low, values_ref, base_ref, own_ref, x_ref, y_ref, gain_ref, grad_ref, *low_ref):
    values = values_ref[...].astype(F32)
    grad = own_ref[...] + x_ref[...].astype(F32) + y_ref[...].astype(F32)
    scale = lax.rsqrt(jnp.mean(values * values, axis=-1, keepdims=True) + EPS)
    normed = values * scale
    pulled = grad * gain_ref[...]
    inner = jnp.mean(normed * pulled, axis=-1, keepdims=True)
    total = base_ref[...] + scale * (pulled - normed * inner)
    grad_ref[...] = total
    if low:
        low_ref[0][...] = total.astype(BF16)


def row_call(kernel, name, arrays, gain, outs):
    rows, width = arrays[0].shape
    tile = rows // 4

    def spec(shape):
        if shape[0] == rows:
            return pl.BlockSpec((tile, width), lambda i: (i, 0))
        return pl.BlockSpec((1, width), lambda i: (0, 0))

    return pl.pallas_call(
        kernel,
        grid=(4,),
        in_specs=[spec(a.shape) for a in arrays] + [spec(gain.shape)],
        out_specs=[spec(o.shape) for o in outs],
        out_shape=outs,
        compiler_params=pltpu.CompilerParams(
            dimension_semantics=("arbitrary",), vmem_limit_bytes=VMEM_LIMIT
        ),
        cost_estimate=pl.CostEstimate(
            flops=16 * rows * width, bytes_accessed=18 * rows * width, transcendentals=rows
        ),
        name=name,
    )(*arrays, gain)


def two_addends(came):
    if len(came) == 2:
        return came
    return [sum(part.astype(F32) for part in came[:-1]), came[-1]]


def middle_and_second(tokens, own, came, gain):
    return row_call(
        middle_kernel, "middle_and_second", [tokens, own, *two_addends(came)], gain[None],
        [jax.ShapeDtypeStruct(own.shape, F32), jax.ShapeDtypeStruct(own.shape, BF16)],
    )


def norm_back(values, base, own, came, gain, low):
    outs = [jax.ShapeDtypeStruct(own.shape, F32)] + [jax.ShapeDtypeStruct(own.shape, BF16)] * low
    return row_call(
        functools.partial(norm_back_kernel, low), "norm_back",
        [values, base, own, *two_addends(came)], gain[None], outs,
    )


def flat_specs(pieces, spec):
    return [spec(piece) for block in pieces for piece in block]


def grouped(refs, counts):
    blocks, start = [], 0
    for count in counts:
        blocks.append(refs[start : start + count])
        start += count
    return blocks, refs[start:]


def split_columns_kernel(counts, sizes, weighed, rank_ref, *refs):
    sources, refs = grouped(refs, counts)
    weights, outs, sums = refs[:weighed], refs[weighed : weighed + len(sizes)], refs[-1]
    block = jnp.bitwise_xor(pl.program_id(0), rank_ref[0])
    for j, pieces in enumerate(sources):

        @pl.when(block == j)
        def _(pieces=pieces):
            top = 0
            for piece in pieces:
                start, stop = 0, top + piece.shape[0]
                for size, out in zip(sizes, outs):
                    out[top:stop, :] = piece[:, start : start + size].astype(F32)
                    start += size
                top = stop

    if weighed:
        part = sum(
            jnp.sum(out[...] * weight[...].astype(F32), axis=1, keepdims=True)
            for out, weight in zip(outs, weights)
        )

        @pl.when(pl.program_id(0) == 0)
        def _():
            sums[...] = jnp.zeros_like(sums)

        sums[...] += part


def split_columns(rank, pieces, sizes, weights=()):
    count, rows = len(pieces), pieces[0][0].shape[0]
    group_specs = [pl.BlockSpec((rows, size), lambda a, r: (0, a)) for size in sizes]
    sum_specs = [pl.BlockSpec((rows, 1), lambda a, r: (0, 0))] if weights else []
    return pl.pallas_call(
        functools.partial(
            split_columns_kernel, [len(block) for block in pieces], sizes, len(weights)
        ),
        grid_spec=pltpu.PrefetchScalarGridSpec(
            num_scalar_prefetch=1,
            grid=(count,),
            in_specs=flat_specs(pieces, lambda p: pl.BlockSpec(p.shape, lambda a, r: (0, 0)))
            + group_specs[: len(weights)],
            out_specs=group_specs + sum_specs,
        ),
        out_shape=[jax.ShapeDtypeStruct((rows, count * size), F32) for size in sizes]
        + [jax.ShapeDtypeStruct((rows, 1), F32)] * len(sum_specs),
        compiler_params=pltpu.CompilerParams(
            dimension_semantics=("arbitrary",), vmem_limit_bytes=VMEM_LIMIT
        ),
        cost_estimate=pl.CostEstimate(
            flops=0, bytes_accessed=6 * rows * count * sum(sizes), transcendentals=0
        ),
        name="split_columns",
    )(rank, *sum(pieces, []), *weights)


def stack_rows_kernel(counts, rank_ref, *refs):
    sources, (out,) = grouped(refs, counts)
    block = jnp.bitwise_xor(pl.program_id(0), rank_ref[0])
    for j, pieces in enumerate(sources):

        @pl.when(block == j)
        def _(pieces=pieces):
            top = 0
            for piece in pieces:
                out[top : top + piece.shape[0], :] = piece[...].astype(F32)
                top += piece.shape[0]


def stack_rows(rank, pieces):
    count, (rows, width) = len(pieces), pieces[0][0].shape
    return pl.pallas_call(
        functools.partial(stack_rows_kernel, [len(block) for block in pieces]),
        grid_spec=pltpu.PrefetchScalarGridSpec(
            num_scalar_prefetch=1,
            grid=(count,),
            in_specs=flat_specs(pieces, lambda p: pl.BlockSpec(p.shape, lambda a, r: (0, 0))),
            out_specs=pl.BlockSpec((rows, width), lambda a, r: (a, 0)),
        ),
        out_shape=jax.ShapeDtypeStruct((count * rows, width), F32),
        compiler_params=pltpu.CompilerParams(
            dimension_semantics=("arbitrary",), vmem_limit_bytes=VMEM_LIMIT
        ),
        cost_estimate=pl.CostEstimate(
            flops=0, bytes_accessed=6 * rows * count * width, transcendentals=0
        ),
        name="stack_rows",
    )(rank, *sum(pieces, []))


def weave_units_kernel(counts, steps, shards, units, rank_ref, *refs):
    sources, (weight, out, sums, held) = grouped(refs, counts)
    step = pl.program_id(0)
    for j, pieces in enumerate(sources):
        place = jnp.bitwise_xor(rank_ref[0], j)
        if len(pieces) == 1:
            held[place] = pieces[0][...].astype(F32)
            continue
        share = steps // len(pieces)
        for k, piece in enumerate(pieces):

            @pl.when((step >= k * share) & (step < (k + 1) * share))
            def _(piece=piece, place=place):
                held[place] = piece[...].astype(F32)

    count = len(counts)
    for a in range(count):
        for f in range(shards):
            start = (f * count + a) * units
            out[:, start : start + units] = held[a, :, f * units : (f + 1) * units]
    sums[...] = jnp.sum(out[...] * weight[...].astype(F32), axis=1, keepdims=True)


def weave_units(rank, pieces, group, weight, shards):
    count, (rows, width) = len(pieces), pieces[0][0].shape
    ffs, steps = width // 2, 4
    tile = rows // steps

    def spec(block, k):
        share = steps // len(block)

        def place(i, r):
            return (jnp.clip(i - k * share, 0, share - 1), group)

        return pl.BlockSpec((tile, ffs), place)

    return pl.pallas_call(
        functools.partial(
            weave_units_kernel, [len(block) for block in pieces], steps, shards, ffs // shards
        ),
        grid_spec=pltpu.PrefetchScalarGridSpec(
            num_scalar_prefetch=1,
            grid=(steps,),
            in_specs=[spec(block, k) for block in pieces for k in range(len(block))]
            + [pl.BlockSpec((tile, count * ffs), lambda i, r: (i, 0))],
            out_specs=[
                pl.BlockSpec((tile, count * ffs), lambda i, r: (i, 0)),
                pl.BlockSpec((tile, 1), lambda i, r: (i, 0)),
            ],
            scratch_shapes=[pltpu.VMEM((count, tile, ffs), F32)],
        ),
        out_shape=[
            jax.ShapeDtypeStruct((rows, count * ffs), F32), jax.ShapeDtypeStruct((rows, 1), F32),
        ],
        compiler_params=pltpu.CompilerParams(
            dimension_semantics=("arbitrary",), vmem_limit_bytes=VMEM_LIMIT
        ),
        cost_estimate=pl.CostEstimate(
            flops=0, bytes_accessed=8 * rows * count * ffs, transcendentals=0
        ),
        name="weave_units",
    )(rank, *sum(pieces, []), weight)


def swap(values, bit, axis="sp"):
    return lax.ppermute(values, axis, [(i, i ^ bit) for i in range(lax.axis_size(axis))])


def sync(*values):
    return lax.optimization_barrier(values)


def gather_start(block):
    return [block] + [swap(block, j) for j in range(1, lax.axis_size("sp"))][: 2 if lax.axis_size("sp") == 4 else None]


def gather_turn(held):
    if lax.axis_size("sp") != 4:
        return held
    half = held[0].shape[0] // 2
    return held + [swap(held[2][:half], 1), swap(held[1][half:], 2)]


def gather_end(held):
    if lax.axis_size("sp") != 4:
        return held
    return held[:3] + [jnp.concatenate(held[3:], axis=0)]


def gather_blocks(block):
    return gather_end(gather_turn(gather_start(block)))


def gather_pieces(held):
    if lax.axis_size("sp") != 4:
        return [[block] for block in held]
    return [[block] for block in held[:3]] + [held[3:]]


def scatter_start(corner):
    if lax.axis_size("sp") != 4:
        return []
    half = corner.shape[0] // 2
    return [swap(corner[:half], 1), swap(corner[half:], 2)]


def scatter_turn(others, came):
    if lax.axis_size("sp") != 4:
        return [swap(part.astype(BF16), j + 1) for j, part in enumerate(others)]
    half = others[0].shape[0] // 2
    to_x = jnp.concatenate([others[0][:half], others[0][half:] + came[1].astype(F32)], axis=0)
    to_y = jnp.concatenate([others[1][:half] + came[0].astype(F32), others[1][half:]], axis=0)
    return [swap(to_x.astype(BF16), 1), swap(to_y.astype(BF16), 2)]


def scatter_end(own, came):
    for part in came:
        own = own + part.astype(F32)
    return own


def corner_rows(make, rows):
    count = lax.axis_size("sp")
    return make((count - 1) * rows, count * rows).astype(BF16) if count == 4 else None


def other_rows(make, rows):
    count = lax.axis_size("sp")
    stop = 3 if count == 4 else count
    whole = make(rows, stop * rows)
    return [whole[j * rows : (j + 1) * rows] for j in range(stop - 1)]


def place_blocks(blocks, rank, axis):
    size = blocks[0].shape[axis]
    shape = list(blocks[0].shape)
    shape[axis] = size * len(blocks)
    whole = jnp.zeros(shape, blocks[0].dtype)
    for j, block in enumerate(blocks):
        whole = lax.dynamic_update_slice_in_dim(
            whole, block, jnp.bitwise_xor(rank, j) * size, axis
        )
    return whole


def halve_start(held, bit):
    shard = lax.axis_index("fsdp")
    mine = jnp.bitwise_and(lax.div(shard, jnp.int32(bit)), 1)
    pairs = held.reshape(held.shape[0] // 2, 2, held.shape[1], held.shape[2])
    sent = lax.dynamic_index_in_dim(pairs, 1 - mine, 1, False)
    kept = lax.dynamic_index_in_dim(pairs, mine, 1, False)
    return kept, swap(sent, bit, "fsdp")


def halve_end(state):
    return (state[0].astype(F32) + state[1].astype(F32)).astype(BF16)


def halve_open(grad):
    shards = lax.axis_size("fsdp")
    return halve_start(grad.reshape(shards, grad.shape[0] // shards, grad.shape[1]), 1)


def halve_next(state, bit):
    return halve_start(halve_end(state), bit)


def halve_close(state):
    held = halve_end(state)
    while held.shape[0] > 1:
        held = halve_end(halve_start(held, lax.axis_size("fsdp") // held.shape[0]))
    return held[0]


def double_over(values, axis):
    bit = 1
    while bit < lax.axis_size(axis):
        values = jnp.concatenate([values, swap(values, bit, axis)], axis=0)
        bit *= 2
    return values


def sum_steps():
    return [
        (axis, 1 << k)
        for axis in ("sp", "fsdp")
        for k in range((lax.axis_size(axis) - 1).bit_length())
    ]


def sum_over(values, steps):
    for axis, bit in steps:
        values = values + swap(values, bit, axis)
    return values


def rms_low(values, gain):
    scale = lax.rsqrt(jnp.mean(values * values, axis=-1, keepdims=True) + EPS)
    return (values * scale * gain).astype(BF16)


def on_device(
    tokens, cotangent, positions, domain_ids, counts, loss_weight, domain_weights,
    q_weight, k_weight, v_weight, g_weight, o_weight, gate_weight, up_weight, down_weight,
    attn_gain, mlp_gain, q_gain, k_gain,
):
    count, shards = lax.axis_size("sp"), lax.axis_size("fsdp")
    rank, shard = lax.axis_index("sp"), lax.axis_index("fsdp")
    rank_ref = rank.astype(jnp.int32).reshape(1)
    _, rows, width = tokens.shape
    heads_local = q_weight.shape[1] // HEAD // count
    kv_local = k_weight.shape[1] // HEAD // count
    groups = heads_local // kv_local
    qcols, kcols = heads_local * HEAD, kv_local * HEAD
    dcols = width // count
    units = down_weight.shape[0] // count
    ffs = units * shards

    def columns(weight, size):
        return lax.dynamic_slice_in_dim(weight, rank * size, size, 1)

    def gather(weight):
        return lax.all_gather(weight, "fsdp", axis=0, tiled=True)

    def unit_columns(weight):
        spread = weight.reshape(weight.shape[0], shards, count, units)
        return lax.dynamic_slice_in_dim(spread, rank, 1, 2).reshape(weight.shape[0], ffs)

    def scatter(grad):
        return lax.psum_scatter(grad, "fsdp", scatter_dimension=0, tiled=True)

    tokens_held = gather_start(tokens[0])
    places = double_over(positions[0][None], "sp").reshape(-1)
    gains = double_over(jnp.concatenate([attn_gain, mlp_gain, q_gain, k_gain])[None], "fsdp")
    attn_full = gather(
        jnp.concatenate(
            [
                columns(q_weight, qcols), columns(k_weight, kcols), columns(v_weight, kcols),
                columns(g_weight, qcols), columns(o_weight, dcols),
            ],
            axis=1,
        )
    )
    in_cols = 2 * (qcols + kcols)
    onehot = (domain_ids[:, None] == jnp.arange(domain_weights.shape[0], dtype=jnp.int32)).astype(F32)
    seq_scale = loss_weight * jnp.sum(onehot * domain_weights[None, :], axis=1) * SEQ_LEN
    seq_scale = (seq_scale / counts.astype(F32))[0]
    upstream = cotangent[0].astype(F32) * seq_scale
    tokens_held, places, gains = sync(tokens_held, places, gains)
    tokens_held = gather_turn(tokens_held)
    gateup_share = jnp.concatenate([unit_columns(gate_weight), unit_columns(up_weight)], axis=1)
    tokens_held, upstream_low, gateup_share = sync(
        tokens_held, upstream.astype(BF16), gateup_share
    )
    gateup = gather(gateup_share)
    w_gate, w_up = gateup[:, :ffs], gateup[:, ffs:]
    upstream_held = gather_start(upstream_low)
    tokens_all = jnp.concatenate(gather_end(tokens_held), axis=0)

    order = jnp.bitwise_xor(jnp.arange(shards, dtype=jnp.int32), shard.astype(jnp.int32))
    gains = jnp.take(gains, order, axis=0).astype(F32)
    part = attn_gain.shape[0]
    first_gain = gains[:, :part].reshape(-1)
    second_gain = gains[:, part : 2 * part].reshape(-1)
    piece = q_gain.shape[0]
    query_gain = gains[:, 2 * part : 2 * part + piece].reshape(1, HEAD)
    key_gain = gains[:, 2 * part + piece :].reshape(1, HEAD)
    inverse = ROPE_BASE ** (-(2.0 * jnp.arange(HALF, dtype=F32)) / HEAD)
    angles = places.astype(F32)[:, None] * inverse
    cosines, sines = jnp.cos(angles), jnp.sin(angles)
    cosines = jnp.concatenate([cosines, cosines], axis=1)
    sines = jnp.concatenate([-sines, sines], axis=1)
    first = rms_low(tokens_all.astype(F32), first_gain)

    upstream_held, first, cosines, sines = sync(upstream_held, first, cosines, sines)
    upstream_held = gather_turn(upstream_held)
    first, upstream_held = sync(first, upstream_held)
    upstream_all = jnp.concatenate(gather_end(upstream_held), axis=0)
    first, upstream_all = sync(first, upstream_all)

    w_in = attn_full[:, :in_cols]
    o_slices = attn_full[:, in_cols:].reshape(count, qcols, dcols)
    o_blocks = [
        lax.dynamic_index_in_dim(o_slices, jnp.bitwise_xor(rank, j), 0, False) for j in range(count)
    ]
    first, o_blocks = sync(first, o_blocks)
    o_blocks = [swap(block, j) if j else block for j, block in enumerate(o_blocks)]
    raw = mm(first, w_in)
    raw, o_blocks = sync(raw, o_blocks)
    w_out = place_blocks(o_blocks, rank, 1)
    gated, mix, lse = attend_forward(
        rank_ref, raw, cosines, sines, query_gain, key_gain, count, groups, kv_local
    )
    down_share = lax.dynamic_slice_in_dim(down_weight, rank * units, units, 0)
    down_share, gated = sync(down_share, gated)
    w_down = gather(down_share)

    def out_rows(lo, hi):
        return mm(gated[lo:hi], w_out)

    corner = scatter_start(corner_rows(out_rows, rows))
    others = other_rows(out_rows, rows)
    own_part = out_rows(0, rows)
    middle, second = middle_and_second(
        tokens[0], own_part, scatter_turn(others, corner), second_gain
    )
    second = jnp.concatenate(gather_blocks(second), axis=0)

    gate_act = mm(second, w_gate)
    up_act = mm(second, w_up)
    opening = jax.nn.sigmoid(gate_act)
    silu = gate_act * opening
    hidden = (silu * up_act).astype(BF16)
    down_grad, hidden, upstream_now = sync(
        mm(hidden, upstream_all, TN).astype(BF16), hidden, upstream_all
    )
    down_share = scatter(down_grad)

    def down_rows(lo, hi):
        return mm(hidden[lo:hi], w_down)

    block_corner = corner_rows(down_rows, rows)
    block_others = other_rows(down_rows, rows)
    block_part = down_rows(0, rows)
    block_corner, block_others, block_part, upstream_now = sync(
        block_corner, block_others, block_part, upstream_now
    )
    block_corner = scatter_start(block_corner)
    grad_hidden = mm(upstream_now, w_down, NT)
    grad_gate = (grad_hidden * up_act * opening * (1.0 + gate_act * (1.0 - opening))).astype(BF16)
    grad_up = (grad_hidden * silu).astype(BF16)
    grad_gate, grad_up, block_corner = sync(grad_gate, grad_up, block_corner)
    block_came = scatter_turn(block_others, block_corner)
    gateup_grad = mm(second, jnp.concatenate([grad_gate, grad_up], axis=1), TN).astype(BF16)
    gateup_grad, grad_gate, grad_up, block_came = sync(gateup_grad, grad_gate, grad_up, block_came)
    gateup_share = scatter(gateup_grad)

    def second_rows(lo, hi):
        return mm(grad_gate[lo:hi], w_gate, NT) + mm(grad_up[lo:hi], w_up, NT)

    corner = scatter_start(corner_rows(second_rows, rows))
    others = other_rows(second_rows, rows)
    own_part = second_rows(0, rows)
    own_part, corner, others = sync(own_part, corner, others)
    came = scatter_turn(others, corner)
    block_out = (middle + scatter_end(block_part, block_came)).astype(BF16)
    came, block_out = sync(came, block_out)
    grad_middle, grad_attn = norm_back(middle, upstream, own_part, came, second_gain, True)
    grad_attn = gather_start(grad_attn)
    grad_attn = jnp.concatenate(gather_end(gather_turn(grad_attn)), axis=0)

    grad_gated = mm(grad_attn, w_out, NT).astype(BF16)
    out_grad = mm(gated, grad_attn, TN).astype(BF16)
    out_blocks = [
        lax.dynamic_slice_in_dim(out_grad, jnp.bitwise_xor(rank, j) * dcols, dcols, 1)
        for j in range(count)
    ]
    grad_gated, out_blocks, down_share = sync(grad_gated, out_blocks, down_share)
    out_blocks = [swap(block, j) if j else block for j, block in enumerate(out_blocks)]
    down_held = gather_start(down_share)
    grad_raw, query_gain_part, key_gain_part = attend_backward(
        rank_ref, raw, cosines, sines, query_gain, key_gain, mix, lse, grad_gated,
        count, groups, kv_local,
    )
    steps = sum_steps()
    gain_sums = jnp.concatenate([query_gain_part, key_gain_part], axis=1)
    attn_grad = mm(first, grad_raw, TN).astype(BF16)
    attn_grad, grad_raw, gain_sums, out_blocks = sync(attn_grad, grad_raw, gain_sums, out_blocks)

    def first_rows(lo, hi):
        return mm(grad_raw[lo:hi], w_in, NT)

    corner = corner_rows(first_rows, rows)
    corner, grad_raw, attn_grad, gain_sums = sync(corner, grad_raw, attn_grad, gain_sums)
    corner = scatter_start(corner)
    gain_sums = sum_over(gain_sums, steps[:1])
    others = other_rows(first_rows, rows)
    first_part = first_rows(0, rows)
    out_grad = place_blocks(out_blocks, rank, 0)
    attn_grad, out_grad, others, first_part, corner, down_held, gain_sums = sync(
        attn_grad, out_grad, others, first_part, corner, down_held, gain_sums
    )
    came = scatter_turn(others, corner)
    gateup_share, attn_grad, out_grad = sync(gateup_share, attn_grad, out_grad)
    attn_share = scatter(attn_grad)
    out_share = scatter(out_grad)
    gateup_held = gather_start(gateup_share)
    gain_sums = sum_over(gain_sums, steps[1:2])
    came, gain_sums, gateup_held = sync(came, gain_sums, gateup_held)
    gateup_held = gather_turn(gateup_held)
    down_held = gather_turn(down_held)
    (input_grad,) = norm_back(tokens[0], grad_middle, first_part, came, first_gain, False)
    gateup_held, gain_sums, input_grad, attn_share, down_held = sync(
        gateup_held, gain_sums, input_grad, attn_share, down_held
    )
    attn_held = gather_start(attn_share)
    gain_sums = sum_over(gain_sums, steps[2:3])
    gateup_pieces = gather_pieces(gateup_held)
    gate_grad, gate_sums = weave_units(rank_ref, gateup_pieces, 0, gate_weight, shards)
    attn_held, out_share, gate_grad, gain_sums = sync(attn_held, out_share, gate_grad, gain_sums)
    attn_held = gather_turn(attn_held)
    out_held = gather_start(out_share)
    gain_sums = sum_over(gain_sums, steps[3:4])
    down_grad = stack_rows(rank_ref, gather_pieces(down_held))
    up_grad, up_sums = weave_units(rank_ref, gateup_pieces, 1, up_weight, shards)
    attn_held, out_held, gain_sums, up_grad, down_grad = sync(
        attn_held, out_held, gain_sums, up_grad, down_grad
    )
    out_held = gather_turn(out_held)
    gain_sums = sum_over(gain_sums, steps[4:])
    *attn_grads, in_sums = split_columns(
        rank_ref, gather_pieces(attn_held), (qcols, kcols, kcols, qcols),
        (q_weight, k_weight, v_weight, g_weight),
    )
    (out_grad,) = split_columns(rank_ref, gather_pieces(out_held), (dcols,))
    attn_gain_grad = in_sums[:, 0] / attn_gain.astype(F32)
    mlp_gain_grad = (gate_sums + up_sums)[:, 0] / mlp_gain.astype(F32)

    def own(values):
        size = values.shape[0] // shards
        return lax.dynamic_slice_in_dim(values, shard * size, size, 0)

    return (
        block_out[None],
        input_grad[None],
        *attn_grads,
        out_grad,
        gate_grad,
        up_grad,
        down_grad,
        attn_gain_grad,
        mlp_gain_grad,
        own(gain_sums[0, :HEAD]),
        own(gain_sums[0, HEAD:]),
    )


def solution(mesh):
    both, over_fsdp = P("fsdp", "sp", None), P("fsdp", None)
    return jax.shard_map(
        on_device,
        mesh=mesh,
        in_specs=(both, both, P("fsdp", "sp"), P("fsdp"), P("fsdp"), P("fsdp"), P())
        + (over_fsdp,) * 8
        + (P("fsdp"),) * 4,
        out_specs=(both, both) + (over_fsdp,) * 8 + (P("fsdp"),) * 4,
        check_vma=False,
    )
```

```python
import functools

import jax
import jax.numpy as jnp
from jax import lax
from jax.experimental import pallas as pl
from jax.experimental.pallas import tpu as pltpu
from jax.sharding import PartitionSpec as P

HEAD = 128
HALF = HEAD // 2
SEQ_LEN = 1024
EPS = 1e-06
ROPE_BASE = 1000000.0
SCALE = HEAD ** (-0.5)
LOG2E = 1.4426950408889634
VMEM_LIMIT = 56 * 1024 * 1024
NT = (((1,), (1,)), ((), ()))
NN = (((1,), (0,)), ((), ()))
TN = (((0,), (0,)), ((), ()))
F32 = jnp.float32
BF16 = jnp.bfloat16


def mm(left, right, dims=NN):
    return lax.dot_general(left, right, dims, preferred_element_type=F32)


def head_norm(raw):
    return lax.rsqrt(jnp.mean(raw * raw, axis=-1, keepdims=True) + EPS)


def turn(values, cosines, sines):
    return values * cosines + pltpu.roll(values, HALF, 1) * sines


def turn_back(values, cosines, sines):
    return values * cosines - pltpu.roll(values, HALF, 1) * sines


def norm_turn(raw, gain, cosines, sines):
    return turn(raw * head_norm(raw) * gain, cosines, sines).astype(BF16)


def norm_turn_back(raw, gain, grad, cosines, sines):
    back = turn_back(grad, cosines, sines)
    scale = head_norm(raw)
    pulled = back * gain
    inner = jnp.mean(raw * pulled, axis=-1, keepdims=True)
    gain_part = jnp.sum(raw * scale * back, axis=0, keepdims=True)
    return scale * pulled - raw * (scale * scale * scale * inner), gain_part


def diagonal_mask(rows, groups):
    keys = lax.broadcasted_iota(jnp.int32, (rows, groups * rows), 0)
    places = lax.broadcasted_iota(jnp.int32, (rows, groups * rows), 1)
    return keys <= lax.rem(places, rows)


def row_block(block, rank, rows):
    return pl.ds(pl.multiple_of(jnp.bitwise_xor(block, rank) * rows, rows), rows)


def attend_fwd_kernel(
    blocks, rows, groups,
    rank_ref, q_ref, k_ref, v_ref, g_ref, cos_ref, sin_ref, qg_ref, kg_ref,
    gated_ref, mix_ref, lse_ref, keys, vals_t,
):
    rank = rank_ref[0]
    factor = SCALE * LOG2E
    for a in range(blocks):
        place = row_block(a, rank, rows)
        here = slice(a * rows, (a + 1) * rows)
        keys[here, :] = norm_turn(k_ref[place, :], kg_ref[...], cos_ref[place, :], sin_ref[place, :])
        vals_t[:, here] = v_ref[place, :].T.astype(BF16)
    mask = diagonal_mask(rows, groups)
    for a in range(blocks):
        place = row_block(a, rank, rows)
        cosines, sines = cos_ref[place, :], sin_ref[place, :]
        queries = jnp.concatenate(
            [
                norm_turn(q_ref[place, h * HEAD : (h + 1) * HEAD], qg_ref[...], cosines, sines)
                for h in range(groups)
            ],
            axis=0,
        )
        low, high = a * rows, (a + 1) * rows
        near = jnp.where(mask, mm(keys[low:high, :], queries, NT), -1e30)
        peak = jnp.max(near, axis=0, keepdims=True)
        if a:
            far = mm(keys[:low, :], queries, NT)
            peak = jnp.maximum(peak, jnp.max(far, axis=0, keepdims=True))
        near = jnp.exp2((near - peak) * factor)
        total = jnp.sum(near, axis=0, keepdims=True)
        if a:
            far = jnp.exp2((far - peak) * factor)
            total = total + jnp.sum(far, axis=0, keepdims=True)
        inverse = 1.0 / total
        mix_t = mm(vals_t[:, low:high], (near * inverse).astype(BF16))
        if a:
            mix_t = mix_t + mm(vals_t[:, :low], (far * inverse).astype(BF16))
        mix = mix_t.T
        for h in range(groups):
            cols = slice(h * HEAD, (h + 1) * HEAD)
            part = mix[h * rows : (h + 1) * rows, :]
            opening = jax.nn.sigmoid(g_ref[place, cols].astype(BF16).astype(F32))
            mix_ref[place, cols] = part
            gated_ref[place, cols] = (part * opening).astype(BF16)
        lse_ref[0, a : a + 1, :] = peak * factor + jnp.log2(total)


def attend_bwd_kernel(
    blocks, rows, groups, kv_local,
    rank_ref, q_ref, k_ref, v_ref, g_ref, cos_ref, sin_ref, qg_ref, kg_ref, mix_ref, lse_ref, up_ref,
    grad_ref, qgain_ref, kgain_ref, keys, keys_t, vals, dkeys, dvals,
):
    rank = rank_ref[0]
    step = pl.program_id(0)
    factor = SCALE * LOG2E
    width = groups * HEAD

    @pl.when(step == 0)
    def _():
        qgain_ref[...] = jnp.zeros_like(qgain_ref)
        kgain_ref[...] = jnp.zeros_like(kgain_ref)

    for a in range(blocks):
        place = row_block(a, rank, rows)
        here = slice(a * rows, (a + 1) * rows)
        block = norm_turn(k_ref[place, :], kg_ref[...], cos_ref[place, :], sin_ref[place, :])
        keys[here, :] = block
        keys_t[:, here] = block.astype(F32).T.astype(BF16)
        vals[here, :] = v_ref[place, :].astype(BF16)
    mask = diagonal_mask(rows, groups)
    qgain = jnp.zeros((1, HEAD), F32)
    for a in reversed(range(blocks)):
        place = row_block(a, rank, rows)
        cosines, sines = cos_ref[place, :], sin_ref[place, :]
        queries, grads = [], []
        for h in range(groups):
            cols = slice(h * HEAD, (h + 1) * HEAD)
            queries.append(norm_turn(q_ref[place, cols], qg_ref[...], cosines, sines))
            upstream = up_ref[place, cols].astype(F32)
            opening = jax.nn.sigmoid(g_ref[place, cols].astype(BF16).astype(F32))
            opened = upstream * opening
            grads.append(opened.astype(BF16))
            grad_ref[
                place, pl.ds((kv_local * (groups + 2)) * HEAD + step * width + h * HEAD, HEAD)
            ] = (opened * mix_ref[place, cols] * (1.0 - opening)).astype(BF16)
        queries = jnp.concatenate(queries, axis=0)
        grads = jnp.concatenate(grads, axis=0)
        lse = lse_ref[0, a : a + 1, :]
        low, high = a * rows, (a + 1) * rows
        spans = [(low, high)] + ([(0, low)] if a else [])
        chances, grad_chances = [], []
        centre = jnp.zeros((1, groups * rows), F32)
        for start, stop in spans:
            part = jnp.exp2(mm(keys[start:stop, :], queries, NT) * factor - lse)
            if start == low:
                part = jnp.where(mask, part, 0.0)
            pull = mm(vals[start:stop, :], grads, NT)
            centre = centre + jnp.sum(part * pull, axis=0, keepdims=True)
            chances.append(part)
            grad_chances.append(pull)
        dq_t = jnp.zeros((HEAD, groups * rows), F32)
        for (start, stop), part, pull in zip(spans, chances, grad_chances):
            grad_products = (part * (pull - centre) * SCALE).astype(BF16)
            dval = mm(part.astype(BF16), grads)
            dkey = mm(grad_products, queries)
            if a == blocks - 1:
                dvals[start:stop, :] = dval
                dkeys[start:stop, :] = dkey
            else:
                dvals[start:stop, :] += dval
                dkeys[start:stop, :] += dkey
            dq_t = dq_t + mm(keys_t[:, start:stop], grad_products)
        dq = dq_t.T
        for h in range(groups):
            grad = dq[h * rows : (h + 1) * rows, :].astype(BF16).astype(F32)
            cols = slice(h * HEAD, (h + 1) * HEAD)
            raw, gain_part = norm_turn_back(q_ref[place, cols], qg_ref[...], grad, cosines, sines)
            grad_ref[place, pl.ds(step * width + h * HEAD, HEAD)] = raw.astype(BF16)
            qgain = qgain + gain_part
    kgain = jnp.zeros((1, HEAD), F32)
    for a in range(blocks):
        place = row_block(a, rank, rows)
        here = slice(a * rows, (a + 1) * rows)
        grad = dkeys[here, :].astype(BF16).astype(F32)
        raw, gain_part = norm_turn_back(
            k_ref[place, :], kg_ref[...], grad, cos_ref[place, :], sin_ref[place, :]
        )
        kgain = kgain + gain_part
        grad_ref[place, pl.ds(kv_local * width + step * HEAD, HEAD)] = raw.astype(BF16)
        grad_ref[place, pl.ds(kv_local * (width + HEAD) + step * HEAD, HEAD)] = dvals[
            here, :
        ].astype(BF16)
    qgain_ref[...] += qgain
    kgain_ref[...] += kgain


def attention_specs(length, groups, kv_local):
    width = groups * HEAD
    return [
        pl.BlockSpec((length, width), lambda g, r: (0, g)),
        pl.BlockSpec((length, HEAD), lambda g, r: (0, kv_local * groups + g)),
        pl.BlockSpec((length, HEAD), lambda g, r: (0, kv_local * (groups + 1) + g)),
        pl.BlockSpec((length, width), lambda g, r: (0, kv_local * (groups + 2) // groups + g)),
        pl.BlockSpec((length, HEAD), lambda g, r: (0, 0)),
        pl.BlockSpec((length, HEAD), lambda g, r: (0, 0)),
        pl.BlockSpec((1, HEAD), lambda g, r: (0, 0)),
        pl.BlockSpec((1, HEAD), lambda g, r: (0, 0)),
    ]


def attend_forward(rank, raw, cosines, sines, q_gain, k_gain, blocks, groups, kv_local):
    length = raw.shape[0]
    rows = length // blocks
    width = groups * HEAD
    flops = 4 * kv_local * groups * length * length * HEAD * (blocks + 1) // (2 * blocks)
    return pl.pallas_call(
        functools.partial(attend_fwd_kernel, blocks, rows, groups),
        grid_spec=pltpu.PrefetchScalarGridSpec(
            num_scalar_prefetch=1,
            grid=(kv_local,),
            in_specs=attention_specs(length, groups, kv_local),
            out_specs=[
                pl.BlockSpec((length, width), lambda g, r: (0, g)),
                pl.BlockSpec((length, width), lambda g, r: (0, g)),
                pl.BlockSpec((1, blocks, groups * rows), lambda g, r: (g, 0, 0)),
            ],
            scratch_shapes=[pltpu.VMEM((length, HEAD), BF16), pltpu.VMEM((HEAD, length), BF16)],
        ),
        out_shape=[
            jax.ShapeDtypeStruct((length, kv_local * width), BF16),
            jax.ShapeDtypeStruct((length, kv_local * width), F32),
            jax.ShapeDtypeStruct((kv_local, blocks, groups * rows), F32),
        ],
        compiler_params=pltpu.CompilerParams(
            dimension_semantics=("arbitrary",), vmem_limit_bytes=VMEM_LIMIT
        ),
        cost_estimate=pl.CostEstimate(
            flops=4 * flops,
            bytes_accessed=raw.size * 4 + length * kv_local * width * 6,
            transcendentals=kv_local * groups * length * length // 2,
        ),
        name="attend_forward",
    )(rank, raw, raw, raw, raw, cosines, sines, q_gain, k_gain)


def attend_backward(
    rank, raw, cosines, sines, q_gain, k_gain, mix, lse, upstream, blocks, groups, kv_local
):
    length = raw.shape[0]
    rows = length // blocks
    width = groups * HEAD
    flops = 10 * kv_local * groups * length * length * HEAD * (blocks + 1) // (2 * blocks)
    return pl.pallas_call(
        functools.partial(attend_bwd_kernel, blocks, rows, groups, kv_local),
        grid_spec=pltpu.PrefetchScalarGridSpec(
            num_scalar_prefetch=1,
            grid=(kv_local,),
            in_specs=attention_specs(length, groups, kv_local)
            + [
                pl.BlockSpec((length, width), lambda g, r: (0, g)),
                pl.BlockSpec((1, blocks, groups * rows), lambda g, r: (g, 0, 0)),
                pl.BlockSpec((length, width), lambda g, r: (0, g)),
            ],
            out_specs=[
                pl.BlockSpec(raw.shape, lambda g, r: (0, 0)),
                pl.BlockSpec((1, HEAD), lambda g, r: (0, 0)),
                pl.BlockSpec((1, HEAD), lambda g, r: (0, 0)),
            ],
            scratch_shapes=[
                pltpu.VMEM((length, HEAD), BF16),
                pltpu.VMEM((HEAD, length), BF16),
                pltpu.VMEM((length, HEAD), BF16),
                pltpu.VMEM((length, HEAD), F32),
                pltpu.VMEM((length, HEAD), F32),
            ],
        ),
        out_shape=[
            jax.ShapeDtypeStruct(raw.shape, BF16),
            jax.ShapeDtypeStruct((1, HEAD), F32),
            jax.ShapeDtypeStruct((1, HEAD), F32),
        ],
        compiler_params=pltpu.CompilerParams(
            dimension_semantics=("arbitrary",), vmem_limit_bytes=VMEM_LIMIT
        ),
        cost_estimate=pl.CostEstimate(
            flops=4 * flops,
            bytes_accessed=raw.size * 6 + length * kv_local * width * 6,
            transcendentals=kv_local * groups * length * length // 2,
        ),
        name="attend_backward",
    )(rank, raw, raw, raw, raw, cosines, sines, q_gain, k_gain, mix, lse, upstream)


def middle_kernel(tokens_ref, own_ref, x_ref, y_ref, gain_ref, middle_ref, second_ref):
    middle = tokens_ref[...].astype(F32) + own_ref[...]
    middle = middle + x_ref[...].astype(F32) + y_ref[...].astype(F32)
    scale = lax.rsqrt(jnp.mean(middle * middle, axis=-1, keepdims=True) + EPS)
    middle_ref[...] = middle
    second_ref[...] = (middle * scale * gain_ref[...]).astype(BF16)


def norm_back_kernel(low, values_ref, base_ref, own_ref, x_ref, y_ref, gain_ref, grad_ref, *low_ref):
    values = values_ref[...].astype(F32)
    grad = own_ref[...] + x_ref[...].astype(F32) + y_ref[...].astype(F32)
    scale = lax.rsqrt(jnp.mean(values * values, axis=-1, keepdims=True) + EPS)
    normed = values * scale
    pulled = grad * gain_ref[...]
    inner = jnp.mean(normed * pulled, axis=-1, keepdims=True)
    total = base_ref[...] + scale * (pulled - normed * inner)
    grad_ref[...] = total
    if low:
        low_ref[0][...] = total.astype(BF16)


def row_call(kernel, name, arrays, gain, outs):
    rows, width = arrays[0].shape
    tile = rows // 4

    def spec(shape):
        if shape[0] == rows:
            return pl.BlockSpec((tile, width), lambda i: (i, 0))
        return pl.BlockSpec((1, width), lambda i: (0, 0))

    return pl.pallas_call(
        kernel,
        grid=(4,),
        in_specs=[spec(a.shape) for a in arrays] + [spec(gain.shape)],
        out_specs=[spec(o.shape) for o in outs],
        out_shape=outs,
        compiler_params=pltpu.CompilerParams(
            dimension_semantics=("arbitrary",), vmem_limit_bytes=VMEM_LIMIT
        ),
        cost_estimate=pl.CostEstimate(
            flops=16 * rows * width, bytes_accessed=18 * rows * width, transcendentals=rows
        ),
        name=name,
    )(*arrays, gain)


def two_addends(came):
    if len(came) == 2:
        return came
    return [sum(part.astype(F32) for part in came[:-1]), came[-1]]


def middle_and_second(tokens, own, came, gain):
    return row_call(
        middle_kernel, "middle_and_second", [tokens, own, *two_addends(came)], gain[None],
        [jax.ShapeDtypeStruct(own.shape, F32), jax.ShapeDtypeStruct(own.shape, BF16)],
    )


def norm_back(values, base, own, came, gain, low):
    outs = [jax.ShapeDtypeStruct(own.shape, F32)] + [jax.ShapeDtypeStruct(own.shape, BF16)] * low
    return row_call(
        functools.partial(norm_back_kernel, low), "norm_back",
        [values, base, own, *two_addends(came)], gain[None], outs,
    )


def flat_specs(pieces, spec):
    return [spec(piece) for block in pieces for piece in block]


def grouped(refs, counts):
    blocks, start = [], 0
    for count in counts:
        blocks.append(refs[start : start + count])
        start += count
    return blocks, refs[start:]


def split_columns_kernel(counts, sizes, weighed, rank_ref, *refs):
    sources, refs = grouped(refs, counts)
    weights, outs, sums = refs[:weighed], refs[weighed : weighed + len(sizes)], refs[-1]
    block = jnp.bitwise_xor(pl.program_id(0), rank_ref[0])
    for j, pieces in enumerate(sources):

        @pl.when(block == j)
        def _(pieces=pieces):
            top = 0
            for piece in pieces:
                start, stop = 0, top + piece.shape[0]
                for size, out in zip(sizes, outs):
                    out[top:stop, :] = piece[:, start : start + size].astype(F32)
                    start += size
                top = stop

    if weighed:
        part = sum(
            jnp.sum(out[...] * weight[...].astype(F32), axis=1, keepdims=True)
            for out, weight in zip(outs, weights)
        )

        @pl.when(pl.program_id(0) == 0)
        def _():
            sums[...] = jnp.zeros_like(sums)

        sums[...] += part


def split_columns(rank, pieces, sizes, weights=()):
    count, rows = len(pieces), pieces[0][0].shape[0]
    group_specs = [pl.BlockSpec((rows, size), lambda a, r: (0, a)) for size in sizes]
    sum_specs = [pl.BlockSpec((rows, 1), lambda a, r: (0, 0))] if weights else []
    return pl.pallas_call(
        functools.partial(
            split_columns_kernel, [len(block) for block in pieces], sizes, len(weights)
        ),
        grid_spec=pltpu.PrefetchScalarGridSpec(
            num_scalar_prefetch=1,
            grid=(count,),
            in_specs=flat_specs(pieces, lambda p: pl.BlockSpec(p.shape, lambda a, r: (0, 0)))
            + group_specs[: len(weights)],
            out_specs=group_specs + sum_specs,
        ),
        out_shape=[jax.ShapeDtypeStruct((rows, count * size), F32) for size in sizes]
        + [jax.ShapeDtypeStruct((rows, 1), F32)] * len(sum_specs),
        compiler_params=pltpu.CompilerParams(
            dimension_semantics=("arbitrary",), vmem_limit_bytes=VMEM_LIMIT
        ),
        cost_estimate=pl.CostEstimate(
            flops=0, bytes_accessed=6 * rows * count * sum(sizes), transcendentals=0
        ),
        name="split_columns",
    )(rank, *sum(pieces, []), *weights)


def stack_rows_kernel(counts, rank_ref, *refs):
    sources, (out,) = grouped(refs, counts)
    block = jnp.bitwise_xor(pl.program_id(0), rank_ref[0])
    for j, pieces in enumerate(sources):

        @pl.when(block == j)
        def _(pieces=pieces):
            top = 0
            for piece in pieces:
                out[top : top + piece.shape[0], :] = piece[...].astype(F32)
                top += piece.shape[0]


def stack_rows(rank, pieces):
    count, (rows, width) = len(pieces), pieces[0][0].shape
    return pl.pallas_call(
        functools.partial(stack_rows_kernel, [len(block) for block in pieces]),
        grid_spec=pltpu.PrefetchScalarGridSpec(
            num_scalar_prefetch=1,
            grid=(count,),
            in_specs=flat_specs(pieces, lambda p: pl.BlockSpec(p.shape, lambda a, r: (0, 0))),
            out_specs=pl.BlockSpec((rows, width), lambda a, r: (a, 0)),
        ),
        out_shape=jax.ShapeDtypeStruct((count * rows, width), F32),
        compiler_params=pltpu.CompilerParams(
            dimension_semantics=("arbitrary",), vmem_limit_bytes=VMEM_LIMIT
        ),
        cost_estimate=pl.CostEstimate(
            flops=0, bytes_accessed=6 * rows * count * width, transcendentals=0
        ),
        name="stack_rows",
    )(rank, *sum(pieces, []))


def weave_units_kernel(counts, steps, shards, units, rank_ref, *refs):
    sources, (weight, out, sums, held) = grouped(refs, counts)
    step = pl.program_id(0)
    for j, pieces in enumerate(sources):
        place = jnp.bitwise_xor(rank_ref[0], j)
        if len(pieces) == 1:
            held[place] = pieces[0][...].astype(F32)
            continue
        share = steps // len(pieces)
        for k, piece in enumerate(pieces):

            @pl.when((step >= k * share) & (step < (k + 1) * share))
            def _(piece=piece, place=place):
                held[place] = piece[...].astype(F32)

    count = len(counts)
    for a in range(count):
        for f in range(shards):
            start = (f * count + a) * units
            out[:, start : start + units] = held[a, :, f * units : (f + 1) * units]
    sums[...] = jnp.sum(out[...] * weight[...].astype(F32), axis=1, keepdims=True)


def weave_units(rank, pieces, group, weight, shards):
    count, (rows, width) = len(pieces), pieces[0][0].shape
    ffs, steps = width // 2, 4
    tile = rows // steps

    def spec(block, k):
        share = steps // len(block)

        def place(i, r):
            return (jnp.clip(i - k * share, 0, share - 1), group)

        return pl.BlockSpec((tile, ffs), place)

    return pl.pallas_call(
        functools.partial(
            weave_units_kernel, [len(block) for block in pieces], steps, shards, ffs // shards
        ),
        grid_spec=pltpu.PrefetchScalarGridSpec(
            num_scalar_prefetch=1,
            grid=(steps,),
            in_specs=[spec(block, k) for block in pieces for k in range(len(block))]
            + [pl.BlockSpec((tile, count * ffs), lambda i, r: (i, 0))],
            out_specs=[
                pl.BlockSpec((tile, count * ffs), lambda i, r: (i, 0)),
                pl.BlockSpec((tile, 1), lambda i, r: (i, 0)),
            ],
            scratch_shapes=[pltpu.VMEM((count, tile, ffs), F32)],
        ),
        out_shape=[
            jax.ShapeDtypeStruct((rows, count * ffs), F32), jax.ShapeDtypeStruct((rows, 1), F32),
        ],
        compiler_params=pltpu.CompilerParams(
            dimension_semantics=("arbitrary",), vmem_limit_bytes=VMEM_LIMIT
        ),
        cost_estimate=pl.CostEstimate(
            flops=0, bytes_accessed=8 * rows * count * ffs, transcendentals=0
        ),
        name="weave_units",
    )(rank, *sum(pieces, []), weight)


def column_shares_kernel(rank_ref, *refs):
    start = 0
    for ref in refs[:-1]:
        refs[-1][:, start : start + ref.shape[1]] = ref[...]
        start += ref.shape[1]


def column_shares(rank, weights, sizes):
    rows, width = weights[0].shape[0], sum(sizes)
    tile = rows // 2
    return pl.pallas_call(
        column_shares_kernel,
        grid_spec=pltpu.PrefetchScalarGridSpec(
            num_scalar_prefetch=1,
            grid=(2,),
            in_specs=[pl.BlockSpec((tile, size), lambda i, r: (i, r[0])) for size in sizes],
            out_specs=pl.BlockSpec((tile, width), lambda i, r: (i, 0)),
        ),
        out_shape=jax.ShapeDtypeStruct((rows, width), weights[0].dtype),
        compiler_params=pltpu.CompilerParams(
            dimension_semantics=("arbitrary",), vmem_limit_bytes=VMEM_LIMIT
        ),
        cost_estimate=pl.CostEstimate(
            flops=0, bytes_accessed=4 * rows * width, transcendentals=0
        ),
        name="column_shares",
    )(rank, *weights)


def swap(values, bit, axis="sp"):
    return lax.ppermute(values, axis, [(i, i ^ bit) for i in range(lax.axis_size(axis))])


def sync(*values):
    return lax.optimization_barrier(values)


def gather_start(block):
    return [block] + [swap(block, j) for j in range(1, lax.axis_size("sp"))][: 2 if lax.axis_size("sp") == 4 else None]


def gather_turn(held):
    if lax.axis_size("sp") != 4:
        return held
    half = held[0].shape[0] // 2
    return held + [swap(held[2][:half], 1), swap(held[1][half:], 2)]


def gather_end(held):
    if lax.axis_size("sp") != 4:
        return held
    return held[:3] + [jnp.concatenate(held[3:], axis=0)]


def gather_blocks(block):
    return gather_end(gather_turn(gather_start(block)))


def gather_pieces(held):
    if lax.axis_size("sp") != 4:
        return [[block] for block in held]
    return [[block] for block in held[:3]] + [held[3:]]


def scatter_start(corner):
    if lax.axis_size("sp") != 4:
        return []
    half = corner.shape[0] // 2
    return [swap(corner[:half], 1), swap(corner[half:], 2)]


def scatter_turn(others, came):
    if lax.axis_size("sp") != 4:
        return [swap(part.astype(BF16), j + 1) for j, part in enumerate(others)]
    half = others[0].shape[0] // 2
    to_x = jnp.concatenate([others[0][:half], others[0][half:] + came[1].astype(F32)], axis=0)
    to_y = jnp.concatenate([others[1][:half] + came[0].astype(F32), others[1][half:]], axis=0)
    return [swap(to_x.astype(BF16), 1), swap(to_y.astype(BF16), 2)]


def scatter_end(own, came):
    for part in came:
        own = own + part.astype(F32)
    return own


def corner_rows(make, rows):
    count = lax.axis_size("sp")
    return make((count - 1) * rows, count * rows).astype(BF16) if count == 4 else None


def other_rows(make, rows):
    count = lax.axis_size("sp")
    stop = 3 if count == 4 else count
    whole = make(rows, stop * rows)
    return [whole[j * rows : (j + 1) * rows] for j in range(stop - 1)]


def place_blocks(blocks, rank, axis):
    size = blocks[0].shape[axis]
    shape = list(blocks[0].shape)
    shape[axis] = size * len(blocks)
    whole = jnp.zeros(shape, blocks[0].dtype)
    for j, block in enumerate(blocks):
        whole = lax.dynamic_update_slice_in_dim(
            whole, block, jnp.bitwise_xor(rank, j) * size, axis
        )
    return whole


def halve_start(held, bit):
    shard = lax.axis_index("fsdp")
    mine = jnp.bitwise_and(lax.div(shard, jnp.int32(bit)), 1)
    pairs = held.reshape(held.shape[0] // 2, 2, held.shape[1], held.shape[2])
    sent = lax.dynamic_index_in_dim(pairs, 1 - mine, 1, False)
    kept = lax.dynamic_index_in_dim(pairs, mine, 1, False)
    return kept, swap(sent, bit, "fsdp")


def halve_end(state):
    return (state[0].astype(F32) + state[1].astype(F32)).astype(BF16)


def halve_open(grad):
    shards = lax.axis_size("fsdp")
    return halve_start(grad.reshape(shards, grad.shape[0] // shards, grad.shape[1]), 1)


def halve_next(state, bit):
    return halve_start(halve_end(state), bit)


def halve_close(state):
    held = halve_end(state)
    while held.shape[0] > 1:
        held = halve_end(halve_start(held, lax.axis_size("fsdp") // held.shape[0]))
    return held[0]


def double_over(values, axis):
    bit = 1
    while bit < lax.axis_size(axis):
        values = jnp.concatenate([values, swap(values, bit, axis)], axis=0)
        bit *= 2
    return values


def sum_steps():
    return [
        (axis, 1 << k)
        for axis in ("sp", "fsdp")
        for k in range((lax.axis_size(axis) - 1).bit_length())
    ]


def sum_over(values, steps):
    for axis, bit in steps:
        values = values + swap(values, bit, axis)
    return values


def rms_low(values, gain):
    scale = lax.rsqrt(jnp.mean(values * values, axis=-1, keepdims=True) + EPS)
    return (values * scale * gain).astype(BF16)


def on_device(
    tokens, cotangent, positions, domain_ids, counts, loss_weight, domain_weights,
    q_weight, k_weight, v_weight, g_weight, o_weight, gate_weight, up_weight, down_weight,
    attn_gain, mlp_gain, q_gain, k_gain,
):
    count, shards = lax.axis_size("sp"), lax.axis_size("fsdp")
    rank, shard = lax.axis_index("sp"), lax.axis_index("fsdp")
    rank_ref = rank.astype(jnp.int32).reshape(1)
    _, rows, width = tokens.shape
    heads_local = q_weight.shape[1] // HEAD // count
    kv_local = k_weight.shape[1] // HEAD // count
    groups = heads_local // kv_local
    qcols, kcols = heads_local * HEAD, kv_local * HEAD
    dcols = width // count
    units = down_weight.shape[0] // count
    ffs = units * shards

    def gather(weight):
        return lax.all_gather(weight, "fsdp", axis=0, tiled=True)

    def unit_columns(weight):
        spread = weight.reshape(weight.shape[0], shards, count, units)
        return lax.dynamic_slice_in_dim(spread, rank, 1, 2).reshape(weight.shape[0], ffs)

    def scatter(grad):
        return lax.psum_scatter(grad, "fsdp", scatter_dimension=0, tiled=True)

    tokens_held = gather_start(tokens[0])
    places = double_over(positions[0][None], "sp").reshape(-1)
    gains = double_over(jnp.concatenate([attn_gain, mlp_gain, q_gain, k_gain])[None], "fsdp")
    attn_full = gather(
        column_shares(
            rank_ref, (q_weight, k_weight, v_weight, g_weight, o_weight),
            (qcols, kcols, kcols, qcols, dcols),
        )
    )
    in_cols = 2 * (qcols + kcols)
    onehot = (domain_ids[:, None] == jnp.arange(domain_weights.shape[0], dtype=jnp.int32)).astype(F32)
    seq_scale = loss_weight * jnp.sum(onehot * domain_weights[None, :], axis=1) * SEQ_LEN
    seq_scale = (seq_scale / counts.astype(F32))[0]
    upstream = cotangent[0].astype(F32) * seq_scale
    tokens_held, places, gains = sync(tokens_held, places, gains)
    tokens_held = gather_turn(tokens_held)
    gateup_share = jnp.concatenate([unit_columns(gate_weight), unit_columns(up_weight)], axis=1)
    tokens_held, upstream_low, gateup_share = sync(
        tokens_held, upstream.astype(BF16), gateup_share
    )
    gateup = gather(gateup_share)
    w_gate, w_up = gateup[:, :ffs], gateup[:, ffs:]
    upstream_held = gather_start(upstream_low)
    tokens_all = jnp.concatenate(gather_end(tokens_held), axis=0)

    order = jnp.bitwise_xor(jnp.arange(shards, dtype=jnp.int32), shard.astype(jnp.int32))
    gains = jnp.take(gains, order, axis=0).astype(F32)
    part = attn_gain.shape[0]
    first_gain = gains[:, :part].reshape(-1)
    second_gain = gains[:, part : 2 * part].reshape(-1)
    piece = q_gain.shape[0]
    query_gain = gains[:, 2 * part : 2 * part + piece].reshape(1, HEAD)
    key_gain = gains[:, 2 * part + piece :].reshape(1, HEAD)
    inverse = ROPE_BASE ** (-(2.0 * jnp.arange(HALF, dtype=F32)) / HEAD)
    angles = places.astype(F32)[:, None] * inverse
    cosines, sines = jnp.cos(angles), jnp.sin(angles)
    cosines = jnp.concatenate([cosines, cosines], axis=1)
    sines = jnp.concatenate([-sines, sines], axis=1)
    first = rms_low(tokens_all.astype(F32), first_gain)

    upstream_held, first, cosines, sines = sync(upstream_held, first, cosines, sines)
    upstream_held = gather_turn(upstream_held)
    first, upstream_held = sync(first, upstream_held)
    upstream_all = jnp.concatenate(gather_end(upstream_held), axis=0)
    first, upstream_all = sync(first, upstream_all)

    w_in = attn_full[:, :in_cols]
    o_slices = attn_full[:, in_cols:].reshape(count, qcols, dcols)
    o_blocks = [
        lax.dynamic_index_in_dim(o_slices, jnp.bitwise_xor(rank, j), 0, False) for j in range(count)
    ]
    first, o_blocks = sync(first, o_blocks)
    o_blocks = [swap(block, j) if j else block for j, block in enumerate(o_blocks)]
    raw = mm(first, w_in)
    raw, o_blocks = sync(raw, o_blocks)
    w_out = place_blocks(o_blocks, rank, 1)
    gated, mix, lse = attend_forward(
        rank_ref, raw, cosines, sines, query_gain, key_gain, count, groups, kv_local
    )
    down_share = lax.dynamic_slice_in_dim(down_weight, rank * units, units, 0)
    down_share, gated = sync(down_share, gated)
    w_down = gather(down_share)

    def out_rows(lo, hi):
        return mm(gated[lo:hi], w_out)

    corner = scatter_start(corner_rows(out_rows, rows))
    others = other_rows(out_rows, rows)
    own_part = out_rows(0, rows)
    middle, second = middle_and_second(
        tokens[0], own_part, scatter_turn(others, corner), second_gain
    )
    second = jnp.concatenate(gather_blocks(second), axis=0)

    gate_act = mm(second, w_gate)
    up_act = mm(second, w_up)
    opening = jax.nn.sigmoid(gate_act)
    silu = gate_act * opening
    hidden = (silu * up_act).astype(BF16)
    down_grad, hidden, upstream_now = sync(
        mm(hidden, upstream_all, TN).astype(BF16), hidden, upstream_all
    )
    down_share = scatter(down_grad)

    def down_rows(lo, hi):
        return mm(hidden[lo:hi], w_down)

    block_corner = corner_rows(down_rows, rows)
    block_others = other_rows(down_rows, rows)
    block_part = down_rows(0, rows)
    block_corner, block_others, block_part, upstream_now = sync(
        block_corner, block_others, block_part, upstream_now
    )
    block_corner = scatter_start(block_corner)
    grad_hidden = mm(upstream_now, w_down, NT)
    grad_gate = (grad_hidden * up_act * opening * (1.0 + gate_act * (1.0 - opening))).astype(BF16)
    grad_up = (grad_hidden * silu).astype(BF16)
    grad_gate, grad_up, block_corner = sync(grad_gate, grad_up, block_corner)
    block_came = scatter_turn(block_others, block_corner)
    gateup_grad = mm(second, jnp.concatenate([grad_gate, grad_up], axis=1), TN).astype(BF16)
    gateup_grad, grad_gate, grad_up, block_came = sync(gateup_grad, grad_gate, grad_up, block_came)
    gateup_share = scatter(gateup_grad)

    def second_rows(lo, hi):
        return mm(grad_gate[lo:hi], w_gate, NT) + mm(grad_up[lo:hi], w_up, NT)

    corner = scatter_start(corner_rows(second_rows, rows))
    others = other_rows(second_rows, rows)
    own_part = second_rows(0, rows)
    own_part, corner, others = sync(own_part, corner, others)
    came = scatter_turn(others, corner)
    block_out = (middle + scatter_end(block_part, block_came)).astype(BF16)
    came, block_out = sync(came, block_out)
    grad_middle, grad_attn = norm_back(middle, upstream, own_part, came, second_gain, True)
    grad_attn = gather_start(grad_attn)
    grad_attn = jnp.concatenate(gather_end(gather_turn(grad_attn)), axis=0)

    grad_gated = mm(grad_attn, w_out, NT).astype(BF16)
    out_grad = mm(gated, grad_attn, TN).astype(BF16)
    out_blocks = [
        lax.dynamic_slice_in_dim(out_grad, jnp.bitwise_xor(rank, j) * dcols, dcols, 1)
        for j in range(count)
    ]
    grad_gated, out_blocks, down_share = sync(grad_gated, out_blocks, down_share)
    out_blocks = [swap(block, j) if j else block for j, block in enumerate(out_blocks)]
    down_held = gather_start(down_share)
    grad_raw, query_gain_part, key_gain_part = attend_backward(
        rank_ref, raw, cosines, sines, query_gain, key_gain, mix, lse, grad_gated,
        count, groups, kv_local,
    )
    steps = sum_steps()
    gain_sums = jnp.concatenate([query_gain_part, key_gain_part], axis=1)
    attn_grad = mm(first, grad_raw, TN).astype(BF16)
    attn_grad, grad_raw, gain_sums, out_blocks = sync(attn_grad, grad_raw, gain_sums, out_blocks)

    def first_rows(lo, hi):
        return mm(grad_raw[lo:hi], w_in, NT)

    corner = corner_rows(first_rows, rows)
    corner, grad_raw, attn_grad, gain_sums = sync(corner, grad_raw, attn_grad, gain_sums)
    corner = scatter_start(corner)
    gain_sums = sum_over(gain_sums, steps[:1])
    others = other_rows(first_rows, rows)
    first_part = first_rows(0, rows)
    out_grad = place_blocks(out_blocks, rank, 0)
    attn_grad, out_grad, others, first_part, corner, down_held, gain_sums = sync(
        attn_grad, out_grad, others, first_part, corner, down_held, gain_sums
    )
    came = scatter_turn(others, corner)
    gateup_share, attn_grad, out_grad = sync(gateup_share, attn_grad, out_grad)
    attn_share = scatter(attn_grad)
    out_share = scatter(out_grad)
    gateup_held = gather_start(gateup_share)
    gain_sums = sum_over(gain_sums, steps[1:2])
    came, gain_sums, gateup_held = sync(came, gain_sums, gateup_held)
    gateup_held = gather_turn(gateup_held)
    down_held = gather_turn(down_held)
    (input_grad,) = norm_back(tokens[0], grad_middle, first_part, came, first_gain, False)
    gateup_held, gain_sums, input_grad, attn_share, down_held = sync(
        gateup_held, gain_sums, input_grad, attn_share, down_held
    )
    attn_held = gather_start(attn_share)
    gain_sums = sum_over(gain_sums, steps[2:3])
    gateup_pieces = gather_pieces(gateup_held)
    gate_grad, gate_sums = weave_units(rank_ref, gateup_pieces, 0, gate_weight, shards)
    down_grad = stack_rows(rank_ref, gather_pieces(down_held))
    attn_held, out_share, gate_grad, gain_sums, down_grad = sync(
        attn_held, out_share, gate_grad, gain_sums, down_grad
    )
    attn_held = gather_turn(attn_held)
    out_held = gather_start(out_share)
    gain_sums = sum_over(gain_sums, steps[3:4])
    up_grad, up_sums = weave_units(rank_ref, gateup_pieces, 1, up_weight, shards)
    attn_held, out_held, gain_sums, up_grad = sync(attn_held, out_held, gain_sums, up_grad)
    out_held = gather_turn(out_held)
    gain_sums = sum_over(gain_sums, steps[4:])
    *attn_grads, in_sums = split_columns(
        rank_ref, gather_pieces(attn_held), (qcols, kcols, kcols, qcols),
        (q_weight, k_weight, v_weight, g_weight),
    )
    (out_grad,) = split_columns(rank_ref, gather_pieces(out_held), (dcols,))
    attn_gain_grad = in_sums[:, 0] / attn_gain.astype(F32)
    mlp_gain_grad = (gate_sums + up_sums)[:, 0] / mlp_gain.astype(F32)

    def own(values):
        size = values.shape[0] // shards
        return lax.dynamic_slice_in_dim(values, shard * size, size, 0)

    return (
        block_out[None],
        input_grad[None],
        *attn_grads,
        out_grad,
        gate_grad,
        up_grad,
        down_grad,
        attn_gain_grad,
        mlp_gain_grad,
        own(gain_sums[0, :HEAD]),
        own(gain_sums[0, HEAD:]),
    )


def solution(mesh):
    both, over_fsdp = P("fsdp", "sp", None), P("fsdp", None)
    return jax.shard_map(
        on_device,
        mesh=mesh,
        in_specs=(both, both, P("fsdp", "sp"), P("fsdp"), P("fsdp"), P("fsdp"), P())
        + (over_fsdp,) * 8
        + (P("fsdp"),) * 4,
        out_specs=(both, both) + (over_fsdp,) * 8 + (P("fsdp"),) * 4,
        check_vma=False,
    )
```

```python
import functools

import jax
import jax.numpy as jnp
from jax import lax
from jax.experimental import pallas as pl
from jax.experimental.pallas import tpu as pltpu
from jax.sharding import PartitionSpec as P

HEAD = 128
HALF = HEAD // 2
SEQ_LEN = 1024
EPS = 1e-06
ROPE_BASE = 1000000.0
SCALE = HEAD ** (-0.5)
LOG2E = 1.4426950408889634
VMEM_LIMIT = 56 * 1024 * 1024
NT = (((1,), (1,)), ((), ()))
NN = (((1,), (0,)), ((), ()))
TN = (((0,), (0,)), ((), ()))
F32 = jnp.float32
BF16 = jnp.bfloat16


def mm(left, right, dims=NN):
    return lax.dot_general(left, right, dims, preferred_element_type=F32)


def head_norm(raw):
    return lax.rsqrt(jnp.mean(raw * raw, axis=-1, keepdims=True) + EPS)


def turn(values, cosines, sines):
    return values * cosines + pltpu.roll(values, HALF, 1) * sines


def turn_back(values, cosines, sines):
    return values * cosines - pltpu.roll(values, HALF, 1) * sines


def norm_turn(raw, gain, cosines, sines):
    return turn(raw * head_norm(raw) * gain, cosines, sines).astype(BF16)


def norm_turn_back(raw, gain, grad, cosines, sines):
    back = turn_back(grad, cosines, sines)
    scale = head_norm(raw)
    pulled = back * gain
    inner = jnp.mean(raw * pulled, axis=-1, keepdims=True)
    gain_part = jnp.sum(raw * scale * back, axis=0, keepdims=True)
    return scale * pulled - raw * (scale * scale * scale * inner), gain_part


def diagonal_mask(rows, groups):
    keys = lax.broadcasted_iota(jnp.int32, (rows, groups * rows), 0)
    places = lax.broadcasted_iota(jnp.int32, (rows, groups * rows), 1)
    return keys <= lax.rem(places, rows)


def row_block(block, rank, rows):
    return pl.ds(pl.multiple_of(jnp.bitwise_xor(block, rank) * rows, rows), rows)


def attend_fwd_kernel(
    blocks, rows, groups,
    rank_ref, q_ref, k_ref, v_ref, g_ref, cos_ref, sin_ref, qg_ref, kg_ref,
    gated_ref, mix_ref, lse_ref, keys, vals_t,
):
    rank = rank_ref[0]
    factor = SCALE * LOG2E
    for a in range(blocks):
        place = row_block(a, rank, rows)
        here = slice(a * rows, (a + 1) * rows)
        keys[here, :] = norm_turn(k_ref[place, :], kg_ref[...], cos_ref[place, :], sin_ref[place, :])
        vals_t[:, here] = v_ref[place, :].T.astype(BF16)
    mask = diagonal_mask(rows, groups)
    for a in range(blocks):
        place = row_block(a, rank, rows)
        cosines, sines = cos_ref[place, :], sin_ref[place, :]
        queries = jnp.concatenate(
            [
                norm_turn(q_ref[place, h * HEAD : (h + 1) * HEAD], qg_ref[...], cosines, sines)
                for h in range(groups)
            ],
            axis=0,
        )
        low, high = a * rows, (a + 1) * rows
        near = jnp.where(mask, mm(keys[low:high, :], queries, NT), -1e30)
        peak = jnp.max(near, axis=0, keepdims=True)
        if a:
            far = mm(keys[:low, :], queries, NT)
            peak = jnp.maximum(peak, jnp.max(far, axis=0, keepdims=True))
        near = jnp.exp2((near - peak) * factor)
        total = jnp.sum(near, axis=0, keepdims=True)
        if a:
            far = jnp.exp2((far - peak) * factor)
            total = total + jnp.sum(far, axis=0, keepdims=True)
        inverse = 1.0 / total
        mix_t = mm(vals_t[:, low:high], (near * inverse).astype(BF16))
        if a:
            mix_t = mix_t + mm(vals_t[:, :low], (far * inverse).astype(BF16))
        mix = mix_t.T
        for h in range(groups):
            cols = slice(h * HEAD, (h + 1) * HEAD)
            part = mix[h * rows : (h + 1) * rows, :]
            opening = jax.nn.sigmoid(g_ref[place, cols].astype(BF16).astype(F32))
            mix_ref[place, cols] = part
            gated_ref[place, cols] = (part * opening).astype(BF16)
        lse_ref[0, a : a + 1, :] = peak * factor + jnp.log2(total)


def attend_bwd_kernel(
    blocks, rows, groups, kv_local,
    rank_ref, q_ref, k_ref, v_ref, g_ref, cos_ref, sin_ref, qg_ref, kg_ref, mix_ref, lse_ref, up_ref,
    grad_ref, qgain_ref, kgain_ref, keys, keys_t, vals, dkeys, dvals,
):
    rank = rank_ref[0]
    step = pl.program_id(0)
    factor = SCALE * LOG2E
    width = groups * HEAD

    @pl.when(step == 0)
    def _():
        qgain_ref[...] = jnp.zeros_like(qgain_ref)
        kgain_ref[...] = jnp.zeros_like(kgain_ref)

    for a in range(blocks):
        place = row_block(a, rank, rows)
        here = slice(a * rows, (a + 1) * rows)
        block = norm_turn(k_ref[place, :], kg_ref[...], cos_ref[place, :], sin_ref[place, :])
        keys[here, :] = block
        keys_t[:, here] = block.astype(F32).T.astype(BF16)
        vals[here, :] = v_ref[place, :].astype(BF16)
    mask = diagonal_mask(rows, groups)
    qgain = jnp.zeros((1, HEAD), F32)
    for a in reversed(range(blocks)):
        place = row_block(a, rank, rows)
        cosines, sines = cos_ref[place, :], sin_ref[place, :]
        queries, grads = [], []
        for h in range(groups):
            cols = slice(h * HEAD, (h + 1) * HEAD)
            queries.append(norm_turn(q_ref[place, cols], qg_ref[...], cosines, sines))
            upstream = up_ref[place, cols].astype(F32)
            opening = jax.nn.sigmoid(g_ref[place, cols].astype(BF16).astype(F32))
            opened = upstream * opening
            grads.append(opened.astype(BF16))
            grad_ref[
                place, pl.ds((kv_local * (groups + 2)) * HEAD + step * width + h * HEAD, HEAD)
            ] = (opened * mix_ref[place, cols] * (1.0 - opening)).astype(BF16)
        queries = jnp.concatenate(queries, axis=0)
        grads = jnp.concatenate(grads, axis=0)
        lse = lse_ref[0, a : a + 1, :]
        low, high = a * rows, (a + 1) * rows
        spans = [(low, high)] + ([(0, low)] if a else [])
        chances, grad_chances = [], []
        centre = jnp.zeros((1, groups * rows), F32)
        for start, stop in spans:
            part = jnp.exp2(mm(keys[start:stop, :], queries, NT) * factor - lse)
            if start == low:
                part = jnp.where(mask, part, 0.0)
            pull = mm(vals[start:stop, :], grads, NT)
            centre = centre + jnp.sum(part * pull, axis=0, keepdims=True)
            chances.append(part)
            grad_chances.append(pull)
        dq_t = jnp.zeros((HEAD, groups * rows), F32)
        for (start, stop), part, pull in zip(spans, chances, grad_chances):
            grad_products = (part * (pull - centre) * SCALE).astype(BF16)
            dval = mm(part.astype(BF16), grads)
            dkey = mm(grad_products, queries)
            if a == blocks - 1:
                dvals[start:stop, :] = dval
                dkeys[start:stop, :] = dkey
            else:
                dvals[start:stop, :] += dval
                dkeys[start:stop, :] += dkey
            dq_t = dq_t + mm(keys_t[:, start:stop], grad_products)
        dq = dq_t.T
        for h in range(groups):
            grad = dq[h * rows : (h + 1) * rows, :].astype(BF16).astype(F32)
            cols = slice(h * HEAD, (h + 1) * HEAD)
            raw, gain_part = norm_turn_back(q_ref[place, cols], qg_ref[...], grad, cosines, sines)
            grad_ref[place, pl.ds(step * width + h * HEAD, HEAD)] = raw.astype(BF16)
            qgain = qgain + gain_part
    kgain = jnp.zeros((1, HEAD), F32)
    for a in range(blocks):
        place = row_block(a, rank, rows)
        here = slice(a * rows, (a + 1) * rows)
        grad = dkeys[here, :].astype(BF16).astype(F32)
        raw, gain_part = norm_turn_back(
            k_ref[place, :], kg_ref[...], grad, cos_ref[place, :], sin_ref[place, :]
        )
        kgain = kgain + gain_part
        grad_ref[place, pl.ds(kv_local * width + step * HEAD, HEAD)] = raw.astype(BF16)
        grad_ref[place, pl.ds(kv_local * (width + HEAD) + step * HEAD, HEAD)] = dvals[
            here, :
        ].astype(BF16)
    qgain_ref[...] += qgain
    kgain_ref[...] += kgain


def attention_specs(length, groups, kv_local):
    width = groups * HEAD
    return [
        pl.BlockSpec((length, width), lambda g, r: (0, g)),
        pl.BlockSpec((length, HEAD), lambda g, r: (0, kv_local * groups + g)),
        pl.BlockSpec((length, HEAD), lambda g, r: (0, kv_local * (groups + 1) + g)),
        pl.BlockSpec((length, width), lambda g, r: (0, kv_local * (groups + 2) // groups + g)),
        pl.BlockSpec((length, HEAD), lambda g, r: (0, 0)),
        pl.BlockSpec((length, HEAD), lambda g, r: (0, 0)),
        pl.BlockSpec((1, HEAD), lambda g, r: (0, 0)),
        pl.BlockSpec((1, HEAD), lambda g, r: (0, 0)),
    ]


def attend_forward(rank, raw, cosines, sines, q_gain, k_gain, blocks, groups, kv_local):
    length = raw.shape[0]
    rows = length // blocks
    width = groups * HEAD
    flops = 4 * kv_local * groups * length * length * HEAD * (blocks + 1) // (2 * blocks)
    return pl.pallas_call(
        functools.partial(attend_fwd_kernel, blocks, rows, groups),
        grid_spec=pltpu.PrefetchScalarGridSpec(
            num_scalar_prefetch=1,
            grid=(kv_local,),
            in_specs=attention_specs(length, groups, kv_local),
            out_specs=[
                pl.BlockSpec((length, width), lambda g, r: (0, g)),
                pl.BlockSpec((length, width), lambda g, r: (0, g)),
                pl.BlockSpec((1, blocks, groups * rows), lambda g, r: (g, 0, 0)),
            ],
            scratch_shapes=[pltpu.VMEM((length, HEAD), BF16), pltpu.VMEM((HEAD, length), BF16)],
        ),
        out_shape=[
            jax.ShapeDtypeStruct((length, kv_local * width), BF16),
            jax.ShapeDtypeStruct((length, kv_local * width), F32),
            jax.ShapeDtypeStruct((kv_local, blocks, groups * rows), F32),
        ],
        compiler_params=pltpu.CompilerParams(
            dimension_semantics=("arbitrary",), vmem_limit_bytes=VMEM_LIMIT
        ),
        cost_estimate=pl.CostEstimate(
            flops=4 * flops,
            bytes_accessed=raw.size * 4 + length * kv_local * width * 6,
            transcendentals=kv_local * groups * length * length // 2,
        ),
        name="attend_forward",
    )(rank, raw, raw, raw, raw, cosines, sines, q_gain, k_gain)


def attend_backward(
    rank, raw, cosines, sines, q_gain, k_gain, mix, lse, upstream, blocks, groups, kv_local
):
    length = raw.shape[0]
    rows = length // blocks
    width = groups * HEAD
    flops = 10 * kv_local * groups * length * length * HEAD * (blocks + 1) // (2 * blocks)
    return pl.pallas_call(
        functools.partial(attend_bwd_kernel, blocks, rows, groups, kv_local),
        grid_spec=pltpu.PrefetchScalarGridSpec(
            num_scalar_prefetch=1,
            grid=(kv_local,),
            in_specs=attention_specs(length, groups, kv_local)
            + [
                pl.BlockSpec((length, width), lambda g, r: (0, g)),
                pl.BlockSpec((1, blocks, groups * rows), lambda g, r: (g, 0, 0)),
                pl.BlockSpec((length, width), lambda g, r: (0, g)),
            ],
            out_specs=[
                pl.BlockSpec(raw.shape, lambda g, r: (0, 0)),
                pl.BlockSpec((1, HEAD), lambda g, r: (0, 0)),
                pl.BlockSpec((1, HEAD), lambda g, r: (0, 0)),
            ],
            scratch_shapes=[
                pltpu.VMEM((length, HEAD), BF16),
                pltpu.VMEM((HEAD, length), BF16),
                pltpu.VMEM((length, HEAD), BF16),
                pltpu.VMEM((length, HEAD), F32),
                pltpu.VMEM((length, HEAD), F32),
            ],
        ),
        out_shape=[
            jax.ShapeDtypeStruct(raw.shape, BF16),
            jax.ShapeDtypeStruct((1, HEAD), F32),
            jax.ShapeDtypeStruct((1, HEAD), F32),
        ],
        compiler_params=pltpu.CompilerParams(
            dimension_semantics=("arbitrary",), vmem_limit_bytes=VMEM_LIMIT
        ),
        cost_estimate=pl.CostEstimate(
            flops=4 * flops,
            bytes_accessed=raw.size * 6 + length * kv_local * width * 6,
            transcendentals=kv_local * groups * length * length // 2,
        ),
        name="attend_backward",
    )(rank, raw, raw, raw, raw, cosines, sines, q_gain, k_gain, mix, lse, upstream)


def middle_kernel(tokens_ref, own_ref, x_ref, y_ref, gain_ref, middle_ref, second_ref):
    middle = tokens_ref[...].astype(F32) + own_ref[...]
    middle = middle + x_ref[...].astype(F32) + y_ref[...].astype(F32)
    scale = lax.rsqrt(jnp.mean(middle * middle, axis=-1, keepdims=True) + EPS)
    middle_ref[...] = middle
    second_ref[...] = (middle * scale * gain_ref[...]).astype(BF16)


def norm_back_kernel(low, values_ref, base_ref, own_ref, x_ref, y_ref, gain_ref, grad_ref, *low_ref):
    values = values_ref[...].astype(F32)
    grad = own_ref[...] + x_ref[...].astype(F32) + y_ref[...].astype(F32)
    scale = lax.rsqrt(jnp.mean(values * values, axis=-1, keepdims=True) + EPS)
    normed = values * scale
    pulled = grad * gain_ref[...]
    inner = jnp.mean(normed * pulled, axis=-1, keepdims=True)
    total = base_ref[...] + scale * (pulled - normed * inner)
    grad_ref[...] = total
    if low:
        low_ref[0][...] = total.astype(BF16)


def row_call(kernel, name, arrays, gain, outs):
    rows, width = arrays[0].shape
    tile = rows // 2

    def spec(shape):
        if shape[0] == rows:
            return pl.BlockSpec((tile, width), lambda i: (i, 0))
        return pl.BlockSpec((1, width), lambda i: (0, 0))

    return pl.pallas_call(
        kernel,
        grid=(2,),
        in_specs=[spec(a.shape) for a in arrays] + [spec(gain.shape)],
        out_specs=[spec(o.shape) for o in outs],
        out_shape=outs,
        compiler_params=pltpu.CompilerParams(
            dimension_semantics=("arbitrary",), vmem_limit_bytes=VMEM_LIMIT
        ),
        cost_estimate=pl.CostEstimate(
            flops=16 * rows * width, bytes_accessed=18 * rows * width, transcendentals=rows
        ),
        name=name,
    )(*arrays, gain)


def two_addends(came):
    if len(came) == 2:
        return came
    return [sum(part.astype(F32) for part in came[:-1]), came[-1]]


def middle_and_second(tokens, own, came, gain):
    return row_call(
        middle_kernel, "middle_and_second", [tokens, own, *two_addends(came)], gain[None],
        [jax.ShapeDtypeStruct(own.shape, F32), jax.ShapeDtypeStruct(own.shape, BF16)],
    )


def norm_back(values, base, own, came, gain, low):
    outs = [jax.ShapeDtypeStruct(own.shape, F32)] + [jax.ShapeDtypeStruct(own.shape, BF16)] * low
    return row_call(
        functools.partial(norm_back_kernel, low), "norm_back",
        [values, base, own, *two_addends(came)], gain[None], outs,
    )


def flat_specs(pieces, spec):
    return [spec(piece) for block in pieces for piece in block]


def grouped(refs, counts):
    blocks, start = [], 0
    for count in counts:
        blocks.append(refs[start : start + count])
        start += count
    return blocks, refs[start:]


def split_columns_kernel(counts, sizes, weighed, rank_ref, *refs):
    sources, refs = grouped(refs, counts)
    weights, outs, sums = refs[:weighed], refs[weighed : weighed + len(sizes)], refs[-1]
    block = jnp.bitwise_xor(pl.program_id(0), rank_ref[0])
    for j, pieces in enumerate(sources):

        @pl.when(block == j)
        def _(pieces=pieces):
            top = 0
            for piece in pieces:
                start, stop = 0, top + piece.shape[0]
                for size, out in zip(sizes, outs):
                    out[top:stop, :] = piece[:, start : start + size].astype(F32)
                    start += size
                top = stop

    if weighed:
        part = sum(
            jnp.sum(out[...] * weight[...].astype(F32), axis=1, keepdims=True)
            for out, weight in zip(outs, weights)
        )

        @pl.when(pl.program_id(0) == 0)
        def _():
            sums[...] = jnp.zeros_like(sums)

        sums[...] += part


def split_columns(rank, pieces, sizes, weights=()):
    count, rows = len(pieces), pieces[0][0].shape[0]
    group_specs = [pl.BlockSpec((rows, size), lambda a, r: (0, a)) for size in sizes]
    sum_specs = [pl.BlockSpec((rows, 1), lambda a, r: (0, 0))] if weights else []
    return pl.pallas_call(
        functools.partial(
            split_columns_kernel, [len(block) for block in pieces], sizes, len(weights)
        ),
        grid_spec=pltpu.PrefetchScalarGridSpec(
            num_scalar_prefetch=1,
            grid=(count,),
            in_specs=flat_specs(pieces, lambda p: pl.BlockSpec(p.shape, lambda a, r: (0, 0)))
            + group_specs[: len(weights)],
            out_specs=group_specs + sum_specs,
        ),
        out_shape=[jax.ShapeDtypeStruct((rows, count * size), F32) for size in sizes]
        + [jax.ShapeDtypeStruct((rows, 1), F32)] * len(sum_specs),
        compiler_params=pltpu.CompilerParams(
            dimension_semantics=("arbitrary",), vmem_limit_bytes=VMEM_LIMIT
        ),
        cost_estimate=pl.CostEstimate(
            flops=0, bytes_accessed=6 * rows * count * sum(sizes), transcendentals=0
        ),
        name="split_columns",
    )(rank, *sum(pieces, []), *weights)


def stack_rows_kernel(counts, rank_ref, *refs):
    sources, (out,) = grouped(refs, counts)
    block = jnp.bitwise_xor(pl.program_id(0), rank_ref[0])
    for j, pieces in enumerate(sources):

        @pl.when(block == j)
        def _(pieces=pieces):
            top = 0
            for piece in pieces:
                out[top : top + piece.shape[0], :] = piece[...].astype(F32)
                top += piece.shape[0]


def stack_rows(rank, pieces):
    count, (rows, width) = len(pieces), pieces[0][0].shape
    return pl.pallas_call(
        functools.partial(stack_rows_kernel, [len(block) for block in pieces]),
        grid_spec=pltpu.PrefetchScalarGridSpec(
            num_scalar_prefetch=1,
            grid=(count,),
            in_specs=flat_specs(pieces, lambda p: pl.BlockSpec(p.shape, lambda a, r: (0, 0))),
            out_specs=pl.BlockSpec((rows, width), lambda a, r: (a, 0)),
        ),
        out_shape=jax.ShapeDtypeStruct((count * rows, width), F32),
        compiler_params=pltpu.CompilerParams(
            dimension_semantics=("arbitrary",), vmem_limit_bytes=VMEM_LIMIT
        ),
        cost_estimate=pl.CostEstimate(
            flops=0, bytes_accessed=6 * rows * count * width, transcendentals=0
        ),
        name="stack_rows",
    )(rank, *sum(pieces, []))


def weave_units_kernel(counts, steps, shards, units, rank_ref, *refs):
    sources, (weight, out, sums, held) = grouped(refs, counts)
    step = pl.program_id(0)
    for j, pieces in enumerate(sources):
        place = jnp.bitwise_xor(rank_ref[0], j)
        if len(pieces) == 1:
            held[place] = pieces[0][...].astype(F32)
            continue
        share = steps // len(pieces)
        for k, piece in enumerate(pieces):

            @pl.when((step >= k * share) & (step < (k + 1) * share))
            def _(piece=piece, place=place):
                held[place] = piece[...].astype(F32)

    count = len(counts)
    for a in range(count):
        for f in range(shards):
            start = (f * count + a) * units
            out[:, start : start + units] = held[a, :, f * units : (f + 1) * units]
    sums[...] = jnp.sum(out[...] * weight[...].astype(F32), axis=1, keepdims=True)


def weave_units(rank, pieces, group, weight, shards):
    count, (rows, width) = len(pieces), pieces[0][0].shape
    ffs, steps = width // 2, 2
    tile = rows // steps

    def spec(block, k):
        share = steps // len(block)

        def place(i, r):
            return (jnp.clip(i - k * share, 0, share - 1), group)

        return pl.BlockSpec((tile, ffs), place)

    return pl.pallas_call(
        functools.partial(
            weave_units_kernel, [len(block) for block in pieces], steps, shards, ffs // shards
        ),
        grid_spec=pltpu.PrefetchScalarGridSpec(
            num_scalar_prefetch=1,
            grid=(steps,),
            in_specs=[spec(block, k) for block in pieces for k in range(len(block))]
            + [pl.BlockSpec((tile, count * ffs), lambda i, r: (i, 0))],
            out_specs=[
                pl.BlockSpec((tile, count * ffs), lambda i, r: (i, 0)),
                pl.BlockSpec((tile, 1), lambda i, r: (i, 0)),
            ],
            scratch_shapes=[pltpu.VMEM((count, tile, ffs), F32)],
        ),
        out_shape=[
            jax.ShapeDtypeStruct((rows, count * ffs), F32), jax.ShapeDtypeStruct((rows, 1), F32),
        ],
        compiler_params=pltpu.CompilerParams(
            dimension_semantics=("arbitrary",), vmem_limit_bytes=VMEM_LIMIT
        ),
        cost_estimate=pl.CostEstimate(
            flops=0, bytes_accessed=8 * rows * count * ffs, transcendentals=0
        ),
        name="weave_units",
    )(rank, *sum(pieces, []), weight)


def column_shares_kernel(rank_ref, *refs):
    start = 0
    for ref in refs[:-1]:
        refs[-1][:, start : start + ref.shape[1]] = ref[...]
        start += ref.shape[1]


def column_shares(rank, weights, sizes):
    rows, width = weights[0].shape[0], sum(sizes)
    tile = rows // 2
    return pl.pallas_call(
        column_shares_kernel,
        grid_spec=pltpu.PrefetchScalarGridSpec(
            num_scalar_prefetch=1,
            grid=(2,),
            in_specs=[pl.BlockSpec((tile, size), lambda i, r: (i, r[0])) for size in sizes],
            out_specs=pl.BlockSpec((tile, width), lambda i, r: (i, 0)),
        ),
        out_shape=jax.ShapeDtypeStruct((rows, width), weights[0].dtype),
        compiler_params=pltpu.CompilerParams(
            dimension_semantics=("arbitrary",), vmem_limit_bytes=VMEM_LIMIT
        ),
        cost_estimate=pl.CostEstimate(
            flops=0, bytes_accessed=4 * rows * width, transcendentals=0
        ),
        name="column_shares",
    )(rank, *weights)


def swap(values, bit, axis="sp"):
    return lax.ppermute(values, axis, [(i, i ^ bit) for i in range(lax.axis_size(axis))])


def sync(*values):
    return lax.optimization_barrier(values)


def gather_start(block):
    return [block] + [swap(block, j) for j in range(1, lax.axis_size("sp"))][: 2 if lax.axis_size("sp") == 4 else None]


def gather_turn(held):
    if lax.axis_size("sp") != 4:
        return held
    half = held[0].shape[0] // 2
    return held + [swap(held[2][:half], 1), swap(held[1][half:], 2)]


def gather_end(held):
    if lax.axis_size("sp") != 4:
        return held
    return held[:3] + [jnp.concatenate(held[3:], axis=0)]


def gather_blocks(block):
    return gather_end(gather_turn(gather_start(block)))


def gather_pieces(held):
    if lax.axis_size("sp") != 4:
        return [[block] for block in held]
    return [[block] for block in held[:3]] + [held[3:]]


def scatter_start(corner):
    if lax.axis_size("sp") != 4:
        return []
    half = corner.shape[0] // 2
    return [swap(corner[:half], 1), swap(corner[half:], 2)]


def scatter_turn(others, came):
    if lax.axis_size("sp") != 4:
        return [swap(part.astype(BF16), j + 1) for j, part in enumerate(others)]
    to_x, to_y = add_corner(others, came)
    return [swap(to_x, 1), swap(to_y, 2)]


def add_corner_kernel(whole_ref, from_x_ref, from_y_ref, to_x_ref, to_y_ref):
    half = from_x_ref.shape[0]

    @pl.when(pl.program_id(0) == 0)
    def _():
        to_x_ref[:half, :] = whole_ref[:half, :].astype(BF16)
        to_x_ref[half:, :] = (whole_ref[half:, :] + from_y_ref[...].astype(F32)).astype(BF16)

    @pl.when(pl.program_id(0) == 1)
    def _():
        to_y_ref[:half, :] = (whole_ref[:half, :] + from_x_ref[...].astype(F32)).astype(BF16)
        to_y_ref[half:, :] = whole_ref[half:, :].astype(BF16)


def add_corner(whole, came):
    rows, width = whole.shape[0] // 2, whole.shape[1]
    half = pl.BlockSpec((rows // 2, width), lambda i: (0, 0))
    out = pl.BlockSpec((rows, width), lambda i: (0, 0))
    return pl.pallas_call(
        add_corner_kernel,
        grid=(2,),
        in_specs=[pl.BlockSpec((rows, width), lambda i: (i, 0)), half, half],
        out_specs=[out, out],
        out_shape=[jax.ShapeDtypeStruct((rows, width), BF16)] * 2,
        compiler_params=pltpu.CompilerParams(
            dimension_semantics=("arbitrary",), vmem_limit_bytes=32 * 1024 * 1024
        ),
        cost_estimate=pl.CostEstimate(
            flops=rows * width, bytes_accessed=14 * rows * width, transcendentals=0
        ),
        name="add_corner",
    )(whole, *came)


def scatter_end(own, came):
    for part in came:
        own = own + part.astype(F32)
    return own


def corner_rows(make, rows):
    count = lax.axis_size("sp")
    return make((count - 1) * rows, count * rows).astype(BF16) if count == 4 else None


def other_rows(make, rows):
    count = lax.axis_size("sp")
    stop = 3 if count == 4 else count
    whole = make(rows, stop * rows)
    if count == 4:
        return whole
    return [whole[j * rows : (j + 1) * rows] for j in range(stop - 1)]


def place_blocks(blocks, rank, axis):
    size = blocks[0].shape[axis]
    shape = list(blocks[0].shape)
    shape[axis] = size * len(blocks)
    whole = jnp.zeros(shape, blocks[0].dtype)
    for j, block in enumerate(blocks):
        whole = lax.dynamic_update_slice_in_dim(
            whole, block, jnp.bitwise_xor(rank, j) * size, axis
        )
    return whole


def halve_start(held, bit):
    shard = lax.axis_index("fsdp")
    mine = jnp.bitwise_and(lax.div(shard, jnp.int32(bit)), 1)
    pairs = held.reshape(held.shape[0] // 2, 2, held.shape[1], held.shape[2])
    sent = lax.dynamic_index_in_dim(pairs, 1 - mine, 1, False)
    kept = lax.dynamic_index_in_dim(pairs, mine, 1, False)
    return kept, swap(sent, bit, "fsdp")


def halve_end(state):
    return (state[0].astype(F32) + state[1].astype(F32)).astype(BF16)


def halve_open(grad):
    shards = lax.axis_size("fsdp")
    return halve_start(grad.reshape(shards, grad.shape[0] // shards, grad.shape[1]), 1)


def halve_next(state, bit):
    return halve_start(halve_end(state), bit)


def halve_close(state):
    held = halve_end(state)
    while held.shape[0] > 1:
        held = halve_end(halve_start(held, lax.axis_size("fsdp") // held.shape[0]))
    return held[0]


def double_over(values, axis):
    bit = 1
    while bit < lax.axis_size(axis):
        values = jnp.concatenate([values, swap(values, bit, axis)], axis=0)
        bit *= 2
    return values


def sum_steps():
    return [
        (axis, 1 << k)
        for axis in ("sp", "fsdp")
        for k in range((lax.axis_size(axis) - 1).bit_length())
    ]


def sum_over(values, steps):
    for axis, bit in steps:
        values = values + swap(values, bit, axis)
    return values


def rms_low(values, gain):
    scale = lax.rsqrt(jnp.mean(values * values, axis=-1, keepdims=True) + EPS)
    return (values * scale * gain).astype(BF16)


def on_device(
    tokens, cotangent, positions, domain_ids, counts, loss_weight, domain_weights,
    q_weight, k_weight, v_weight, g_weight, o_weight, gate_weight, up_weight, down_weight,
    attn_gain, mlp_gain, q_gain, k_gain,
):
    count, shards = lax.axis_size("sp"), lax.axis_size("fsdp")
    rank, shard = lax.axis_index("sp"), lax.axis_index("fsdp")
    rank_ref = rank.astype(jnp.int32).reshape(1)
    _, rows, width = tokens.shape
    heads_local = q_weight.shape[1] // HEAD // count
    kv_local = k_weight.shape[1] // HEAD // count
    groups = heads_local // kv_local
    qcols, kcols = heads_local * HEAD, kv_local * HEAD
    dcols = width // count
    units = down_weight.shape[0] // count
    ffs = units * shards

    def gather(weight):
        return lax.all_gather(weight, "fsdp", axis=0, tiled=True)

    def unit_columns(weight):
        spread = weight.reshape(weight.shape[0], shards, count, units)
        return lax.dynamic_slice_in_dim(spread, rank, 1, 2).reshape(weight.shape[0], ffs)

    def scatter(grad):
        return lax.psum_scatter(grad, "fsdp", scatter_dimension=0, tiled=True)

    tokens_held = gather_start(tokens[0])
    places = double_over(positions[0][None], "sp").reshape(-1)
    gains = double_over(jnp.concatenate([attn_gain, mlp_gain, q_gain, k_gain])[None], "fsdp")
    attn_full = gather(
        column_shares(
            rank_ref, (q_weight, k_weight, v_weight, g_weight, o_weight),
            (qcols, kcols, kcols, qcols, dcols),
        )
    )
    in_cols = 2 * (qcols + kcols)
    onehot = (domain_ids[:, None] == jnp.arange(domain_weights.shape[0], dtype=jnp.int32)).astype(F32)
    seq_scale = loss_weight * jnp.sum(onehot * domain_weights[None, :], axis=1) * SEQ_LEN
    seq_scale = (seq_scale / counts.astype(F32))[0]
    upstream = cotangent[0].astype(F32) * seq_scale
    tokens_held, places, gains = sync(tokens_held, places, gains)
    tokens_held = gather_turn(tokens_held)
    gateup_share = jnp.concatenate([unit_columns(gate_weight), unit_columns(up_weight)], axis=1)
    tokens_held, upstream_low, gateup_share = sync(
        tokens_held, upstream.astype(BF16), gateup_share
    )
    gateup = gather(gateup_share)
    w_gate, w_up = gateup[:, :ffs], gateup[:, ffs:]
    upstream_held = gather_start(upstream_low)
    tokens_all = jnp.concatenate(gather_end(tokens_held), axis=0)

    order = jnp.bitwise_xor(jnp.arange(shards, dtype=jnp.int32), shard.astype(jnp.int32))
    gains = jnp.take(gains, order, axis=0).astype(F32)
    part = attn_gain.shape[0]
    first_gain = gains[:, :part].reshape(-1)
    second_gain = gains[:, part : 2 * part].reshape(-1)
    piece = q_gain.shape[0]
    query_gain = gains[:, 2 * part : 2 * part + piece].reshape(1, HEAD)
    key_gain = gains[:, 2 * part + piece :].reshape(1, HEAD)
    inverse = ROPE_BASE ** (-(2.0 * jnp.arange(HALF, dtype=F32)) / HEAD)
    angles = places.astype(F32)[:, None] * inverse
    cosines, sines = jnp.cos(angles), jnp.sin(angles)
    cosines = jnp.concatenate([cosines, cosines], axis=1)
    sines = jnp.concatenate([-sines, sines], axis=1)
    first = rms_low(tokens_all.astype(F32), first_gain)

    upstream_held, first, cosines, sines = sync(upstream_held, first, cosines, sines)
    upstream_held = gather_turn(upstream_held)
    first, upstream_held = sync(first, upstream_held)
    upstream_all = jnp.concatenate(gather_end(upstream_held), axis=0)
    first, upstream_all = sync(first, upstream_all)

    w_in = attn_full[:, :in_cols]
    o_slices = attn_full[:, in_cols:].reshape(count, qcols, dcols)
    o_blocks = [
        lax.dynamic_index_in_dim(o_slices, jnp.bitwise_xor(rank, j), 0, False) for j in range(count)
    ]
    first, o_blocks = sync(first, o_blocks)
    o_blocks = [swap(block, j) if j else block for j, block in enumerate(o_blocks)]
    raw = mm(first, w_in)
    raw, o_blocks = sync(raw, o_blocks)
    w_out = place_blocks(o_blocks, rank, 1)
    gated, mix, lse = attend_forward(
        rank_ref, raw, cosines, sines, query_gain, key_gain, count, groups, kv_local
    )
    down_share = lax.dynamic_slice_in_dim(down_weight, rank * units, units, 0)
    down_share, gated = sync(down_share, gated)
    w_down = gather(down_share)

    def out_rows(lo, hi):
        return mm(gated[lo:hi], w_out)

    corner = scatter_start(corner_rows(out_rows, rows))
    others = other_rows(out_rows, rows)
    own_part = out_rows(0, rows)
    middle, second = middle_and_second(
        tokens[0], own_part, scatter_turn(others, corner), second_gain
    )
    second = jnp.concatenate(gather_blocks(second), axis=0)

    gate_act = mm(second, w_gate)
    up_act = mm(second, w_up)
    opening = jax.nn.sigmoid(gate_act)
    silu = gate_act * opening
    hidden = (silu * up_act).astype(BF16)
    down_grad, hidden, upstream_now = sync(
        mm(hidden, upstream_all, TN).astype(BF16), hidden, upstream_all
    )
    down_share = scatter(down_grad)

    def down_rows(lo, hi):
        return mm(hidden[lo:hi], w_down)

    block_corner = corner_rows(down_rows, rows)
    block_others = other_rows(down_rows, rows)
    block_part = down_rows(0, rows)
    block_corner, block_others, block_part, upstream_now = sync(
        block_corner, block_others, block_part, upstream_now
    )
    block_corner = scatter_start(block_corner)
    grad_hidden = mm(upstream_now, w_down, NT)
    grad_gate = (grad_hidden * up_act * opening * (1.0 + gate_act * (1.0 - opening))).astype(BF16)
    grad_up = (grad_hidden * silu).astype(BF16)
    grad_gate, grad_up, block_corner = sync(grad_gate, grad_up, block_corner)
    block_came = scatter_turn(block_others, block_corner)
    gateup_grad = mm(second, jnp.concatenate([grad_gate, grad_up], axis=1), TN).astype(BF16)
    gateup_grad, grad_gate, grad_up, block_came = sync(gateup_grad, grad_gate, grad_up, block_came)
    gateup_share = scatter(gateup_grad)

    def second_rows(lo, hi):
        return mm(grad_gate[lo:hi], w_gate, NT) + mm(grad_up[lo:hi], w_up, NT)

    corner = scatter_start(corner_rows(second_rows, rows))
    others = other_rows(second_rows, rows)
    own_part = second_rows(0, rows)
    own_part, corner, others = sync(own_part, corner, others)
    came = scatter_turn(others, corner)
    block_out = (middle + scatter_end(block_part, block_came)).astype(BF16)
    came, block_out = sync(came, block_out)
    grad_middle, grad_attn = norm_back(middle, upstream, own_part, came, second_gain, True)
    grad_attn = gather_start(grad_attn)
    grad_attn = jnp.concatenate(gather_end(gather_turn(grad_attn)), axis=0)

    grad_gated = mm(grad_attn, w_out, NT).astype(BF16)
    out_grad = mm(gated, grad_attn, TN).astype(BF16)
    out_blocks = [
        lax.dynamic_slice_in_dim(out_grad, jnp.bitwise_xor(rank, j) * dcols, dcols, 1)
        for j in range(count)
    ]
    grad_gated, out_blocks, down_share = sync(grad_gated, out_blocks, down_share)
    out_blocks = [swap(block, j) if j else block for j, block in enumerate(out_blocks)]
    down_held = gather_start(down_share)
    grad_raw, query_gain_part, key_gain_part = attend_backward(
        rank_ref, raw, cosines, sines, query_gain, key_gain, mix, lse, grad_gated,
        count, groups, kv_local,
    )
    steps = sum_steps()
    gain_sums = jnp.concatenate([query_gain_part, key_gain_part], axis=1)
    attn_grad = mm(first, grad_raw, TN).astype(BF16)
    attn_grad, grad_raw, gain_sums = sync(attn_grad, grad_raw, gain_sums)

    def first_rows(lo, hi):
        return mm(grad_raw[lo:hi], w_in, NT)

    corner = corner_rows(first_rows, rows)
    corner, grad_raw, attn_grad, gain_sums, out_blocks = sync(
        corner, grad_raw, attn_grad, gain_sums, out_blocks
    )
    corner = scatter_start(corner)
    gain_sums = sum_over(gain_sums, steps[:1])
    others = other_rows(first_rows, rows)
    first_part = first_rows(0, rows)
    out_grad = place_blocks(out_blocks, rank, 0)
    attn_grad, out_grad, others, first_part, corner, down_held, gain_sums = sync(
        attn_grad, out_grad, others, first_part, corner, down_held, gain_sums
    )
    came = scatter_turn(others, corner)
    gateup_share, attn_grad, out_grad = sync(gateup_share, attn_grad, out_grad)
    attn_share = scatter(attn_grad)
    out_share = scatter(out_grad)
    gateup_held = gather_start(gateup_share)
    gain_sums = sum_over(gain_sums, steps[1:2])
    came, gain_sums, gateup_held = sync(came, gain_sums, gateup_held)
    gateup_held = gather_turn(gateup_held)
    down_held = gather_turn(down_held)
    (input_grad,) = norm_back(tokens[0], grad_middle, first_part, came, first_gain, False)
    gateup_held, gain_sums, input_grad, attn_share, down_held = sync(
        gateup_held, gain_sums, input_grad, attn_share, down_held
    )
    attn_held = gather_start(attn_share)
    gain_sums = sum_over(gain_sums, steps[2:3])
    gateup_pieces = gather_pieces(gateup_held)
    gate_grad, gate_sums = weave_units(rank_ref, gateup_pieces, 0, gate_weight, shards)
    down_grad = stack_rows(rank_ref, gather_pieces(down_held))
    attn_held, out_share, gate_grad, gain_sums, down_grad = sync(
        attn_held, out_share, gate_grad, gain_sums, down_grad
    )
    attn_held = gather_turn(attn_held)
    out_held = gather_start(out_share)
    gain_sums = sum_over(gain_sums, steps[3:4])
    up_grad, up_sums = weave_units(rank_ref, gateup_pieces, 1, up_weight, shards)
    attn_held, out_held, gain_sums, up_grad = sync(attn_held, out_held, gain_sums, up_grad)
    out_held = gather_turn(out_held)
    gain_sums = sum_over(gain_sums, steps[4:])
    *attn_grads, in_sums = split_columns(
        rank_ref, gather_pieces(attn_held), (qcols, kcols, kcols, qcols),
        (q_weight, k_weight, v_weight, g_weight),
    )
    (out_grad,) = split_columns(rank_ref, gather_pieces(out_held), (dcols,))
    attn_gain_grad = in_sums[:, 0] / attn_gain.astype(F32)
    mlp_gain_grad = (gate_sums + up_sums)[:, 0] / mlp_gain.astype(F32)

    def own(values):
        size = values.shape[0] // shards
        return lax.dynamic_slice_in_dim(values, shard * size, size, 0)

    return (
        block_out[None],
        input_grad[None],
        *attn_grads,
        out_grad,
        gate_grad,
        up_grad,
        down_grad,
        attn_gain_grad,
        mlp_gain_grad,
        own(gain_sums[0, :HEAD]),
        own(gain_sums[0, HEAD:]),
    )


def solution(mesh):
    both, over_fsdp = P("fsdp", "sp", None), P("fsdp", None)
    return jax.shard_map(
        on_device,
        mesh=mesh,
        in_specs=(both, both, P("fsdp", "sp"), P("fsdp"), P("fsdp"), P("fsdp"), P())
        + (over_fsdp,) * 8
        + (P("fsdp"),) * 4,
        out_specs=(both, both) + (over_fsdp,) * 8 + (P("fsdp"),) * 4,
        check_vma=False,
    )
```

```python
import functools

import jax
import jax.numpy as jnp
from jax import lax
from jax.experimental import pallas as pl
from jax.experimental.pallas import tpu as pltpu
from jax.sharding import PartitionSpec as P

HEAD = 128
HALF = HEAD // 2
SEQ_LEN = 1024
EPS = 1e-06
ROPE_BASE = 1000000.0
SCALE = HEAD ** (-0.5)
LOG2E = 1.4426950408889634
VMEM_LIMIT = 56 * 1024 * 1024
NT = (((1,), (1,)), ((), ()))
NN = (((1,), (0,)), ((), ()))
TN = (((0,), (0,)), ((), ()))
F32 = jnp.float32
BF16 = jnp.bfloat16


def mm(left, right, dims=NN):
    return lax.dot_general(left, right, dims, preferred_element_type=F32)


def head_norm(raw):
    return lax.rsqrt(jnp.mean(raw * raw, axis=-1, keepdims=True) + EPS)


def turn(values, cosines, sines):
    return values * cosines + pltpu.roll(values, HALF, 1) * sines


def turn_back(values, cosines, sines):
    return values * cosines - pltpu.roll(values, HALF, 1) * sines


def norm_turn(raw, gain, cosines, sines):
    return turn(raw * head_norm(raw) * gain, cosines, sines).astype(BF16)


def norm_turn_back(raw, gain, grad, cosines, sines):
    back = turn_back(grad, cosines, sines)
    scale = head_norm(raw)
    pulled = back * gain
    inner = jnp.mean(raw * pulled, axis=-1, keepdims=True)
    gain_part = jnp.sum(raw * scale * back, axis=0, keepdims=True)
    return scale * pulled - raw * (scale * scale * scale * inner), gain_part


def diagonal_mask(rows, groups):
    keys = lax.broadcasted_iota(jnp.int32, (rows, groups * rows), 0)
    places = lax.broadcasted_iota(jnp.int32, (rows, groups * rows), 1)
    return keys <= lax.rem(places, rows)


def row_block(block, rank, rows):
    return pl.ds(pl.multiple_of(jnp.bitwise_xor(block, rank) * rows, rows), rows)


def attend_fwd_kernel(
    blocks, rows, groups,
    rank_ref, q_ref, k_ref, v_ref, g_ref, cos_ref, sin_ref, qg_ref, kg_ref,
    gated_ref, mix_ref, lse_ref, keys, vals_t,
):
    rank = rank_ref[0]
    factor = SCALE * LOG2E
    for a in range(blocks):
        place = row_block(a, rank, rows)
        here = slice(a * rows, (a + 1) * rows)
        keys[here, :] = norm_turn(k_ref[place, :], kg_ref[...], cos_ref[place, :], sin_ref[place, :])
        vals_t[:, here] = v_ref[place, :].T.astype(BF16)
    mask = diagonal_mask(rows, groups)
    for a in range(blocks):
        place = row_block(a, rank, rows)
        cosines, sines = cos_ref[place, :], sin_ref[place, :]
        queries = jnp.concatenate(
            [
                norm_turn(q_ref[place, h * HEAD : (h + 1) * HEAD], qg_ref[...], cosines, sines)
                for h in range(groups)
            ],
            axis=0,
        )
        low, high = a * rows, (a + 1) * rows
        near = jnp.where(mask, mm(keys[low:high, :], queries, NT), -1e30)
        peak = jnp.max(near, axis=0, keepdims=True)
        if a:
            far = mm(keys[:low, :], queries, NT)
            peak = jnp.maximum(peak, jnp.max(far, axis=0, keepdims=True))
        near = jnp.exp2((near - peak) * factor)
        total = jnp.sum(near, axis=0, keepdims=True)
        if a:
            far = jnp.exp2((far - peak) * factor)
            total = total + jnp.sum(far, axis=0, keepdims=True)
        inverse = 1.0 / total
        mix_t = mm(vals_t[:, low:high], (near * inverse).astype(BF16))
        if a:
            mix_t = mix_t + mm(vals_t[:, :low], (far * inverse).astype(BF16))
        mix = mix_t.T
        for h in range(groups):
            cols = slice(h * HEAD, (h + 1) * HEAD)
            part = mix[h * rows : (h + 1) * rows, :]
            opening = jax.nn.sigmoid(g_ref[place, cols].astype(BF16).astype(F32))
            mix_ref[place, cols] = part
            gated_ref[place, cols] = (part * opening).astype(BF16)
        lse_ref[0, a : a + 1, :] = peak * factor + jnp.log2(total)


def attend_bwd_kernel(
    blocks, rows, groups, kv_local,
    rank_ref, q_ref, k_ref, v_ref, g_ref, cos_ref, sin_ref, qg_ref, kg_ref, mix_ref, lse_ref, up_ref,
    grad_ref, qgain_ref, kgain_ref, keys, keys_t, vals, dkeys, dvals,
):
    rank = rank_ref[0]
    step = pl.program_id(0)
    factor = SCALE * LOG2E
    width = groups * HEAD

    @pl.when(step == 0)
    def _():
        qgain_ref[...] = jnp.zeros_like(qgain_ref)
        kgain_ref[...] = jnp.zeros_like(kgain_ref)

    for a in range(blocks):
        place = row_block(a, rank, rows)
        here = slice(a * rows, (a + 1) * rows)
        block = norm_turn(k_ref[place, :], kg_ref[...], cos_ref[place, :], sin_ref[place, :])
        keys[here, :] = block
        keys_t[:, here] = block.astype(F32).T.astype(BF16)
        vals[here, :] = v_ref[place, :].astype(BF16)
    mask = diagonal_mask(rows, groups)
    qgain = jnp.zeros((1, HEAD), F32)
    for a in reversed(range(blocks)):
        place = row_block(a, rank, rows)
        cosines, sines = cos_ref[place, :], sin_ref[place, :]
        queries, grads = [], []
        for h in range(groups):
            cols = slice(h * HEAD, (h + 1) * HEAD)
            queries.append(norm_turn(q_ref[place, cols], qg_ref[...], cosines, sines))
            upstream = up_ref[place, cols].astype(F32)
            opening = jax.nn.sigmoid(g_ref[place, cols].astype(BF16).astype(F32))
            opened = upstream * opening
            grads.append(opened.astype(BF16))
            grad_ref[
                place, pl.ds((kv_local * (groups + 2)) * HEAD + step * width + h * HEAD, HEAD)
            ] = (opened * mix_ref[place, cols] * (1.0 - opening)).astype(BF16)
        queries = jnp.concatenate(queries, axis=0)
        grads = jnp.concatenate(grads, axis=0)
        lse = lse_ref[0, a : a + 1, :]
        low, high = a * rows, (a + 1) * rows
        spans = [(low, high)] + ([(0, low)] if a else [])
        chances, grad_chances = [], []
        centre = jnp.zeros((1, groups * rows), F32)
        for start, stop in spans:
            part = jnp.exp2(mm(keys[start:stop, :], queries, NT) * factor - lse)
            if start == low:
                part = jnp.where(mask, part, 0.0)
            pull = mm(vals[start:stop, :], grads, NT)
            centre = centre + jnp.sum(part * pull, axis=0, keepdims=True)
            chances.append(part)
            grad_chances.append(pull)
        dq_t = jnp.zeros((HEAD, groups * rows), F32)
        for (start, stop), part, pull in zip(spans, chances, grad_chances):
            grad_products = (part * (pull - centre) * SCALE).astype(BF16)
            dval = mm(part.astype(BF16), grads)
            dkey = mm(grad_products, queries)
            if a == blocks - 1:
                dvals[start:stop, :] = dval
                dkeys[start:stop, :] = dkey
            else:
                dvals[start:stop, :] += dval
                dkeys[start:stop, :] += dkey
            dq_t = dq_t + mm(keys_t[:, start:stop], grad_products)
        dq = dq_t.T
        for h in range(groups):
            grad = dq[h * rows : (h + 1) * rows, :].astype(BF16).astype(F32)
            cols = slice(h * HEAD, (h + 1) * HEAD)
            raw, gain_part = norm_turn_back(q_ref[place, cols], qg_ref[...], grad, cosines, sines)
            grad_ref[place, pl.ds(step * width + h * HEAD, HEAD)] = raw.astype(BF16)
            qgain = qgain + gain_part
    kgain = jnp.zeros((1, HEAD), F32)
    for a in range(blocks):
        place = row_block(a, rank, rows)
        here = slice(a * rows, (a + 1) * rows)
        grad = dkeys[here, :].astype(BF16).astype(F32)
        raw, gain_part = norm_turn_back(
            k_ref[place, :], kg_ref[...], grad, cos_ref[place, :], sin_ref[place, :]
        )
        kgain = kgain + gain_part
        grad_ref[place, pl.ds(kv_local * width + step * HEAD, HEAD)] = raw.astype(BF16)
        grad_ref[place, pl.ds(kv_local * (width + HEAD) + step * HEAD, HEAD)] = dvals[
            here, :
        ].astype(BF16)
    qgain_ref[...] += qgain
    kgain_ref[...] += kgain


def attention_specs(length, groups, kv_local):
    width = groups * HEAD
    return [
        pl.BlockSpec((length, width), lambda g, r: (0, g)),
        pl.BlockSpec((length, HEAD), lambda g, r: (0, kv_local * groups + g)),
        pl.BlockSpec((length, HEAD), lambda g, r: (0, kv_local * (groups + 1) + g)),
        pl.BlockSpec((length, width), lambda g, r: (0, kv_local * (groups + 2) // groups + g)),
        pl.BlockSpec((length, HEAD), lambda g, r: (0, 0)),
        pl.BlockSpec((length, HEAD), lambda g, r: (0, 0)),
        pl.BlockSpec((1, HEAD), lambda g, r: (0, 0)),
        pl.BlockSpec((1, HEAD), lambda g, r: (0, 0)),
    ]


def attend_forward(rank, raw, cosines, sines, q_gain, k_gain, blocks, groups, kv_local):
    length = raw.shape[0]
    rows = length // blocks
    width = groups * HEAD
    flops = 4 * kv_local * groups * length * length * HEAD * (blocks + 1) // (2 * blocks)
    return pl.pallas_call(
        functools.partial(attend_fwd_kernel, blocks, rows, groups),
        grid_spec=pltpu.PrefetchScalarGridSpec(
            num_scalar_prefetch=1,
            grid=(kv_local,),
            in_specs=attention_specs(length, groups, kv_local),
            out_specs=[
                pl.BlockSpec((length, width), lambda g, r: (0, g)),
                pl.BlockSpec((length, width), lambda g, r: (0, g)),
                pl.BlockSpec((1, blocks, groups * rows), lambda g, r: (g, 0, 0)),
            ],
            scratch_shapes=[pltpu.VMEM((length, HEAD), BF16), pltpu.VMEM((HEAD, length), BF16)],
        ),
        out_shape=[
            jax.ShapeDtypeStruct((length, kv_local * width), BF16),
            jax.ShapeDtypeStruct((length, kv_local * width), F32),
            jax.ShapeDtypeStruct((kv_local, blocks, groups * rows), F32),
        ],
        compiler_params=pltpu.CompilerParams(
            dimension_semantics=("arbitrary",), vmem_limit_bytes=VMEM_LIMIT
        ),
        cost_estimate=pl.CostEstimate(
            flops=4 * flops,
            bytes_accessed=raw.size * 4 + length * kv_local * width * 6,
            transcendentals=kv_local * groups * length * length // 2,
        ),
        name="attend_forward",
    )(rank, raw, raw, raw, raw, cosines, sines, q_gain, k_gain)


def attend_backward(
    rank, raw, cosines, sines, q_gain, k_gain, mix, lse, upstream, blocks, groups, kv_local
):
    length = raw.shape[0]
    rows = length // blocks
    width = groups * HEAD
    flops = 10 * kv_local * groups * length * length * HEAD * (blocks + 1) // (2 * blocks)
    return pl.pallas_call(
        functools.partial(attend_bwd_kernel, blocks, rows, groups, kv_local),
        grid_spec=pltpu.PrefetchScalarGridSpec(
            num_scalar_prefetch=1,
            grid=(kv_local,),
            in_specs=attention_specs(length, groups, kv_local)
            + [
                pl.BlockSpec((length, width), lambda g, r: (0, g)),
                pl.BlockSpec((1, blocks, groups * rows), lambda g, r: (g, 0, 0)),
                pl.BlockSpec((length, width), lambda g, r: (0, g)),
            ],
            out_specs=[
                pl.BlockSpec(raw.shape, lambda g, r: (0, 0)),
                pl.BlockSpec((1, HEAD), lambda g, r: (0, 0)),
                pl.BlockSpec((1, HEAD), lambda g, r: (0, 0)),
            ],
            scratch_shapes=[
                pltpu.VMEM((length, HEAD), BF16),
                pltpu.VMEM((HEAD, length), BF16),
                pltpu.VMEM((length, HEAD), BF16),
                pltpu.VMEM((length, HEAD), F32),
                pltpu.VMEM((length, HEAD), F32),
            ],
        ),
        out_shape=[
            jax.ShapeDtypeStruct(raw.shape, BF16),
            jax.ShapeDtypeStruct((1, HEAD), F32),
            jax.ShapeDtypeStruct((1, HEAD), F32),
        ],
        compiler_params=pltpu.CompilerParams(
            dimension_semantics=("arbitrary",), vmem_limit_bytes=VMEM_LIMIT
        ),
        cost_estimate=pl.CostEstimate(
            flops=4 * flops,
            bytes_accessed=raw.size * 6 + length * kv_local * width * 6,
            transcendentals=kv_local * groups * length * length // 2,
        ),
        name="attend_backward",
    )(rank, raw, raw, raw, raw, cosines, sines, q_gain, k_gain, mix, lse, upstream)


def middle_kernel(tokens_ref, own_ref, x_ref, y_ref, gain_ref, middle_ref, second_ref):
    middle = tokens_ref[...].astype(F32) + own_ref[...]
    middle = middle + x_ref[...].astype(F32) + y_ref[...].astype(F32)
    scale = lax.rsqrt(jnp.mean(middle * middle, axis=-1, keepdims=True) + EPS)
    middle_ref[...] = middle
    second_ref[...] = (middle * scale * gain_ref[...]).astype(BF16)


def norm_back_kernel(low, values_ref, base_ref, own_ref, x_ref, y_ref, gain_ref, grad_ref, *low_ref):
    values = values_ref[...].astype(F32)
    grad = own_ref[...] + x_ref[...].astype(F32) + y_ref[...].astype(F32)
    scale = lax.rsqrt(jnp.mean(values * values, axis=-1, keepdims=True) + EPS)
    normed = values * scale
    pulled = grad * gain_ref[...]
    inner = jnp.mean(normed * pulled, axis=-1, keepdims=True)
    total = base_ref[...] + scale * (pulled - normed * inner)
    grad_ref[...] = total
    if low:
        low_ref[0][...] = total.astype(BF16)


def row_call(kernel, name, arrays, gain, outs):
    rows, width = arrays[0].shape
    tile = rows // 2

    def spec(shape):
        if shape[0] == rows:
            return pl.BlockSpec((tile, width), lambda i: (i, 0))
        return pl.BlockSpec((1, width), lambda i: (0, 0))

    return pl.pallas_call(
        kernel,
        grid=(2,),
        in_specs=[spec(a.shape) for a in arrays] + [spec(gain.shape)],
        out_specs=[spec(o.shape) for o in outs],
        out_shape=outs,
        compiler_params=pltpu.CompilerParams(
            dimension_semantics=("arbitrary",), vmem_limit_bytes=VMEM_LIMIT
        ),
        cost_estimate=pl.CostEstimate(
            flops=16 * rows * width, bytes_accessed=18 * rows * width, transcendentals=rows
        ),
        name=name,
    )(*arrays, gain)


def two_addends(came):
    if len(came) == 2:
        return came
    return [sum(part.astype(F32) for part in came[:-1]), came[-1]]


def middle_and_second(tokens, own, came, gain):
    return row_call(
        middle_kernel, "middle_and_second", [tokens, own, *two_addends(came)], gain[None],
        [jax.ShapeDtypeStruct(own.shape, F32), jax.ShapeDtypeStruct(own.shape, BF16)],
    )


def norm_back(values, base, own, came, gain, low):
    outs = [jax.ShapeDtypeStruct(own.shape, F32)] + [jax.ShapeDtypeStruct(own.shape, BF16)] * low
    return row_call(
        functools.partial(norm_back_kernel, low), "norm_back",
        [values, base, own, *two_addends(came)], gain[None], outs,
    )


def flat_specs(pieces, spec):
    return [spec(piece) for block in pieces for piece in block]


def grouped(refs, counts):
    blocks, start = [], 0
    for count in counts:
        blocks.append(refs[start : start + count])
        start += count
    return blocks, refs[start:]


def split_columns_kernel(counts, sizes, weighed, rank_ref, *refs):
    sources = []
    for group in counts:
        blocks, refs = grouped(refs, group)
        sources.append(blocks)
    weights, outs, sums = refs[:weighed], refs[weighed:-1], refs[-1]
    block = jnp.bitwise_xor(pl.program_id(0), rank_ref[0])
    for j in range(len(counts[0])):

        @pl.when(block == j)
        def _(j=j):
            done = 0
            for blocks, group_sizes in zip(sources, sizes):
                top = 0
                for piece in blocks[j]:
                    start, stop = 0, top + piece.shape[0]
                    for size, out in zip(group_sizes, outs[done:]):
                        out[top:stop, :] = piece[:, start : start + size].astype(F32)
                        start += size
                    top = stop
                done += len(group_sizes)

    part = sum(
        jnp.sum(out[...] * weight[...].astype(F32), axis=1, keepdims=True)
        for out, weight in zip(outs, weights)
    )

    @pl.when(pl.program_id(0) == 0)
    def _():
        sums[...] = jnp.zeros_like(sums)

    sums[...] += part


def split_columns(rank, groups, sizes, weights):
    count, rows = len(groups[0]), groups[0][0][0].shape[0]
    pieces, flat = sum(groups, []), sum(sizes, ())
    part_specs = [pl.BlockSpec((rows, size), lambda a, r: (0, a)) for size in flat]
    return pl.pallas_call(
        functools.partial(
            split_columns_kernel, [[len(block) for block in group] for group in groups], sizes,
            len(weights),
        ),
        grid_spec=pltpu.PrefetchScalarGridSpec(
            num_scalar_prefetch=1,
            grid=(count,),
            in_specs=flat_specs(pieces, lambda p: pl.BlockSpec(p.shape, lambda a, r: (0, 0)))
            + part_specs[: len(weights)],
            out_specs=part_specs + [pl.BlockSpec((rows, 1), lambda a, r: (0, 0))],
        ),
        out_shape=[jax.ShapeDtypeStruct((rows, count * size), F32) for size in flat]
        + [jax.ShapeDtypeStruct((rows, 1), F32)],
        compiler_params=pltpu.CompilerParams(
            dimension_semantics=("arbitrary",), vmem_limit_bytes=VMEM_LIMIT
        ),
        cost_estimate=pl.CostEstimate(
            flops=0, bytes_accessed=6 * rows * count * sum(flat), transcendentals=0
        ),
        name="split_columns",
    )(rank, *sum(pieces, []), *weights)


def stack_rows_kernel(counts, rank_ref, *refs):
    sources, (out,) = grouped(refs, counts)
    block = jnp.bitwise_xor(pl.program_id(0), rank_ref[0])
    for j, pieces in enumerate(sources):

        @pl.when(block == j)
        def _(pieces=pieces):
            top = 0
            for piece in pieces:
                out[top : top + piece.shape[0], :] = piece[...].astype(F32)
                top += piece.shape[0]


def stack_rows(rank, pieces):
    count, (rows, width) = len(pieces), pieces[0][0].shape
    return pl.pallas_call(
        functools.partial(stack_rows_kernel, [len(block) for block in pieces]),
        grid_spec=pltpu.PrefetchScalarGridSpec(
            num_scalar_prefetch=1,
            grid=(count,),
            in_specs=flat_specs(pieces, lambda p: pl.BlockSpec(p.shape, lambda a, r: (0, 0))),
            out_specs=pl.BlockSpec((rows, width), lambda a, r: (a, 0)),
        ),
        out_shape=jax.ShapeDtypeStruct((count * rows, width), F32),
        compiler_params=pltpu.CompilerParams(
            dimension_semantics=("arbitrary",), vmem_limit_bytes=VMEM_LIMIT
        ),
        cost_estimate=pl.CostEstimate(
            flops=0, bytes_accessed=6 * rows * count * width, transcendentals=0
        ),
        name="stack_rows",
    )(rank, *sum(pieces, []))


def weave_units_kernel(counts, steps, shards, units, rank_ref, *refs):
    sources, (weight, out, sums, held) = grouped(refs, counts)
    step = pl.program_id(0)
    for j, pieces in enumerate(sources):
        place = jnp.bitwise_xor(rank_ref[0], j)
        if len(pieces) == 1:
            held[place] = pieces[0][...].astype(F32)
            continue
        share = steps // len(pieces)
        for k, piece in enumerate(pieces):

            @pl.when((step >= k * share) & (step < (k + 1) * share))
            def _(piece=piece, place=place):
                held[place] = piece[...].astype(F32)

    count = len(counts)
    for a in range(count):
        for f in range(shards):
            start = (f * count + a) * units
            out[:, start : start + units] = held[a, :, f * units : (f + 1) * units]
    sums[...] = jnp.sum(out[...] * weight[...].astype(F32), axis=1, keepdims=True)


def weave_units(rank, pieces, group, weight, shards):
    count, (rows, width) = len(pieces), pieces[0][0].shape
    ffs, steps = width // 2, 2
    tile = rows // steps

    def spec(block, k):
        share = steps // len(block)

        def place(i, r):
            return (jnp.clip(i - k * share, 0, share - 1), group)

        return pl.BlockSpec((tile, ffs), place)

    return pl.pallas_call(
        functools.partial(
            weave_units_kernel, [len(block) for block in pieces], steps, shards, ffs // shards
        ),
        grid_spec=pltpu.PrefetchScalarGridSpec(
            num_scalar_prefetch=1,
            grid=(steps,),
            in_specs=[spec(block, k) for block in pieces for k in range(len(block))]
            + [pl.BlockSpec((tile, count * ffs), lambda i, r: (i, 0))],
            out_specs=[
                pl.BlockSpec((tile, count * ffs), lambda i, r: (i, 0)),
                pl.BlockSpec((tile, 1), lambda i, r: (i, 0)),
            ],
            scratch_shapes=[pltpu.VMEM((count, tile, ffs), F32)],
        ),
        out_shape=[
            jax.ShapeDtypeStruct((rows, count * ffs), F32), jax.ShapeDtypeStruct((rows, 1), F32),
        ],
        compiler_params=pltpu.CompilerParams(
            dimension_semantics=("arbitrary",), vmem_limit_bytes=VMEM_LIMIT
        ),
        cost_estimate=pl.CostEstimate(
            flops=0, bytes_accessed=8 * rows * count * ffs, transcendentals=0
        ),
        name="weave_units",
    )(rank, *sum(pieces, []), weight)


def column_shares_kernel(rank_ref, *refs):
    start = 0
    for ref in refs[:-1]:
        refs[-1][:, start : start + ref.shape[1]] = ref[...]
        start += ref.shape[1]


def column_shares(rank, weights, sizes):
    rows, width = weights[0].shape[0], sum(sizes)
    tile = rows // 2
    return pl.pallas_call(
        column_shares_kernel,
        grid_spec=pltpu.PrefetchScalarGridSpec(
            num_scalar_prefetch=1,
            grid=(2,),
            in_specs=[pl.BlockSpec((tile, size), lambda i, r: (i, r[0])) for size in sizes],
            out_specs=pl.BlockSpec((tile, width), lambda i, r: (i, 0)),
        ),
        out_shape=jax.ShapeDtypeStruct((rows, width), weights[0].dtype),
        compiler_params=pltpu.CompilerParams(
            dimension_semantics=("arbitrary",), vmem_limit_bytes=VMEM_LIMIT
        ),
        cost_estimate=pl.CostEstimate(
            flops=0, bytes_accessed=4 * rows * width, transcendentals=0
        ),
        name="column_shares",
    )(rank, *weights)


def swap(values, bit, axis="sp"):
    return lax.ppermute(values, axis, [(i, i ^ bit) for i in range(lax.axis_size(axis))])


def sync(*values):
    return lax.optimization_barrier(values)


def gather_start(block):
    return [block] + [swap(block, j) for j in range(1, lax.axis_size("sp"))][: 2 if lax.axis_size("sp") == 4 else None]


def gather_turn(held):
    if lax.axis_size("sp") != 4:
        return held
    half = held[0].shape[0] // 2
    return held + [swap(held[2][:half], 1), swap(held[1][half:], 2)]


def gather_end(held):
    if lax.axis_size("sp") != 4:
        return held
    return held[:3] + [jnp.concatenate(held[3:], axis=0)]


def gather_blocks(block):
    return gather_end(gather_turn(gather_start(block)))


def gather_pieces(held):
    if lax.axis_size("sp") != 4:
        return [[block] for block in held]
    return [[block] for block in held[:3]] + [held[3:]]


def scatter_start(corner):
    if lax.axis_size("sp") != 4:
        return []
    half = corner.shape[0] // 2
    return [swap(corner[:half], 1), swap(corner[half:], 2)]


def scatter_turn(others, came):
    if lax.axis_size("sp") != 4:
        return [swap(part.astype(BF16), j + 1) for j, part in enumerate(others)]
    to_x, to_y = add_corner(others, came)
    return [swap(to_x, 1), swap(to_y, 2)]


def add_corner_kernel(whole_ref, from_x_ref, from_y_ref, to_x_ref, to_y_ref):
    half = from_x_ref.shape[0]

    @pl.when(pl.program_id(0) == 0)
    def _():
        to_x_ref[:half, :] = whole_ref[:half, :].astype(BF16)
        to_x_ref[half:, :] = (whole_ref[half:, :] + from_y_ref[...].astype(F32)).astype(BF16)

    @pl.when(pl.program_id(0) == 1)
    def _():
        to_y_ref[:half, :] = (whole_ref[:half, :] + from_x_ref[...].astype(F32)).astype(BF16)
        to_y_ref[half:, :] = whole_ref[half:, :].astype(BF16)


def add_corner(whole, came):
    rows, width = whole.shape[0] // 2, whole.shape[1]
    half = pl.BlockSpec((rows // 2, width), lambda i: (0, 0))
    out = pl.BlockSpec((rows, width), lambda i: (0, 0))
    return pl.pallas_call(
        add_corner_kernel,
        grid=(2,),
        in_specs=[pl.BlockSpec((rows, width), lambda i: (i, 0)), half, half],
        out_specs=[out, out],
        out_shape=[jax.ShapeDtypeStruct((rows, width), BF16)] * 2,
        compiler_params=pltpu.CompilerParams(
            dimension_semantics=("arbitrary",), vmem_limit_bytes=32 * 1024 * 1024
        ),
        cost_estimate=pl.CostEstimate(
            flops=rows * width, bytes_accessed=14 * rows * width, transcendentals=0
        ),
        name="add_corner",
    )(whole, *came)


def scatter_end(own, came):
    for part in came:
        own = own + part.astype(F32)
    return own


def corner_rows(make, rows):
    count = lax.axis_size("sp")
    return make((count - 1) * rows, count * rows).astype(BF16) if count == 4 else None


def other_rows(make, rows):
    count = lax.axis_size("sp")
    stop = 3 if count == 4 else count
    whole = make(rows, stop * rows)
    if count == 4:
        return whole
    return [whole[j * rows : (j + 1) * rows] for j in range(stop - 1)]


def place_blocks(blocks, rank, axis):
    size = blocks[0].shape[axis]
    shape = list(blocks[0].shape)
    shape[axis] = size * len(blocks)
    whole = jnp.zeros(shape, blocks[0].dtype)
    for j, block in enumerate(blocks):
        whole = lax.dynamic_update_slice_in_dim(
            whole, block, jnp.bitwise_xor(rank, j) * size, axis
        )
    return whole


def halve_start(held, bit):
    shard = lax.axis_index("fsdp")
    mine = jnp.bitwise_and(lax.div(shard, jnp.int32(bit)), 1)
    pairs = held.reshape(held.shape[0] // 2, 2, held.shape[1], held.shape[2])
    sent = lax.dynamic_index_in_dim(pairs, 1 - mine, 1, False)
    kept = lax.dynamic_index_in_dim(pairs, mine, 1, False)
    return kept, swap(sent, bit, "fsdp")


def halve_end(state):
    return (state[0].astype(F32) + state[1].astype(F32)).astype(BF16)


def halve_open(grad):
    shards = lax.axis_size("fsdp")
    return halve_start(grad.reshape(shards, grad.shape[0] // shards, grad.shape[1]), 1)


def halve_next(state, bit):
    return halve_start(halve_end(state), bit)


def halve_close(state):
    held = halve_end(state)
    while held.shape[0] > 1:
        held = halve_end(halve_start(held, lax.axis_size("fsdp") // held.shape[0]))
    return held[0]


def double_over(values, axis):
    bit = 1
    while bit < lax.axis_size(axis):
        values = jnp.concatenate([values, swap(values, bit, axis)], axis=0)
        bit *= 2
    return values


def sum_steps():
    return [
        (axis, 1 << k)
        for axis in ("sp", "fsdp")
        for k in range((lax.axis_size(axis) - 1).bit_length())
    ]


def sum_over(values, steps):
    for axis, bit in steps:
        values = values + swap(values, bit, axis)
    return values


def rms_low(values, gain):
    scale = lax.rsqrt(jnp.mean(values * values, axis=-1, keepdims=True) + EPS)
    return (values * scale * gain).astype(BF16)


def on_device(
    tokens, cotangent, positions, domain_ids, counts, loss_weight, domain_weights,
    q_weight, k_weight, v_weight, g_weight, o_weight, gate_weight, up_weight, down_weight,
    attn_gain, mlp_gain, q_gain, k_gain,
):
    count, shards = lax.axis_size("sp"), lax.axis_size("fsdp")
    rank, shard = lax.axis_index("sp"), lax.axis_index("fsdp")
    rank_ref = rank.astype(jnp.int32).reshape(1)
    _, rows, width = tokens.shape
    heads_local = q_weight.shape[1] // HEAD // count
    kv_local = k_weight.shape[1] // HEAD // count
    groups = heads_local // kv_local
    qcols, kcols = heads_local * HEAD, kv_local * HEAD
    dcols = width // count
    units = down_weight.shape[0] // count
    ffs = units * shards

    def gather(weight):
        return lax.all_gather(weight, "fsdp", axis=0, tiled=True)

    def unit_columns(weight):
        spread = weight.reshape(weight.shape[0], shards, count, units)
        return lax.dynamic_slice_in_dim(spread, rank, 1, 2).reshape(weight.shape[0], ffs)

    def scatter(grad):
        return lax.psum_scatter(grad, "fsdp", scatter_dimension=0, tiled=True)

    tokens_held = gather_start(tokens[0])
    places = double_over(positions[0][None], "sp").reshape(-1)
    gains = double_over(jnp.concatenate([attn_gain, mlp_gain, q_gain, k_gain])[None], "fsdp")
    attn_full = gather(
        column_shares(
            rank_ref, (q_weight, k_weight, v_weight, g_weight, o_weight),
            (qcols, kcols, kcols, qcols, dcols),
        )
    )
    in_cols = 2 * (qcols + kcols)
    onehot = (domain_ids[:, None] == jnp.arange(domain_weights.shape[0], dtype=jnp.int32)).astype(F32)
    seq_scale = loss_weight * jnp.sum(onehot * domain_weights[None, :], axis=1) * SEQ_LEN
    seq_scale = (seq_scale / counts.astype(F32))[0]
    upstream = cotangent[0].astype(F32) * seq_scale
    tokens_held, places, gains = sync(tokens_held, places, gains)
    tokens_held = gather_turn(tokens_held)
    gateup_share = jnp.concatenate([unit_columns(gate_weight), unit_columns(up_weight)], axis=1)
    tokens_held, upstream_low, gateup_share = sync(
        tokens_held, upstream.astype(BF16), gateup_share
    )
    gateup = gather(gateup_share)
    w_gate, w_up = gateup[:, :ffs], gateup[:, ffs:]
    upstream_held = gather_start(upstream_low)
    tokens_all = jnp.concatenate(gather_end(tokens_held), axis=0)

    order = jnp.bitwise_xor(jnp.arange(shards, dtype=jnp.int32), shard.astype(jnp.int32))
    gains = jnp.take(gains, order, axis=0).astype(F32)
    part = attn_gain.shape[0]
    first_gain = gains[:, :part].reshape(-1)
    second_gain = gains[:, part : 2 * part].reshape(-1)
    piece = q_gain.shape[0]
    query_gain = gains[:, 2 * part : 2 * part + piece].reshape(1, HEAD)
    key_gain = gains[:, 2 * part + piece :].reshape(1, HEAD)
    inverse = ROPE_BASE ** (-(2.0 * jnp.arange(HALF, dtype=F32)) / HEAD)
    angles = places.astype(F32)[:, None] * inverse
    cosines, sines = jnp.cos(angles), jnp.sin(angles)
    cosines = jnp.concatenate([cosines, cosines], axis=1)
    sines = jnp.concatenate([-sines, sines], axis=1)
    first = rms_low(tokens_all.astype(F32), first_gain)

    upstream_held, first, cosines, sines = sync(upstream_held, first, cosines, sines)
    upstream_held = gather_turn(upstream_held)
    first, upstream_held = sync(first, upstream_held)
    upstream_all = jnp.concatenate(gather_end(upstream_held), axis=0)
    first, upstream_all = sync(first, upstream_all)

    w_in = attn_full[:, :in_cols]
    o_slices = attn_full[:, in_cols:].reshape(count, qcols, dcols)
    o_blocks = [
        lax.dynamic_index_in_dim(o_slices, jnp.bitwise_xor(rank, j), 0, False) for j in range(count)
    ]
    first, o_blocks = sync(first, o_blocks)
    o_blocks = [swap(block, j) if j else block for j, block in enumerate(o_blocks)]
    raw = mm(first, w_in)
    raw, o_blocks = sync(raw, o_blocks)
    w_out = place_blocks(o_blocks, rank, 1)
    gated, mix, lse = attend_forward(
        rank_ref, raw, cosines, sines, query_gain, key_gain, count, groups, kv_local
    )
    down_share = lax.dynamic_slice_in_dim(down_weight, rank * units, units, 0)
    down_share, gated = sync(down_share, gated)
    w_down = gather(down_share)

    def out_rows(lo, hi):
        return mm(gated[lo:hi], w_out)

    corner = scatter_start(corner_rows(out_rows, rows))
    others = other_rows(out_rows, rows)
    own_part = out_rows(0, rows)
    middle, second = middle_and_second(
        tokens[0], own_part, scatter_turn(others, corner), second_gain
    )
    second = jnp.concatenate(gather_blocks(second), axis=0)

    gate_act = mm(second, w_gate)
    up_act = mm(second, w_up)
    opening = jax.nn.sigmoid(gate_act)
    silu = gate_act * opening
    hidden = (silu * up_act).astype(BF16)
    down_grad, hidden, upstream_now = sync(
        mm(hidden, upstream_all, TN).astype(BF16), hidden, upstream_all
    )
    down_share = scatter(down_grad)

    def down_rows(lo, hi):
        return mm(hidden[lo:hi], w_down)

    block_corner = corner_rows(down_rows, rows)
    block_others = other_rows(down_rows, rows)
    block_part = down_rows(0, rows)
    block_corner, block_others, block_part, upstream_now = sync(
        block_corner, block_others, block_part, upstream_now
    )
    block_corner = scatter_start(block_corner)
    grad_hidden = mm(upstream_now, w_down, NT)
    grad_gate = (grad_hidden * up_act * opening * (1.0 + gate_act * (1.0 - opening))).astype(BF16)
    grad_up = (grad_hidden * silu).astype(BF16)
    grad_gate, grad_up, block_corner = sync(grad_gate, grad_up, block_corner)
    block_came = scatter_turn(block_others, block_corner)
    gateup_grad = mm(second, jnp.concatenate([grad_gate, grad_up], axis=1), TN).astype(BF16)
    gateup_grad, grad_gate, grad_up, block_came = sync(gateup_grad, grad_gate, grad_up, block_came)
    gateup_share = scatter(gateup_grad)

    def second_rows(lo, hi):
        return mm(grad_gate[lo:hi], w_gate, NT) + mm(grad_up[lo:hi], w_up, NT)

    corner = scatter_start(corner_rows(second_rows, rows))
    others = other_rows(second_rows, rows)
    own_part = second_rows(0, rows)
    own_part, corner, others = sync(own_part, corner, others)
    came = scatter_turn(others, corner)
    block_out = (middle + scatter_end(block_part, block_came)).astype(BF16)
    came, block_out = sync(came, block_out)
    grad_middle, grad_attn = norm_back(middle, upstream, own_part, came, second_gain, True)
    grad_attn = gather_start(grad_attn)
    grad_attn = jnp.concatenate(gather_end(gather_turn(grad_attn)), axis=0)

    grad_gated = mm(grad_attn, w_out, NT).astype(BF16)
    out_grad = mm(gated, grad_attn, TN).astype(BF16)
    out_blocks = [
        lax.dynamic_slice_in_dim(out_grad, jnp.bitwise_xor(rank, j) * dcols, dcols, 1)
        for j in range(count)
    ]
    grad_gated, out_blocks, down_share = sync(grad_gated, out_blocks, down_share)
    out_blocks = [swap(block, j) if j else block for j, block in enumerate(out_blocks)]
    down_held = gather_start(down_share)
    grad_raw, query_gain_part, key_gain_part = attend_backward(
        rank_ref, raw, cosines, sines, query_gain, key_gain, mix, lse, grad_gated,
        count, groups, kv_local,
    )
    steps = sum_steps()
    gain_sums = jnp.concatenate([query_gain_part, key_gain_part], axis=1)
    attn_grad = mm(first, grad_raw, TN).astype(BF16)
    attn_grad, grad_raw, gain_sums = sync(attn_grad, grad_raw, gain_sums)

    def first_rows(lo, hi):
        return mm(grad_raw[lo:hi], w_in, NT)

    corner = corner_rows(first_rows, rows)
    corner, grad_raw, attn_grad, gain_sums, out_blocks = sync(
        corner, grad_raw, attn_grad, gain_sums, out_blocks
    )
    corner = scatter_start(corner)
    gain_sums = sum_over(gain_sums, steps[:1])
    others = other_rows(first_rows, rows)
    first_part = first_rows(0, rows)
    out_grad = place_blocks(out_blocks, rank, 0)
    attn_grad, out_grad, others, first_part, corner, down_held, gain_sums = sync(
        attn_grad, out_grad, others, first_part, corner, down_held, gain_sums
    )
    came = scatter_turn(others, corner)
    gateup_share, attn_grad, out_grad = sync(gateup_share, attn_grad, out_grad)
    attn_share = scatter(attn_grad)
    out_share = scatter(out_grad)
    gateup_held = gather_start(gateup_share)
    gain_sums = sum_over(gain_sums, steps[1:2])
    came, gain_sums, gateup_held = sync(came, gain_sums, gateup_held)
    gateup_held = gather_turn(gateup_held)
    down_held = gather_turn(down_held)
    (input_grad,) = norm_back(tokens[0], grad_middle, first_part, came, first_gain, False)
    gateup_held, gain_sums, input_grad, attn_share, down_held = sync(
        gateup_held, gain_sums, input_grad, attn_share, down_held
    )
    attn_held = gather_start(attn_share)
    gain_sums = sum_over(gain_sums, steps[2:3])
    gateup_pieces = gather_pieces(gateup_held)
    gate_grad, gate_sums = weave_units(rank_ref, gateup_pieces, 0, gate_weight, shards)
    down_grad = stack_rows(rank_ref, gather_pieces(down_held))
    attn_held, out_share, gate_grad, gain_sums, down_grad = sync(
        attn_held, out_share, gate_grad, gain_sums, down_grad
    )
    attn_held = gather_turn(attn_held)
    out_held = gather_start(out_share)
    gain_sums = sum_over(gain_sums, steps[3:4])
    up_grad, up_sums = weave_units(rank_ref, gateup_pieces, 1, up_weight, shards)
    attn_held, out_held, gain_sums, up_grad = sync(attn_held, out_held, gain_sums, up_grad)
    out_held = gather_turn(out_held)
    gain_sums = sum_over(gain_sums, steps[4:])
    *attn_grads, out_grad, in_sums = split_columns(
        rank_ref, [gather_pieces(attn_held), gather_pieces(out_held)],
        [(qcols, kcols, kcols, qcols), (dcols,)], (q_weight, k_weight, v_weight, g_weight),
    )
    attn_gain_grad = in_sums[:, 0] / attn_gain.astype(F32)
    mlp_gain_grad = (gate_sums + up_sums)[:, 0] / mlp_gain.astype(F32)

    def own(values):
        size = values.shape[0] // shards
        return lax.dynamic_slice_in_dim(values, shard * size, size, 0)

    return (
        block_out[None],
        input_grad[None],
        *attn_grads,
        out_grad,
        gate_grad,
        up_grad,
        down_grad,
        attn_gain_grad,
        mlp_gain_grad,
        own(gain_sums[0, :HEAD]),
        own(gain_sums[0, HEAD:]),
    )


def solution(mesh):
    both, over_fsdp = P("fsdp", "sp", None), P("fsdp", None)
    return jax.shard_map(
        on_device,
        mesh=mesh,
        in_specs=(both, both, P("fsdp", "sp"), P("fsdp"), P("fsdp"), P("fsdp"), P())
        + (over_fsdp,) * 8
        + (P("fsdp"),) * 4,
        out_specs=(both, both) + (over_fsdp,) * 8 + (P("fsdp"),) * 4,
        check_vma=False,
    )
```
